512 devices in a mesh: sec: 2 (over x_lo), gx: 128 (over y, z, core), gy: 2 (over x_hi).
Axes of the slice: x: 4 (x_hi: 2, x_lo: 2; x = x_hi * 2 + x_lo), y: 8, z: 8, core: 2. Of those that a mesh axis runs over, the one named last changes fastest.
Arguments:
- sections: float32 [2, 8, 2048, 64, 128], P('sec', None, 'gx', 'gy'), may hold values from -4 to 8, as said below
- fiber_angles: float32 [8, 2], replicated, may hold values from -3.140625 to 3.140625
- fiber_class: int32 [2048, 64, 8], P('gx', 'gy'), may hold values from 0 to 7
- row_map: int32 [128, 2, 512], P('gx', 'gy'), may hold values from 0 to 511, each once within a row
- interface_rows: int32 [2, 128, 2, 32], P(None, 'gx', 'gy'), may hold values from 0 to 31, each once within a row
Outputs:
- updated: float32 [2, 4, 2048, 64, 128], P('sec', None, 'gx', 'gy')
The draws below stay inside these ranges and needn't reach their ends.
Inputs may be any that keep to these rules, and one draw needn't show every extreme that they name: sections[0] holds calcium of 0.05 to 1, gates of 0 to 1, a bound buffer of 0 to 0.8 and tension of 0 to 1; sections[1] holds a stiffness of 0.5 to 2 and an activation coefficient of 2 to 8. `fiber_class`: the class of each column's block of 16 cells through the thickness. `row_map`: each block's list is a permutation of its 512 column places. `interface_rows`: for each side and block, a permutation of the 32 rows.
All inputs are finite; a program needn't handle non-finite values.
Results may differ from the reference program's by a relative error of at most 0.00002.
Values sent between devices are 32-bit elements; how exact they have to be, the bound alone decides.
A program may use at most 64 MiB of HBM per device.

```python
import math
import jax
import jax.numpy as jnp

CX = 16
CY = 32
NZ = 128
CLASSES = 8
STEPS = 2
SWEEPS = 2
NX = 2048
NY = 64
NZB = 8
COLS = 512
N_GX = 128
N_GY = 2


def draw_sections(key, part):
    grid_shape = (NX, NY, NZ)
    subkeys = jax.random.split(key, 16)
    voltage = jnp.clip(0.8 * jax.random.normal(subkeys[0], grid_shape, jnp.float32), -3.0, 3.0)
    motion = [jnp.clip(0.5 * jax.random.normal(subkeys[8 + channel], grid_shape, jnp.float32), -2.5, 2.5) for channel in range(3)]
    load_list = [jnp.clip(jax.random.normal(subkeys[11 + channel], grid_shape, jnp.float32), -4.0, 4.0) for channel in range(3)]
    calcium = jax.random.uniform(subkeys[1], grid_shape, jnp.float32, 0.05, 1.0)
    gate_list = [jax.random.uniform(subkeys[2 + channel], grid_shape, jnp.float32, 0.0, 1.0) for channel in range(4)]
    buffered = jax.random.uniform(subkeys[6], grid_shape, jnp.float32, 0.0, 0.8)
    tension = jax.random.uniform(subkeys[7], grid_shape, jnp.float32, 0.0, 1.0)
    stiffness = jnp.exp(jax.random.uniform(subkeys[14], grid_shape, jnp.float32, math.log(0.5), math.log(2.0)))
    coupling = jnp.exp(jax.random.uniform(subkeys[15], grid_shape, jnp.float32, math.log(2.0), math.log(8.0)))
    electric = jnp.stack([voltage, calcium] + gate_list + [buffered, tension])
    mechanic = jnp.stack(motion + load_list + [stiffness, coupling])
    return jnp.stack([electric, mechanic]).astype(jnp.float32)


def with_ends(values, own_key, smallest, largest):
    spot = [jax.random.randint(jax.random.fold_in(own_key, axis), (), 0, length) for axis, length in enumerate(values.shape)]
    longest = values.shape.index(max(values.shape))
    next_to = spot[:longest] + [(spot[longest] + 1) % values.shape[longest]] + spot[longest + 1:]
    return values.at[tuple(spot)].set(smallest).at[tuple(next_to)].set(largest)


def setup_inputs(seed: int = 0) -> dict:
    key_of = jax.random.split(jax.random.key(seed), 6)
    sections = draw_sections(jax.random.fold_in(key_of[5], 71), 0)
    fiber_angles = jnp.clip(jax.random.uniform(key_of[1], (CLASSES, 2), jnp.float32, -3.140625, 3.140625), -3.140625, 3.140625)
    fiber_class = with_ends(jax.random.randint(key_of[2], (NX, NY, NZB), 0, CLASSES), jax.random.fold_in(key_of[2], 1), 0, CLASSES - 1).astype(jnp.int32)
    row_map = jax.vmap(lambda own: jax.random.permutation(own, COLS))(jax.random.split(key_of[3], N_GX * N_GY)).reshape((N_GX, N_GY, COLS)).astype(jnp.int32)
    interface_rows = jax.vmap(lambda own: jax.random.permutation(own, CY))(jax.random.split(key_of[4], 2 * N_GX * N_GY)).reshape((2, N_GX, N_GY, CY)).astype(jnp.int32)
    return {"sections": sections, "fiber_angles": fiber_angles, "fiber_class": fiber_class, "row_map": row_map, "interface_rows": interface_rows}


sigma_long = 1.0
sigma_cross = 0.25
time_step = 0.1
shear_modulus = 1.0
lame_first = 1.0
relax_weight = 0.6
tie_stiffness = 2.0
diagonal_coef = 10.0


def fiber_table(fiber_angles):
    azimuth = fiber_angles[:, 0]
    elevation = fiber_angles[:, 1]
    fiber_dir = [jnp.cos(azimuth) * jnp.cos(elevation), jnp.sin(azimuth) * jnp.cos(elevation), jnp.sin(elevation)]
    spread_gap = sigma_long - sigma_cross
    return jnp.stack(fiber_dir + [
        sigma_cross + spread_gap * fiber_dir[0] * fiber_dir[0],
        sigma_cross + spread_gap * fiber_dir[1] * fiber_dir[1],
        sigma_cross + spread_gap * fiber_dir[2] * fiber_dir[2],
        spread_gap * fiber_dir[0] * fiber_dir[1],
        spread_gap * fiber_dir[0] * fiber_dir[2],
        spread_gap * fiber_dir[1] * fiber_dir[2]])


def shifted(values, offset):
    rolled = jnp.roll(values, -offset[0], axis=-3)
    rolled = jnp.roll(rolled, -offset[1], axis=-2)
    widths = [(0, 0)] * (values.ndim - 1) + [(1, 1)]
    padded = jnp.pad(rolled, widths)
    size_z = values.shape[-1]
    return padded[..., 1 + offset[2]:1 + offset[2] + size_z]


def unit_vec(axis_a, factor):
    return tuple(factor if place_a == axis_a else 0 for place_a in range(3))


def add_offsets(first_off, second_off):
    return tuple(first_off[place_a] + second_off[place_a] for place_a in range(3))


def second_diff(pick_cells, values, axis_a, centre):
    return pick_cells(values, unit_vec(axis_a, 1)) - 2.0 * centre + pick_cells(values, unit_vec(axis_a, -1))


def cross_diff(pick_cells, values, axis_a, axis_b):
    plus_a, minus_a = unit_vec(axis_a, 1), unit_vec(axis_a, -1)
    plus_b, minus_b = unit_vec(axis_b, 1), unit_vec(axis_b, -1)
    return 0.25 * (pick_cells(values, add_offsets(plus_a, plus_b)) - pick_cells(values, add_offsets(plus_a, minus_b))
                   - pick_cells(values, add_offsets(minus_a, plus_b)) + pick_cells(values, add_offsets(minus_a, minus_b)))


def diffuse(pick_cells, values, cell_fiber):
    centre = pick_cells(values, (0, 0, 0))
    result = jnp.zeros_like(centre)
    for axis_a in range(3):
        result = result + cell_fiber[3 + axis_a] * second_diff(pick_cells, values, axis_a, centre)
    for pair_axes, slot_index in (((0, 1), 6), ((0, 2), 7), ((1, 2), 8)):
        result = result + 2.0 * cell_fiber[slot_index] * cross_diff(pick_cells, values, pair_axes[0], pair_axes[1])
    return result


def ionic_step(cell_state, diffusion):
    voltage, calcium, activation, inactivation, potassium, slow_gate, buffered, tension = cell_state
    bound_share = calcium * calcium / (calcium * calcium + 0.25)
    calcium_flow = 1.2 * activation * inactivation * (voltage - 2.0)
    current_sum = calcium_flow + 0.8 * potassium * (voltage + 1.0) + 0.6 * bound_share * slow_gate * (voltage + 1.0) + 0.1 * voltage
    binding = 2.0 * calcium * (1.0 - buffered) - 0.4 * buffered
    return [voltage + time_step * (diffusion - current_sum),
            calcium + time_step * (-0.3 * calcium_flow - 0.5 * calcium - binding),
            activation + time_step * (jax.nn.sigmoid(2.0 * voltage + 1.0) - activation) / 0.5,
            inactivation + time_step * (jax.nn.sigmoid(-2.0 * voltage) - inactivation) / 3.0,
            potassium + time_step * (jax.nn.sigmoid(2.0 * voltage) - potassium),
            slow_gate + time_step * (jax.nn.sigmoid(voltage - 0.5) - slow_gate) / 5.0,
            buffered + time_step * binding,
            tension + time_step * (bound_share - tension) / 2.0]


def navier(pick_cells, motion, stiffness):
    centre = pick_cells(motion, (0, 0, 0))
    laplace = jnp.zeros_like(centre)
    for axis_a in range(3):
        laplace = laplace + second_diff(pick_cells, motion, axis_a, centre)
    pieces = []
    for component in range(3):
        component_term = second_diff(pick_cells, motion[component], component, centre[component])
        for other_axis in range(3):
            if other_axis != component:
                component_term = component_term + cross_diff(pick_cells, motion[other_axis], component, other_axis)
        pieces.append(component_term)
    graddiv = jnp.stack(pieces)
    return centre, -stiffness * (shear_modulus * laplace + (lame_first + shear_modulus) * graddiv)


def reference(sections, fiber_angles, fiber_class, row_map, interface_rows):
    fiber_rows = fiber_table(fiber_angles)
    block_depth = NZ // fiber_class.shape[-1]
    cell_fiber = jnp.repeat(jnp.moveaxis(fiber_rows.T[fiber_class], -1, 0), block_depth, axis=-1)
    cell_state = [sections[0, channel] for channel in range(8)]
    for repeat in range(STEPS):
        diffusion = diffuse(shifted, cell_state[0], cell_fiber)
        cell_state = ionic_step(cell_state, diffusion)
    tension_out = cell_state[7]
    blocks = tension_out.reshape(N_GX, CX, N_GY, CY, NZ).transpose(0, 2, 1, 3, 4).reshape(N_GX, N_GY, CX * CY, NZ)
    index_map = jnp.broadcast_to(row_map.astype(jnp.int32)[..., None], blocks.shape)
    remapped = jnp.take_along_axis(blocks, index_map, axis=2)
    remapped = remapped.reshape(N_GX, N_GY, CX, CY, NZ).transpose(0, 2, 1, 3, 4).reshape(NX, NY, NZ)
    activity = sections[1, 7] * remapped
    motion = sections[1, 0:3]
    stiffness = sections[1, 6]
    drive = sections[1, 3:6] + activity * cell_fiber[0:3]
    for repeat in range(SWEEPS):
        partial_value = (tie_stiffness * stiffness) * motion
        grid6 = partial_value.reshape(3, N_GX, CX, N_GY, CY, NZ)
        first_plane = grid6[:, :, 0]
        last_plane = grid6[:, :, -1]
        from_left = jnp.roll(last_plane, 1, axis=1)
        from_right = jnp.roll(first_plane, -1, axis=1)
        rows_first = jnp.broadcast_to(interface_rows[0].astype(jnp.int32)[None, :, :, :, None], first_plane.shape)
        rows_last = jnp.broadcast_to(interface_rows[1].astype(jnp.int32)[None, :, :, :, None], first_plane.shape)
        left_term = jnp.take_along_axis(from_left, rows_first, axis=3) - first_plane
        right_term = jnp.take_along_axis(from_right, rows_last, axis=3) - last_plane
        tie_force = jnp.zeros_like(grid6).at[:, :, 0].add(left_term).at[:, :, -1].add(right_term)
        tie_force = tie_force.reshape(3, NX, NY, NZ)
        centre, applied = navier(shifted, motion, stiffness)
        motion = centre + relax_weight * (drive + tie_force - applied) / (diagonal_coef * stiffness)
    electric_out = jnp.stack([cell_state[0], cell_state[1], cell_state[4], cell_state[7]])
    mechanic_out = jnp.concatenate([motion, activity[None]], axis=0)
    return jnp.stack([electric_out, mechanic_out])
```

```python
import functools

import jax
import jax.numpy as jnp
from jax import lax
from jax.experimental import pallas as pl
from jax.experimental.pallas import tpu as pltpu
from jax.sharding import PartitionSpec as P

MESH = pl.DeviceIdType.MESH
F32, BF16 = jnp.float32, jnp.bfloat16

CX, CY, NZ = 16, 32, 128
COLS = CX * CY
TOP = COLS + CY
EXT = COLS + 2 * CY
CLASSES = 8
DT = 0.1

CHUNKS = (((1, 5), ((1, 4),)), ((5, 9), ((4, 8),)), ((9, 13), ((8, 12),)), ((13, 15), ((12, 15), (0, 1), (15, 16))))

LEFT, RIGHT, ACROSS, DIAG_LEFT, DIAG_RIGHT, STIFF_LEFT, STIFF_RIGHT = range(7)
TEN_FIRST, TEN_LAST, TEN_ROWS, TEN_BULK = 16, 17, 18, 19
N_COPIES = TEN_BULK + len(CHUNKS)


def rows_of(x, count=1):
    if isinstance(x, int):
        return pl.ds(x * CY, count * CY)
    return pl.ds(pl.multiple_of(x * CY, CY), count * CY)


def lanes():
    return lax.broadcasted_iota(jnp.int32, (CY, NZ), 1)


def sublanes():
    return lax.broadcasted_iota(jnp.int32, (CY, NZ), 0)


def z_up(a):
    return jnp.where(lanes() == NZ - 1, 0.0, pltpu.roll(a, NZ - 1, 1))


def z_down(a):
    return jnp.where(lanes() == 0, 0.0, pltpu.roll(a, 1, 1))


def y_up(a, row):
    return jnp.where(sublanes() == CY - 1, jnp.broadcast_to(row, (CY, NZ)), pltpu.roll(a, CY - 1, 0))


def y_down(a, row):
    return jnp.where(sublanes() == 0, jnp.broadcast_to(row, (CY, NZ)), pltpu.roll(a, 1, 0))


def sig(v):
    return 1.0 / (1.0 + jnp.exp(-v))


def split3(a):
    high = a.astype(BF16)
    rest = a - high.astype(F32)
    mid = rest.astype(BF16)
    low = (rest - mid.astype(F32)).astype(BF16)
    return high, mid, low


def kernel(n_gx, sec_ref, ang_ref, cls_ref, rmap_ref, irow_ref, out_ref,
           inp, ext0, ext1, fib, base, outb, clsx, tbuf, trow, perm, parts, rperm, tie, tbl,
           halo, ypk, corner_out, corner_in, hal, kx, ang, cls, rmap, irow,
           load_sem, send_sem, recv_sem, out_sem):
    sec, gx, gy = lax.axis_index("sec"), lax.axis_index("gx"), lax.axis_index("gy")
    left, right = lax.rem(gx + n_gx - 1, n_gx), lax.rem(gx + 1, n_gx)
    across = 1 - gy
    near = {
        LEFT: (sec, left, gy), RIGHT: (sec, right, gy), ACROSS: (sec, gx, across),
        DIAG_LEFT: (sec, left, across), DIAG_RIGHT: (sec, right, across),
    }
    near[STIFF_LEFT], near[STIFF_RIGHT] = near[LEFT], near[RIGHT]
    partner = (1 - sec, gx, gy)
    ext = (ext0, ext1)

    barrier = pltpu.get_barrier_semaphore()
    for direction in range(5):
        pl.semaphore_signal(barrier, inc=1, device_id=near[direction], device_id_type=MESH)

    def load(src, dst, slot):
        return pltpu.make_async_copy(src, dst, load_sem.at[slot])

    def remote(src, dst, slot, device):
        return pltpu.make_async_remote_copy(
            src_ref=src, dst_ref=dst, send_sem=send_sem.at[slot], recv_sem=recv_sem.at[slot],
            device_id=device, device_id_type=MESH)

    def store(rows, first, count, slot):
        part = pl.ds(first, count)
        return pltpu.make_async_copy(outb.at[part, rows], out_ref.at[part, rows], out_sem.at[slot])

    def halo_copies(phase, fields):
        first, own = pl.ds(0, fields), ext[phase]
        if phase == 0:
            low, high = sec_ref.at[first, pl.ds(0, CY)], sec_ref.at[first, pl.ds(COLS - CY, CY)]
        else:
            low, high = own.at[first, pl.ds(CY, CY)], own.at[first, pl.ds(COLS, CY)]
        both = pl.ds(0, 2 * fields)
        slot = phase * 8
        return (
            remote(low, own.at[first, pl.ds(TOP, CY)], slot + LEFT, near[LEFT]),
            remote(high, own.at[first, pl.ds(0, CY)], slot + RIGHT, near[RIGHT]),
            remote(ypk.at[phase, both], halo.at[phase, both, pl.ds(8, CX)], slot + ACROSS, near[ACROSS]),
            remote(corner_out.at[phase, 0], corner_in.at[phase, 1], slot + DIAG_LEFT, near[DIAG_LEFT]),
            remote(corner_out.at[phase, 1], corner_in.at[phase, 0], slot + DIAG_RIGHT, near[DIAG_RIGHT]),
        )

    def pack_corners(phase, fields):
        for k in range(2 * fields):
            corner_out[phase, 0, k:k + 1] = ypk[phase, k, 0:1]
            corner_out[phase, 1, k:k + 1] = ypk[phase, k, CX - 1:CX]

    def pack_rows(phase, fields):
        for field in range(fields):
            ypk[phase, field] = ext[phase][field, pl.ds(CY + CY - 1, CX, stride=CY)]
            ypk[phase, fields + field] = ext[phase][field, pl.ds(CY, CX, stride=CY)]

    def unpack_corners(phase, fields):
        for k in range(2 * fields):
            halo[phase, k, 7:8] = corner_in[phase, 0, k:k + 1]
            halo[phase, k, 8 + CX:9 + CX] = corner_in[phase, 1, k:k + 1]

    def halo_row(phase, k):
        return halo[phase, k, 8:8 + CX]

    def halo_diff(phase, k):
        return halo[phase, k, 9:9 + CX] - halo[phase, k, 7:7 + CX]

    def row_at(k, x):
        return hal[k, pl.ds(x, 1)]

    def fiber_table():
        azimuth, elevation = ang[:, 0:1], ang[:, 1:2]
        flat = jnp.cos(elevation)
        for k, value in enumerate((jnp.cos(azimuth) * flat, jnp.sin(azimuth) * flat, jnp.sin(elevation))):
            tbl[k] = jnp.broadcast_to(value, (CLASSES, NZ))

    def expand_classes():
        spread = lax.broadcasted_iota(jnp.int32, (8, NZ), 1) // 16 == lax.broadcasted_iota(jnp.int32, (8, NZ), 0)
        spread = jnp.where(spread, 1.0, 0.0).astype(BF16)
        clsx[...] = jnp.dot(cls[...].astype(F32).astype(BF16), spread, preferred_element_type=F32)

    def fiber_of(x):
        kind = clsx[rows_of(x)]
        bit2 = kind >= 3.5
        kind = jnp.where(bit2, kind - 4.0, kind)
        bit1 = kind >= 1.5
        bit0 = jnp.where(bit1, kind - 2.0, kind) >= 0.5
        fields = []
        for k in range(3):
            pick = [jnp.broadcast_to(tbl[k, c:c + 1], (CY, NZ)) for c in range(CLASSES)]
            pick = [jnp.where(bit0, pick[2 * c + 1], pick[2 * c]) for c in range(4)]
            pick = [jnp.where(bit1, pick[2 * c + 1], pick[2 * c]) for c in range(2)]
            fields.append(jnp.where(bit2, pick[1], pick[0]))
        return fields


    @pl.when(sec == 0)
    def _():
        loads = [load(sec_ref.at[0], ext0.at[0, pl.ds(CY, COLS)], 0)]
        loads += [load(sec_ref.at[k], inp.at[k], k) for k in range(1, 8)]
        load_map = load(rmap_ref, rmap, 8)
        load_cls = load(cls_ref, cls, 9)
        load_ang = load(ang_ref, ang, 10)
        load_map.start()
        for k in (0, 1, 2, 3, 6, 7, 4, 5):
            loads[k].start()
        load_cls.start()
        load_ang.start()

        load_map.wait()
        source = jnp.broadcast_to(rmap[0].astype(F32), (8, COLS)).T[:, 0:1]
        spot = lax.broadcasted_iota(jnp.int32, (COLS, COLS), 1).astype(F32)
        perm[...] = jnp.where(jnp.broadcast_to(source, (COLS, COLS)) == spot, 1.0, 0.0).astype(BF16)

        loads[0].wait()
        pack_rows(0, 1)
        pack_corners(0, 1)
        pl.semaphore_wait(barrier, 6)
        first_halo = halo_copies(0, 1)
        for copy in first_halo:
            copy.start()

        for k in (1, 2, 3, 6, 7):
            loads[k].wait()

        def tension_plane(x, carry):
            rows = rows_of(x)
            v = ext0[0, rows_of(x + 1)]
            c, d, f, b, s = inp[1, rows], inp[2, rows], inp[3, rows], inp[6, rows], inp[7, rows]
            square = c * c
            q = square / (square + 0.25)
            flow = 1.2 * d * f * (v - 2.0)
            binding = 2.0 * c * (1.0 - b) - 0.4 * b
            c = c + DT * (-0.3 * flow - 0.5 * c - binding)
            base[0, rows] = c
            base[1, rows] = q
            base[2, rows] = flow
            inp[6, rows] = b + DT * binding
            s = s + DT * (q - s) / 2.0
            square = c * c
            q = square / (square + 0.25)
            outb[1, rows] = q
            s = s + DT * (q - s) / 2.0
            outb[3, rows] = s
            for k, part in enumerate(split3(s)):
                parts[rows, k * NZ:(k + 1) * NZ] = part
            return carry

        lax.fori_loop(0, CX, tension_plane, 0)
        moved = jnp.dot(perm[...], parts[...], preferred_element_type=F32)
        tbuf[...] = moved[:, 0:NZ] + (moved[:, NZ:2 * NZ] + moved[:, 2 * NZ:])
        trow[0] = tbuf[pl.ds(CY - 1, CX, stride=CY)]
        trow[1] = tbuf[pl.ds(0, CX, stride=CY)]
        tension = [
            remote(tbuf.at[rows_of(0)], tbuf.at[rows_of(0)], TEN_FIRST, partner),
            remote(tbuf.at[rows_of(CX - 1)], tbuf.at[rows_of(CX - 1)], TEN_LAST, partner),
            remote(trow, trow, TEN_ROWS, partner),
        ]
        for k, ((low, high), _) in enumerate(CHUNKS):
            rows = rows_of(low, high - low)
            tension.append(remote(tbuf.at[rows], tbuf.at[rows], TEN_BULK + k, partner))
        for copy in tension:
            copy.start()
        everything = pl.ds(0, COLS)
        out_s = store(everything, 3, 1, 0)
        out_s.start()

        load_ang.wait()
        load_cls.wait()
        fiber_table()
        expand_classes()

        def fiber_plane(x, carry):
            for k, value in enumerate(fiber_of(x)):
                fib[k, rows_of(x)] = value
            return carry

        lax.fori_loop(0, CX, fiber_plane, 0)

        def diffusion(phase, x):
            here = ext[phase]
            c, p, m = here[0, rows_of(x + 1)], here[0, rows_of(x + 2)], here[0, rows_of(x)]
            f0, f1, f2 = fib[0, rows_of(x)], fib[1, rows_of(x)], fib[2, rows_of(x)]
            d = p - m
            yu, yd = y_up(c, row_at(0, x)), y_down(c, row_at(1, x))
            e = yu - yd
            twice = 2.0 * c
            v00 = p + m - twice
            v11 = yu + yd - twice
            v22 = z_up(c) + z_down(c) - twice
            x01 = y_up(d, row_at(2, x)) - y_down(d, row_at(3, x))
            x02 = z_up(d) - z_down(d)
            x12 = z_up(e) - z_down(e)
            along = (f0 * (f0 * v00 + 0.5 * (f1 * x01 + f2 * x02))
                     + f1 * (f1 * v11 + 0.5 * (f2 * x12)) + f2 * f2 * v22)
            return c, 0.25 * (v00 + v11 + v22) + 0.75 * along

        def halo_rows(phase):
            unpack_corners(phase, 1)
            hal[0] = halo_row(phase, 1)
            hal[1] = halo_row(phase, 0)
            hal[2] = halo_diff(phase, 1)
            hal[3] = halo_diff(phase, 0)

        loads[4].wait()
        loads[5].wait()
        for copy in first_halo:
            copy.wait_recv()
        halo_rows(0)

        def first_step(x, carry):
            rows = rows_of(x)
            v, spread = diffusion(0, x)
            d, f, n, r = inp[2, rows], inp[3, rows], inp[4, rows], inp[5, rows]
            flow, q = base[2, rows], base[1, rows]
            current = flow + 0.8 * n * (v + 1.0) + 0.6 * q * r * (v + 1.0) + 0.1 * v
            ext1[0, rows_of(x + 1)] = v + DT * (spread - current)
            inp[2, rows] = d + DT * (sig(2.0 * v + 1.0) - d) / 0.5
            inp[3, rows] = f + DT * (sig(-2.0 * v) - f) / 3.0
            inp[4, rows] = n + DT * (sig(2.0 * v) - n)
            inp[5, rows] = r + DT * (sig(v - 0.5) - r) / 5.0
            return carry

        lax.fori_loop(0, CX, first_step, 0)
        pack_rows(1, 1)
        pack_corners(1, 1)
        second_halo = halo_copies(1, 1)
        for copy in second_halo:
            copy.start()

        def second_ions(x, carry):
            rows = rows_of(x)
            v, c, q = ext1[0, rows_of(x + 1)], base[0, rows], outb[1, rows]
            d, f, n, r, b = inp[2, rows], inp[3, rows], inp[4, rows], inp[5, rows], inp[6, rows]
            flow = 1.2 * d * f * (v - 2.0)
            current = flow + 0.8 * n * (v + 1.0) + 0.6 * q * r * (v + 1.0) + 0.1 * v
            binding = 2.0 * c * (1.0 - b) - 0.4 * b
            base[1, rows] = v - DT * current
            outb[1, rows] = c + DT * (-0.3 * flow - 0.5 * c - binding)
            outb[2, rows] = n + DT * (sig(2.0 * v) - n)
            return carry

        lax.fori_loop(0, CX, second_ions, 0)
        out_ions = store(everything, 1, 2, 1)
        out_ions.start()
        for copy in second_halo:
            copy.wait_recv()
        halo_rows(1)

        def second_step(x, carry):
            rows = rows_of(x)
            _, spread = diffusion(1, x)
            outb[0, rows] = base[1, rows] + DT * spread
            return carry

        lax.fori_loop(0, CX, second_step, 0)
        out_v = store(everything, 0, 1, 2)
        out_v.start()
        for copy in (*first_halo, *second_halo, *tension):
            copy.wait_send()
        for copy in (out_s, out_ions, out_v):
            copy.wait()


    @pl.when(sec == 1)
    def _():
        pl.semaphore_signal(barrier, inc=1, device_id=partner, device_id_type=MESH)
        load_u = load(sec_ref.at[pl.ds(0, 3)], ext0.at[:, pl.ds(CY, COLS)], 0)
        load_rest = load(sec_ref.at[pl.ds(3, 5)], inp.at[pl.ds(3, 5)], 1)
        load_row = load(irow_ref, irow, 8)
        load_cls = load(cls_ref, cls, 9)
        load_ang = load(ang_ref, ang, 10)
        load_u.start()
        load_ang.start()
        load_cls.start()
        load_rest.start()
        load_row.start()

        pl.semaphore_wait(barrier, 5)
        first_halo = halo_copies(0, 3)
        stiff = (
            remote(sec_ref.at[6, pl.ds(0, CY)], kx.at[1], STIFF_LEFT, near[STIFF_LEFT]),
            remote(sec_ref.at[6, pl.ds(COLS - CY, CY)], kx.at[0], STIFF_RIGHT, near[STIFF_RIGHT]),
        )
        for copy in (first_halo[0], first_halo[1], *stiff):
            copy.start()
        load_u.wait()
        pack_rows(0, 3)
        pack_corners(0, 3)
        for copy in first_halo[2:]:
            copy.start()

        load_ang.wait()
        load_cls.wait()
        fiber_table()
        expand_classes()
        load_row.wait()
        for side in range(2):
            source = jnp.broadcast_to(irow[side, 0].astype(F32), (CY, CY)).T
            spot = lax.broadcasted_iota(jnp.int32, (CY, CY), 1).astype(F32)
            rperm[side] = jnp.where(source == spot, 1.0, 0.0).astype(BF16)
        load_rest.wait()

        def weight_plane(x, carry):
            rows = rows_of(x)
            relax = 0.06 / inp[6, rows]
            inp[6, rows] = relax
            drive = relax * inp[7, rows]
            for k, value in enumerate(fiber_of(x)):
                fib[k, rows] = drive * value
                inp[3 + k, rows] = relax * inp[3 + k, rows]
            return carry

        kx_own = (0, CX - 1)
        lax.fori_loop(0, CX, weight_plane, 0)

        def halo_rows(phase):
            unpack_corners(phase, 3)
            for side, sign in ((1, 0.5), (0, -0.5)):
                k = 3 * side
                at = 4 * (1 - side)
                hal[at] = halo_row(phase, k) + sign * halo_diff(phase, k + 1)
                hal[at + 1] = 3.0 * halo_row(phase, k + 1) + sign * halo_diff(phase, k)
                hal[at + 2] = halo_row(phase, k + 1)
                hal[at + 3] = halo_row(phase, k + 2)

        def relaxed(phase, x):
            here = ext[phase]
            mid, p, m = rows_of(x + 1), rows_of(x + 2), rows_of(x)
            c0, c1, c2 = here[0, mid], here[1, mid], here[2, mid]
            p0, p1, p2 = here[0, p], here[1, p], here[2, p]
            m0, m1, m2 = here[0, m], here[1, m], here[2, m]
            d0, d1, d2 = 0.5 * (p0 - m0), 0.5 * (p1 - m1), 0.5 * (p2 - m2)
            y2u, y2d = y_up(c2, row_at(3, x)), y_down(c2, row_at(7, x))
            e1 = 0.5 * (y_up(c1, row_at(2, x)) - y_down(c1, row_at(6, x)))
            e2 = 0.5 * (y2u - y2d)
            t1, t2 = 3.0 * c1, 3.0 * c2
            cross = d0 + e1
            s0 = (3.0 * (p0 + m0) + (y_up(c0 + d1, row_at(0, x)) + y_down(c0 - d1, row_at(4, x)))
                  + (z_up(c0 + d2) + z_down(c0 - d2)))
            s1 = ((p1 + m1) + (y_up(t1 + d0, row_at(1, x)) + y_down(t1 - d0, row_at(5, x)))
                  + (z_up(c1 + e2) + z_down(c1 - e2)))
            s2 = (p2 + m2) + (y2u + y2d) + (z_up(t2 + cross) + z_down(t2 - cross))
            return 0.4 * c0 + 0.06 * s0, 0.4 * c1 + 0.06 * s1, 0.4 * c2 + 0.06 * s2

        def tie_forces(phase):
            here = ext[phase]
            for side in range(2):
                far = pl.ds((0, TOP)[side], CY)
                pieces = []
                for k in range(3):
                    pieces += list(split3((2.0 * kx[side]) * here[k, far]))
                got = jnp.dot(rperm[side], jnp.concatenate(pieces, axis=1), preferred_element_type=F32)
                x = kx_own[side]
                relax = inp[6, rows_of(x)]
                for k in range(3):
                    at = 3 * NZ * k
                    picked = got[:, at:at + NZ] + (got[:, at + NZ:at + 2 * NZ] + got[:, at + 2 * NZ:at + 3 * NZ])
                    tie[side, k] = relax * picked - 0.12 * here[k, rows_of(x + 1)]

        for copy in (*first_halo, *stiff):
            copy.wait_recv()
        halo_rows(0)

        def base_plane(x, carry):
            rows = rows_of(x)
            for k, value in enumerate(relaxed(0, x)):
                base[k, rows] = value + inp[3 + k, rows]
            return carry

        lax.fori_loop(0, CX, base_plane, 0)
        tie_forces(0)
        for side in range(2):
            rows = rows_of(kx_own[side])
            for k in range(3):
                base[k, rows] = base[k, rows] + tie[side, k]

        def receive(slot, ref):
            remote(ref, ref, slot, partner).wait_recv()

        def activate(x):
            rows = rows_of(x)
            tension = tbuf[rows]
            outb[3, rows] = inp[7, rows] * tension
            for k in range(3):
                ext1[k, rows_of(x + 1)] = base[k, rows] + fib[k, rows] * tension

        second_halo = halo_copies(1, 3)
        stores = []
        for side, slot in ((0, TEN_FIRST), (1, TEN_LAST)):
            x = kx_own[side]
            receive(slot, tbuf.at[rows_of(x)])
            activate(x)
            second_halo[side].start()
            stores.append(store(rows_of(x), 3, 1, side))
            stores[-1].start()
        receive(TEN_ROWS, trow)
        for side, y in ((0, CY - 1), (1, 0)):
            for k in range(3):
                own = pl.ds(y, CX, stride=CY)
                ypk[1, 3 * side + k] = base[k, own] + fib[k, own] * trow[side]
        pack_corners(1, 3)
        for copy in second_halo[2:]:
            copy.start()

        def activate_plane(x, carry):
            activate(x)
            return carry

        def last_plane(x, carry):
            rows = rows_of(x)
            tension = tbuf[rows]
            for k, value in enumerate(relaxed(1, x)):
                outb[k, rows] = value + inp[3 + k, rows] + fib[k, rows] * tension
            return carry

        slot = 2
        for index, ((low, high), ready) in enumerate(CHUNKS):
            rows = rows_of(low, high - low)
            receive(TEN_BULK + index, tbuf.at[rows])
            lax.fori_loop(low, high, activate_plane, 0)
            stores.append(store(rows, 3, 1, slot))
            stores[-1].start()
            slot += 1
            if index == 0:
                for copy in second_halo:
                    copy.wait_recv()
                halo_rows(1)
                tie_forces(1)
            for low, high in ready:
                rows = rows_of(low, high - low)
                lax.fori_loop(low, high, last_plane, 0)
                if low in kx_own:
                    side = kx_own.index(low)
                    for k in range(3):
                        outb[k, rows] = outb[k, rows] + tie[side, k]
                stores.append(store(rows, 0, 3, slot))
                stores[-1].start()
                slot += 1
        for copy in (*first_halo, *second_halo, *stiff):
            copy.wait_send()
        for copy in stores:
            copy.wait()


def solution(mesh):
    n_gx = mesh.shape["gx"]

    def local(sections, fiber_angles, fiber_class, row_map, interface_rows):
        vmem = pltpu.VMEM
        field, padded = (COLS, NZ), (EXT, NZ)
        out = pl.pallas_call(
            functools.partial(kernel, n_gx),
            out_shape=jax.ShapeDtypeStruct((4, COLS, NZ), F32),
            in_specs=[pl.BlockSpec(memory_space=pl.ANY)] * 5,
            out_specs=pl.BlockSpec(memory_space=pl.ANY),
            scratch_shapes=[
                vmem((8, *field), F32),
                vmem((3, *padded), F32),
                vmem((3, *padded), F32),
                vmem((3, *field), F32),
                vmem((3, *field), F32),
                vmem((4, *field), F32),
                vmem(field, F32),
                vmem(field, F32),
                vmem((2, CX, NZ), F32),
                vmem((COLS, COLS), BF16),
                vmem((COLS, 3 * NZ), BF16),
                vmem((2, CY, CY), BF16),
                vmem((2, 3, CY, NZ), F32),
                vmem((3, CLASSES, NZ), F32),
                vmem((2, 6, 32, NZ), F32),
                vmem((2, 6, CX, NZ), F32),
                vmem((2, 2, 8, NZ), F32),
                vmem((2, 2, 8, NZ), F32),
                vmem((8, CX, NZ), F32),
                vmem((2, CY, NZ), F32),
                vmem((CLASSES, 2), F32),
                vmem((COLS, 8), jnp.int32),
                vmem((1, 1, COLS), jnp.int32),
                vmem((2, 1, 1, CY), jnp.int32),
                pltpu.SemaphoreType.DMA((11,)),
                pltpu.SemaphoreType.DMA((N_COPIES,)),
                pltpu.SemaphoreType.DMA((N_COPIES,)),
                pltpu.SemaphoreType.DMA((16,)),
            ],
            compiler_params=pltpu.CompilerParams(
                collective_id=0, has_side_effects=True, vmem_limit_bytes=24 * 1024 * 1024),
        )(
            sections.reshape(8, COLS, NZ), fiber_angles, fiber_class.reshape(COLS, 8), row_map, interface_rows
        )
        return out.reshape(1, 4, CX, CY, NZ)

    in_specs = (
        P("sec", None, "gx", "gy", None),
        P(),
        P("gx", "gy", None),
        P("gx", "gy", None),
        P(None, "gx", "gy", None),
    )
    out_specs = P("sec", None, "gx", "gy", None)
    return jax.shard_map(local, mesh=mesh, in_specs=in_specs, out_specs=out_specs, check_vma=False)
```

```python
import functools

import jax
import jax.numpy as jnp
from jax import lax
from jax.experimental import pallas as pl
from jax.experimental.pallas import tpu as pltpu
from jax.sharding import PartitionSpec as P

MESH = pl.DeviceIdType.MESH
F32, BF16 = jnp.float32, jnp.bfloat16

CX, CY, NZ = 16, 32, 128
COLS = CX * CY
TOP = COLS + CY
EXT = COLS + 2 * CY
CLASSES = 8
DT = 0.1

CHUNKS = (((1, 5), (1, 4)), ((5, 9), (4, 8)), ((9, 13), (8, 12)), ((13, 15), (12, 14)))

LEFT, RIGHT, ACROSS, DIAG_LEFT, DIAG_RIGHT, STIFF_LEFT, STIFF_RIGHT = range(7)
TEN_FIRST, TEN_LAST, TEN_ROWS, TEN_BULK = 16, 17, 18, 19
N_COPIES = TEN_BULK + len(CHUNKS)
ENDS = (0, CX - 1)


def rows_of(x, count=1):
    if isinstance(x, int):
        return pl.ds(x * CY, count * CY)
    return pl.ds(pl.multiple_of(x * CY, CY), count * CY)


def lanes():
    return lax.broadcasted_iota(jnp.int32, (CY, NZ), 1)


def sublanes():
    return lax.broadcasted_iota(jnp.int32, (CY, NZ), 0)


def z_up(a):
    return jnp.where(lanes() == NZ - 1, 0.0, pltpu.roll(a, NZ - 1, 1))


def z_down(a):
    return jnp.where(lanes() == 0, 0.0, pltpu.roll(a, 1, 1))


def y_up(a, row):
    return jnp.where(sublanes() == CY - 1, jnp.broadcast_to(row, (CY, NZ)), pltpu.roll(a, CY - 1, 0))


def y_down(a, row):
    return jnp.where(sublanes() == 0, jnp.broadcast_to(row, (CY, NZ)), pltpu.roll(a, 1, 0))


def sig(v):
    return 1.0 / (1.0 + jnp.exp(-v))


def split3(a):
    high = a.astype(BF16)
    rest = a - high.astype(F32)
    mid = rest.astype(BF16)
    low = (rest - mid.astype(F32)).astype(BF16)
    return high, mid, low


def kernel(n_gx, sec_ref, ang_ref, cls_ref, rmap_ref, irow_ref, out_ref,
           inp, ext0, ext1, fib, base, packed, tbuf, trow, perm, parts, rperm, tie,
           halo, ypk, corner_out, corner_in, hal, kx, ang, cls, rmap, irow,
           load_sem, send_sem, recv_sem):
    sec, gx, gy = lax.axis_index("sec"), lax.axis_index("gx"), lax.axis_index("gy")
    left, right = lax.rem(gx + n_gx - 1, n_gx), lax.rem(gx + 1, n_gx)
    across = 1 - gy
    near = {
        LEFT: (sec, left, gy), RIGHT: (sec, right, gy), ACROSS: (sec, gx, across),
        DIAG_LEFT: (sec, left, across), DIAG_RIGHT: (sec, right, across),
    }
    near[STIFF_LEFT], near[STIFF_RIGHT] = near[LEFT], near[RIGHT]
    partner = (1 - sec, gx, gy)
    ext = (ext0, ext1)

    barrier = pltpu.get_barrier_semaphore()
    for direction in range(5):
        pl.semaphore_signal(barrier, inc=1, device_id=near[direction], device_id_type=MESH)

    def load(src, dst, slot):
        return pltpu.make_async_copy(src, dst, load_sem.at[slot])

    def remote(src, dst, slot, device):
        return pltpu.make_async_remote_copy(
            src_ref=src, dst_ref=dst, send_sem=send_sem.at[slot], recv_sem=recv_sem.at[slot],
            device_id=device, device_id_type=MESH)

    def halo_copies(phase, fields):
        first, own = pl.ds(0, fields), ext[phase]
        if phase == 0:
            low, high = sec_ref.at[first, pl.ds(0, CY)], sec_ref.at[first, pl.ds(COLS - CY, CY)]
        else:
            low, high = own.at[first, pl.ds(CY, CY)], own.at[first, pl.ds(COLS, CY)]
        both = pl.ds(0, 2 * fields)
        slot = phase * 8
        return (
            remote(low, own.at[first, pl.ds(TOP, CY)], slot + LEFT, near[LEFT]),
            remote(high, own.at[first, pl.ds(0, CY)], slot + RIGHT, near[RIGHT]),
            remote(ypk.at[phase, both], halo.at[phase, both, pl.ds(8, CX)], slot + ACROSS, near[ACROSS]),
            remote(corner_out.at[phase, 0], corner_in.at[phase, 1], slot + DIAG_LEFT, near[DIAG_LEFT]),
            remote(corner_out.at[phase, 1], corner_in.at[phase, 0], slot + DIAG_RIGHT, near[DIAG_RIGHT]),
        )

    def pack_corners(phase, fields, side):
        for k in range(fields):
            for part, y in ((0, CY - 1), (1, 0)):
                row = CY + ENDS[side] * CY + y
                at = part * fields + k
                corner_out[phase, side, at:at + 1] = ext[phase][k, row:row + 1]

    def pack_rows(phase, fields):
        for field in range(fields):
            ypk[phase, field] = ext[phase][field, pl.ds(CY + CY - 1, CX, stride=CY)]
            ypk[phase, fields + field] = ext[phase][field, pl.ds(CY, CX, stride=CY)]

    def wait_side(copies, side):
        copies[1 - side].wait_recv()
        copies[DIAG_RIGHT - side].wait_recv()

    def unpack_corners(phase, fields, side):
        row = (7, 8 + CX)[side]
        for k in range(2 * fields):
            halo[phase, k, row:row + 1] = corner_in[phase, side, k:k + 1]

    def halo_row(phase, k):
        return halo[phase, k, 8:8 + CX]

    def halo_diff(phase, k):
        return halo[phase, k, 9:9 + CX] - halo[phase, k, 7:7 + CX]

    def row_at(k, x):
        return hal[k, pl.ds(x, 1)]

    def pack_fibers():
        azimuth, elevation = ang[0:1, :], ang[1:2, :]
        flat = jnp.cos(elevation)
        table = (jnp.cos(azimuth) * flat, jnp.sin(azimuth) * flat, jnp.sin(elevation))
        kind = cls[...].astype(F32).T
        for k, value in enumerate(table):
            total = jnp.broadcast_to(value[:, 0:1], (CY, NZ))
            for c in range(1, CLASSES):
                total = jnp.where(kind == float(c), jnp.broadcast_to(value[:, c:c + 1], (CY, NZ)), total)
            packed[k] = total

    def fiber_of(x):
        place = lanes() // 16 + 8 * x
        return [jnp.take_along_axis(packed[k], place, axis=1) for k in range(3)]


    @pl.when(sec == 0)
    def _():
        loads = [load(sec_ref.at[0], ext0.at[0, pl.ds(CY, COLS)], 0)]
        loads += [load(sec_ref.at[k], inp.at[k], k) for k in range(1, 8)]
        load_map = load(rmap_ref, rmap, 8)
        load_cls = load(cls_ref, cls, 9)
        load_ang = load(ang_ref, ang, 10)
        load_map.start()
        for k in (0, 1, 2, 3, 6, 7):
            loads[k].start()
        load_cls.start()
        load_ang.start()
        loads[4].start()
        loads[5].start()

        load_map.wait()
        source = jnp.broadcast_to(rmap[0].astype(F32), (8, COLS)).T[:, 0:1]
        spot = lax.broadcasted_iota(jnp.int32, (COLS, COLS), 1).astype(F32)
        perm[...] = jnp.where(jnp.broadcast_to(source, (COLS, COLS)) == spot, 1.0, 0.0).astype(BF16)

        for k in (0, 1, 2, 3, 6, 7):
            loads[k].wait()

        def tension_plane(x, carry):
            rows = rows_of(x)
            v = ext0[0, rows_of(x + 1)]
            c, d, f, b, s = inp[1, rows], inp[2, rows], inp[3, rows], inp[6, rows], inp[7, rows]
            square = c * c
            q = square / (square + 0.25)
            flow = 1.2 * d * f * (v - 2.0)
            binding = 2.0 * c * (1.0 - b) - 0.4 * b
            c = c + DT * (-0.3 * flow - 0.5 * c - binding)
            base[0, rows] = c
            base[1, rows] = q
            base[2, rows] = flow
            inp[6, rows] = b + DT * binding
            s = s + DT * (q - s) / 2.0
            square = c * c
            q = square / (square + 0.25)
            out_ref[1, rows] = q
            s = s + DT * (q - s) / 2.0
            out_ref[3, rows] = s
            for k, part in enumerate(split3(s)):
                parts[rows, k * NZ:(k + 1) * NZ] = part
            return carry

        lax.fori_loop(0, CX, tension_plane, 0)

        def permuted(low, high):
            moved = jnp.dot(perm[low * CY:high * CY], parts[...], preferred_element_type=F32)
            tbuf[low * CY:high * CY] = moved[:, 0:NZ] + (moved[:, NZ:2 * NZ] + moved[:, 2 * NZ:])

        permuted(CX - 1, CX)
        permuted(0, CX - 1)
        trow[0] = tbuf[pl.ds(CY - 1, CX, stride=CY)]
        trow[1] = tbuf[pl.ds(0, CX, stride=CY)]
        pack_rows(0, 1)
        pack_corners(0, 1, 0)
        pack_corners(0, 1, 1)

        pl.semaphore_wait(barrier, 6)
        first_halo = halo_copies(0, 1)
        for copy in first_halo:
            copy.start()
        tension = [
            remote(tbuf.at[rows_of(CX - 1)], tbuf.at[rows_of(CX - 1)], TEN_LAST, partner),
            remote(tbuf.at[rows_of(0)], tbuf.at[rows_of(0)], TEN_FIRST, partner),
            remote(trow, trow, TEN_ROWS, partner),
        ]
        for k, ((low, high), _) in enumerate(CHUNKS):
            rows = rows_of(low, high - low)
            tension.append(remote(tbuf.at[rows], tbuf.at[rows], TEN_BULK + k, partner))
        for copy in tension:
            copy.start()

        load_ang.wait()
        load_cls.wait()
        pack_fibers()

        def fiber_plane(x, carry):
            for k, value in enumerate(fiber_of(x)):
                fib[k, rows_of(x)] = value
            return carry

        lax.fori_loop(0, CX, fiber_plane, 0)

        def diffusion(phase, x):
            here = ext[phase]
            c, p, m = here[0, rows_of(x + 1)], here[0, rows_of(x + 2)], here[0, rows_of(x)]
            f0, f1, f2 = fib[0, rows_of(x)], fib[1, rows_of(x)], fib[2, rows_of(x)]
            d = p - m
            yu, yd = y_up(c, row_at(0, x)), y_down(c, row_at(1, x))
            e = yu - yd
            twice = 2.0 * c
            v00 = p + m - twice
            v11 = yu + yd - twice
            v22 = z_up(c) + z_down(c) - twice
            x01 = y_up(d, row_at(2, x)) - y_down(d, row_at(3, x))
            x02 = z_up(d) - z_down(d)
            x12 = z_up(e) - z_down(e)
            along = (f0 * (f0 * v00 + 0.5 * (f1 * x01 + f2 * x02))
                     + f1 * (f1 * v11 + 0.5 * (f2 * x12)) + f2 * f2 * v22)
            return c, 0.25 * (v00 + v11 + v22) + 0.75 * along

        def halo_rows(phase):
            hal[0] = halo_row(phase, 1)
            hal[1] = halo_row(phase, 0)
            hal[2] = halo_diff(phase, 1)
            hal[3] = halo_diff(phase, 0)

        loads[4].wait()
        loads[5].wait()

        def first_step(x, carry):
            rows = rows_of(x)
            v, spread = diffusion(0, x)
            d, f, n, r = inp[2, rows], inp[3, rows], inp[4, rows], inp[5, rows]
            flow, q = base[2, rows], base[1, rows]
            current = flow + 0.8 * n * (v + 1.0) + 0.6 * q * r * (v + 1.0) + 0.1 * v
            ext1[0, rows_of(x + 1)] = v + DT * (spread - current)
            inp[2, rows] = d + DT * (sig(2.0 * v + 1.0) - d) / 0.5
            inp[3, rows] = f + DT * (sig(-2.0 * v) - f) / 3.0
            inp[4, rows] = n + DT * (sig(2.0 * v) - n)
            inp[5, rows] = r + DT * (sig(v - 0.5) - r) / 5.0
            return carry

        first_halo[ACROSS].wait_recv()
        halo_rows(0)
        lax.fori_loop(1, CX - 1, first_step, 0)
        second_halo = halo_copies(1, 1)
        for side in (1, 0):
            wait_side(first_halo, side)
            unpack_corners(0, 1, side)
            halo_rows(0)
            first_step(ENDS[side], 0)
            pack_corners(1, 1, side)
            second_halo[side].start()
            second_halo[DIAG_LEFT + side].start()
        pack_rows(1, 1)
        second_halo[ACROSS].start()

        def second_ions(x, carry):
            rows = rows_of(x)
            v, c, q = ext1[0, rows_of(x + 1)], base[0, rows], out_ref[1, rows]
            d, f, n, r, b = inp[2, rows], inp[3, rows], inp[4, rows], inp[5, rows], inp[6, rows]
            flow = 1.2 * d * f * (v - 2.0)
            current = flow + 0.8 * n * (v + 1.0) + 0.6 * q * r * (v + 1.0) + 0.1 * v
            binding = 2.0 * c * (1.0 - b) - 0.4 * b
            base[1, rows] = v - DT * current
            out_ref[1, rows] = c + DT * (-0.3 * flow - 0.5 * c - binding)
            out_ref[2, rows] = n + DT * (sig(2.0 * v) - n)
            return carry

        lax.fori_loop(0, CX, second_ions, 0)

        def second_step(x, carry):
            rows = rows_of(x)
            _, spread = diffusion(1, x)
            out_ref[0, rows] = base[1, rows] + DT * spread
            return carry

        second_halo[ACROSS].wait_recv()
        halo_rows(1)
        lax.fori_loop(1, CX - 1, second_step, 0)
        for side in (1, 0):
            wait_side(second_halo, side)
            unpack_corners(1, 1, side)
            halo_rows(1)
            second_step(ENDS[side], 0)
        for copy in (*first_halo, *second_halo, *tension):
            copy.wait_send()


    @pl.when(sec == 1)
    def _():
        pl.semaphore_signal(barrier, inc=1, device_id=partner, device_id_type=MESH)
        load_u = load(sec_ref.at[pl.ds(0, 3)], ext0.at[:, pl.ds(CY, COLS)], 0)
        load_rest = load(sec_ref.at[pl.ds(3, 5)], inp.at[pl.ds(3, 5)], 1)
        load_row = load(irow_ref, irow, 8)
        load_cls = load(cls_ref, cls, 9)
        load_ang = load(ang_ref, ang, 10)
        load_ang.start()
        load_cls.start()
        load_row.start()
        load_rest.start()
        load_u.start()

        load_ang.wait()
        load_cls.wait()
        pack_fibers()
        load_row.wait()
        for side in range(2):
            source = jnp.broadcast_to(irow[side, 0].astype(F32), (CY, CY)).T
            spot = lax.broadcasted_iota(jnp.int32, (CY, CY), 1).astype(F32)
            rperm[side] = jnp.where(source == spot, 1.0, 0.0).astype(BF16)
        load_rest.wait()

        def weight_plane(x, carry):
            rows = rows_of(x)
            relax = 0.06 / inp[6, rows]
            inp[6, rows] = relax
            drive = relax * inp[7, rows]
            for k, value in enumerate(fiber_of(x)):
                fib[k, rows] = drive * value
                inp[3 + k, rows] = relax * inp[3 + k, rows]
            return carry

        lax.fori_loop(0, CX, weight_plane, 0)
        load_u.wait()
        pack_rows(0, 3)
        pack_corners(0, 3, 0)
        pack_corners(0, 3, 1)

        pl.semaphore_wait(barrier, 5)
        first_halo = halo_copies(0, 3)
        stiff = (
            remote(sec_ref.at[6, pl.ds(0, CY)], kx.at[1], STIFF_LEFT, near[STIFF_LEFT]),
            remote(sec_ref.at[6, pl.ds(COLS - CY, CY)], kx.at[0], STIFF_RIGHT, near[STIFF_RIGHT]),
        )
        for copy in (*first_halo, *stiff):
            copy.start()

        def halo_rows(phase):
            for side, sign in ((1, 0.5), (0, -0.5)):
                k = 3 * side
                at = 4 * (1 - side)
                hal[at] = halo_row(phase, k) + sign * halo_diff(phase, k + 1)
                hal[at + 1] = 3.0 * halo_row(phase, k + 1) + sign * halo_diff(phase, k)
                hal[at + 2] = halo_row(phase, k + 1)
                hal[at + 3] = halo_row(phase, k + 2)

        def relaxed(phase, x):
            here = ext[phase]
            mid, p, m = rows_of(x + 1), rows_of(x + 2), rows_of(x)
            c0, c1, c2 = here[0, mid], here[1, mid], here[2, mid]
            p0, p1, p2 = here[0, p], here[1, p], here[2, p]
            m0, m1, m2 = here[0, m], here[1, m], here[2, m]
            d0, d1, d2 = 0.5 * (p0 - m0), 0.5 * (p1 - m1), 0.5 * (p2 - m2)
            y2u, y2d = y_up(c2, row_at(3, x)), y_down(c2, row_at(7, x))
            e1 = 0.5 * (y_up(c1, row_at(2, x)) - y_down(c1, row_at(6, x)))
            e2 = 0.5 * (y2u - y2d)
            t1, t2 = 3.0 * c1, 3.0 * c2
            cross = d0 + e1
            s0 = (3.0 * (p0 + m0) + (y_up(c0 + d1, row_at(0, x)) + y_down(c0 - d1, row_at(4, x)))
                  + (z_up(c0 + d2) + z_down(c0 - d2)))
            s1 = ((p1 + m1) + (y_up(t1 + d0, row_at(1, x)) + y_down(t1 - d0, row_at(5, x)))
                  + (z_up(c1 + e2) + z_down(c1 - e2)))
            s2 = (p2 + m2) + (y2u + y2d) + (z_up(t2 + cross) + z_down(t2 - cross))
            return 0.4 * c0 + 0.06 * s0, 0.4 * c1 + 0.06 * s1, 0.4 * c2 + 0.06 * s2

        def tie_forces(phase, side):
            here = ext[phase]
            far = pl.ds((0, TOP)[side], CY)
            pieces = []
            for k in range(3):
                pieces += list(split3((2.0 * kx[side]) * here[k, far]))
            got = jnp.dot(rperm[side], jnp.concatenate(pieces, axis=1), preferred_element_type=F32)
            x = ENDS[side]
            relax = inp[6, rows_of(x)]
            result = []
            for k in range(3):
                at = 3 * NZ * k
                picked = got[:, at:at + NZ] + (got[:, at + NZ:at + 2 * NZ] + got[:, at + 2 * NZ:at + 3 * NZ])
                result.append(relax * picked - 0.12 * here[k, rows_of(x + 1)])
            return result

        def receive(slot, ref):
            remote(ref, ref, slot, partner).wait_recv()

        def base_plane(x, carry):
            rows = rows_of(x)
            for k, value in enumerate(relaxed(0, x)):
                base[k, rows] = value + inp[3 + k, rows]
            return carry

        def activate_plane(x, carry):
            rows = rows_of(x)
            tension = tbuf[rows]
            out_ref[3, rows] = inp[7, rows] * tension
            for k in range(3):
                ext1[k, rows_of(x + 1)] = base[k, rows] + fib[k, rows] * tension
            return carry

        def last_plane(x, carry):
            rows = rows_of(x)
            tension = tbuf[rows]
            for k, value in enumerate(relaxed(1, x)):
                out_ref[k, rows] = value + inp[3 + k, rows] + fib[k, rows] * tension
            return carry

        first_halo[ACROSS].wait_recv()
        halo_rows(0)
        lax.fori_loop(1, CX - 1, base_plane, 0)
        second_halo = halo_copies(1, 3)
        for side, slot in ((1, TEN_LAST), (0, TEN_FIRST)):
            x = ENDS[side]
            wait_side(first_halo, side)
            stiff[1 - side].wait_recv()
            unpack_corners(0, 3, side)
            halo_rows(0)
            base_plane(x, 0)
            for k, value in enumerate(tie_forces(0, side)):
                base[k, rows_of(x)] += value
            receive(slot, tbuf.at[rows_of(x)])
            activate_plane(x, 0)
            pack_corners(1, 3, side)
            second_halo[side].start()
            second_halo[DIAG_LEFT + side].start()
        receive(TEN_ROWS, trow)
        for side, y in ((0, CY - 1), (1, 0)):
            for k in range(3):
                own = pl.ds(y, CX, stride=CY)
                ypk[1, 3 * side + k] = base[k, own] + fib[k, own] * trow[side]
        second_halo[ACROSS].start()

        for index, ((low, high), ready) in enumerate(CHUNKS):
            rows = rows_of(low, high - low)
            receive(TEN_BULK + index, tbuf.at[rows])
            lax.fori_loop(low, high, activate_plane, 0)
            if index == 0:
                second_halo[ACROSS].wait_recv()
                halo_rows(1)
            lax.fori_loop(*ready, last_plane, 0)
        last_plane(CX - 2, 0)
        for side in (1, 0):
            x = ENDS[side]
            wait_side(second_halo, side)
            unpack_corners(1, 3, side)
            halo_rows(1)
            last_plane(x, 0)
            for k, value in enumerate(tie_forces(1, side)):
                out_ref[k, rows_of(x)] += value
        for copy in (*first_halo, *second_halo, *stiff):
            copy.wait_send()


def solution(mesh):
    n_gx = mesh.shape["gx"]

    def local(sections, fiber_angles, fiber_class, row_map, interface_rows):
        vmem = pltpu.VMEM
        field, padded = (COLS, NZ), (EXT, NZ)
        out = pl.pallas_call(
            functools.partial(kernel, n_gx),
            out_shape=jax.ShapeDtypeStruct((4, COLS, NZ), F32),
            in_specs=[pl.BlockSpec(memory_space=pltpu.HBM)] * 5,
            out_specs=pl.BlockSpec(memory_space=pltpu.VMEM),
            scratch_shapes=[
                vmem((8, *field), F32),
                vmem((3, *padded), F32),
                vmem((3, *padded), F32),
                vmem((3, *field), F32),
                vmem((3, *field), F32),
                vmem((3, CY, NZ), F32),
                vmem(field, F32),
                vmem((2, CX, NZ), F32),
                vmem((COLS, COLS), BF16),
                vmem((COLS, 3 * NZ), BF16),
                vmem((2, CY, CY), BF16),
                vmem((2, 3, CY, NZ), F32),
                vmem((2, 6, 32, NZ), F32),
                vmem((2, 6, CX, NZ), F32),
                vmem((2, 2, 8, NZ), F32),
                vmem((2, 2, 8, NZ), F32),
                vmem((8, CX, NZ), F32),
                vmem((2, CY, NZ), F32),
                vmem((2, CLASSES), F32),
                vmem((CX * 8, CY), jnp.int32),
                vmem((1, 1, COLS), jnp.int32),
                vmem((2, 1, 1, CY), jnp.int32),
                pltpu.SemaphoreType.DMA((11,)),
                pltpu.SemaphoreType.DMA((N_COPIES,)),
                pltpu.SemaphoreType.DMA((N_COPIES,)),
            ],
            compiler_params=pltpu.CompilerParams(
                collective_id=0, has_side_effects=True, vmem_limit_bytes=24 * 1024 * 1024),
        )(*[pltpu.with_memory_space_constraint(operand, pltpu.HBM) for operand in (
            sections.reshape(8, COLS, NZ), fiber_angles.T, fiber_class.transpose(0, 2, 1).reshape(CX * 8, CY), row_map,
            interface_rows)])
        return out.reshape(1, 4, CX, CY, NZ)

    in_specs = (
        P("sec", None, "gx", "gy", None),
        P(),
        P("gx", "gy", None),
        P("gx", "gy", None),
        P(None, "gx", "gy", None),
    )
    out_specs = P("sec", None, "gx", "gy", None)
    return jax.shard_map(local, mesh=mesh, in_specs=in_specs, out_specs=out_specs, check_vma=False)
```

```python
import functools

import jax
import jax.numpy as jnp
from jax import lax
from jax.experimental import pallas as pl
from jax.experimental.pallas import tpu as pltpu
from jax.sharding import PartitionSpec as P

MESH = pl.DeviceIdType.MESH
F32, BF16 = jnp.float32, jnp.bfloat16

CX, CY, NZ = 16, 32, 128
COLS = CX * CY
TOP = COLS + CY
EXT = COLS + 2 * CY
CLASSES = 8
DT = 0.1

CHUNKS = (((1, 5), (2, 4)), ((5, 9), (4, 8)), ((9, 13), (8, 12)), ((13, 15), (12, 14)))

LEFT, RIGHT, ACROSS, DIAG_LEFT, DIAG_RIGHT, STIFF_LEFT, STIFF_RIGHT = range(7)
ACROSS_FIRST, ACROSS_LAST = 5, 6
EDGE_LEFT, EDGE_RIGHT = 5, 6
TEN_FIRST, TEN_LAST, TEN_ROWS, TEN_BULK = 16, 17, 18, 19
N_COPIES = TEN_BULK + len(CHUNKS)
ENDS = (0, CX - 1)


def rows_of(x, count=1):
    if isinstance(x, int):
        return pl.ds(x * CY, count * CY)
    return pl.ds(pl.multiple_of(x * CY, CY), count * CY)


def lanes(count=CY):
    return lax.broadcasted_iota(jnp.int32, (count, NZ), 1)


def sublanes():
    return lax.broadcasted_iota(jnp.int32, (CY, NZ), 0)


def z_up(a):
    return jnp.where(lanes(a.shape[0]) == NZ - 1, 0.0, pltpu.roll(a, NZ - 1, 1))


def z_down(a):
    return jnp.where(lanes(a.shape[0]) == 0, 0.0, pltpu.roll(a, 1, 1))


def y_up(a, row):
    moved = pltpu.roll(a, CY - 1, 0)
    return moved if row is None else jnp.where(sublanes() == CY - 1, jnp.broadcast_to(row, (CY, NZ)), moved)


def y_down(a, row):
    moved = pltpu.roll(a, 1, 0)
    return moved if row is None else jnp.where(sublanes() == 0, jnp.broadcast_to(row, (CY, NZ)), moved)


def sig(v):
    return 1.0 / (1.0 + jnp.exp(-v))


def split3(a):
    high = a.astype(BF16)
    rest = a - high.astype(F32)
    mid = rest.astype(BF16)
    low = (rest - mid.astype(F32)).astype(BF16)
    return high, mid, low


def kernel(n_gx, sec_ref, ang_ref, cls_ref, rmap_ref, irow_ref, out_ref,
           inp, ext0, ext1, fib, base, rel, tbl, clsx, tbuf, trow, perm, parts, rperm, tie,
           halo, ypk, corner_out, corner_in, edge_out, edge_in, hal, kx, ang, cls, rmap, irow,
           load_sem, send_sem, recv_sem):
    sec, gx, gy = lax.axis_index("sec"), lax.axis_index("gx"), lax.axis_index("gy")
    left, right = lax.rem(gx + n_gx - 1, n_gx), lax.rem(gx + 1, n_gx)
    across = 1 - gy
    near = {
        LEFT: (sec, left, gy), RIGHT: (sec, right, gy), ACROSS: (sec, gx, across),
        DIAG_LEFT: (sec, left, across), DIAG_RIGHT: (sec, right, across),
    }
    near[STIFF_LEFT], near[STIFF_RIGHT] = near[LEFT], near[RIGHT]
    partner = (1 - sec, gx, gy)
    ext = (ext0, ext1)

    barrier = pltpu.get_barrier_semaphore()
    for direction in (LEFT, RIGHT, ACROSS):
        pl.semaphore_signal(barrier, inc=1, device_id=near[direction], device_id_type=MESH)

    def load(src, dst, slot):
        return pltpu.make_async_copy(src, dst, load_sem.at[slot])

    def remote(src, dst, slot, device):
        return pltpu.make_async_remote_copy(
            src_ref=src, dst_ref=dst, send_sem=send_sem.at[slot], recv_sem=recv_sem.at[slot],
            device_id=device, device_id_type=MESH)

    def halo_copies(phase, fields):
        first, own = pl.ds(0, fields), ext[phase]
        low, high = own.at[first, pl.ds(CY, CY)], own.at[first, pl.ds(COLS, CY)]
        both = pl.ds(0, 2 * fields)
        slot = phase * 8
        copies = (
            remote(low, own.at[first, pl.ds(TOP, CY)], slot + LEFT, near[LEFT]),
            remote(high, own.at[first, pl.ds(0, CY)], slot + RIGHT, near[RIGHT]),
            remote(ypk.at[phase, both], halo.at[phase, both, pl.ds(8, CX)], slot + ACROSS, near[ACROSS]),
        )
        if phase == 1:
            copies += (
                remote(corner_out.at[0], corner_in.at[1], slot + DIAG_LEFT, near[DIAG_LEFT]),
                remote(corner_out.at[1], corner_in.at[0], slot + DIAG_RIGHT, near[DIAG_RIGHT]),
                remote(corner_out.at[0], corner_in.at[2], slot + ACROSS_FIRST, near[ACROSS]),
                remote(corner_out.at[1], corner_in.at[3], slot + ACROSS_LAST, near[ACROSS]),
            )
        return copies

    def plane_row(part, side):
        return CY + ENDS[side] * CY + (CY - 1, 0)[part]

    def far_row(part, side):
        return (0, TOP)[side] + (CY - 1, 0)[part]

    def pack_corners(fields, raw, side):
        for part in range(2):
            row = plane_row(part, side)
            for k in range(fields):
                at = part * fields + k
                corner_out[side, at:at + 1] = ext1[k, row:row + 1]
            for k in range(raw):
                at = 2 * fields + part * raw + k
                corner_out[side, at:at + 1] = ext0[k, row:row + 1]

    def pack_rows(phase, fields):
        for field in range(fields):
            ypk[phase, field] = ext[phase][field, pl.ds(CY + CY - 1, CX, stride=CY)]
            ypk[phase, fields + field] = ext[phase][field, pl.ds(CY, CX, stride=CY)]

    def wait_side(copies, side):
        copies[1 - side].wait_recv()
        if len(copies) > 3:
            copies[DIAG_RIGHT - side].wait_recv()
            copies[ACROSS_FIRST + side].wait_recv()

    def start_side(copies, side):
        copies[side].start()
        if len(copies) > 3:
            copies[DIAG_LEFT + side].start()
            copies[ACROSS_FIRST + side].start()

    def finish_side(fields, side, added):
        sign = (-1.0, 1.0)[side]
        for part in range(2):
            opposite = 1 - part
            own, far = plane_row(part, side), far_row(part, side)
            row, corner = (8, 7 + CX)[side], (7, 8 + CX)[side]
            signed = sign * (1.0, -1.0)[part]

            def across_old(k, part=part):
                at = (1 - part) * fields + k
                return halo[0, at, row:row + 1]

            def diag_old(k, part=part):
                return corner_in[side, added.raw_at(1 - part, k):added.raw_at(1 - part, k) + 1]

            def own_old(k, part=part):
                at = plane_row(1 - part, side)
                return ext0[k, at:at + 1]

            def far_old(k, part=part):
                at = far_row(1 - part, side)
                return ext0[k, at:at + 1]

            for k in range(fields):
                at = part * fields + k
                if k < 2:
                    ext1[k, own:own + 1] += signed * added(k, "own", part, side, diag_old)
                    ext1[k, far:far + 1] -= signed * added(k, "far", part, side, across_old)
                halo[1, at, corner:corner + 1] = (
                    corner_in[side, at:at + 1] - signed * added(k, "diag", part, side, own_old))
                halo[1, at, row:row + 1] = (
                    corner_in[2 + side, at:at + 1] + signed * added(k, "across", part, side, far_old))

    for k in range(6):
        for row in (7, 8 + CX):
            halo[0, k, row:row + 1] = jnp.zeros((1, NZ), F32)

    def halo_row(phase, k):
        return halo[phase, k, 8:8 + CX]

    def halo_diff(phase, k):
        return halo[phase, k, 9:9 + CX] - halo[phase, k, 7:7 + CX]

    def row_at(k, x, inner):
        return None if inner else hal[k, pl.ds(x, 1)]

    def row_set(phase, fields, y):
        sets = []
        for at in (y, y + 1, y - 1):
            if at in (-1, CY):
                first = fields if at == CY else 0
                rows = [halo[phase, first + field, 8:8 + CX] for field in range(fields)]
            else:
                rows = [ext[phase][field, pl.ds(CY + at, CX, stride=CY)] for field in range(fields)]
            sets.append([(row, pltpu.roll(row, CX - 1, 0), pltpu.roll(row, 1, 0)) for row in rows])
        return sets

    def spread_fibers():
        azimuth, elevation = ang[0:1, :], ang[1:2, :]
        flat = jnp.cos(elevation)
        for k, value in enumerate((jnp.cos(azimuth) * flat, jnp.sin(azimuth) * flat, jnp.sin(elevation))):
            for c in range(CLASSES):
                tbl[k, c:c + 1] = jnp.broadcast_to(value[:, c:c + 1], (1, NZ))
        kind = cls[...].astype(F32).T.astype(BF16)
        from_lane = lax.broadcasted_iota(jnp.int32, (NZ, CX * NZ), 0)
        to_lane = lax.broadcasted_iota(jnp.int32, (NZ, CX * NZ), 1) // 16
        spread = jnp.where(from_lane == to_lane, 1.0, 0.0).astype(BF16)
        wide = jnp.dot(kind, spread, preferred_element_type=F32)
        for x in range(CX):
            clsx[x * CY:(x + 1) * CY] = wide[:, x * NZ:(x + 1) * NZ]

    def fiber_of(x):
        kind = clsx[rows_of(x)]
        bit2 = kind >= 3.5
        kind = jnp.where(bit2, kind - 4.0, kind)
        bit1 = kind >= 1.5
        bit0 = jnp.where(bit1, kind - 2.0, kind) >= 0.5
        fields = []
        for k in range(3):
            pick = [jnp.broadcast_to(tbl[k, c:c + 1], (CY, NZ)) for c in range(CLASSES)]
            pick = [jnp.where(bit0, pick[2 * c + 1], pick[2 * c]) for c in range(4)]
            pick = [jnp.where(bit1, pick[2 * c + 1], pick[2 * c]) for c in range(2)]
            fields.append(jnp.where(bit2, pick[1], pick[0]))
        return fields


    @pl.when(sec == 0)
    def _():
        loads = [load(sec_ref.at[0], ext0.at[0, pl.ds(CY, COLS)], 0)]
        loads += [load(sec_ref.at[k], inp.at[k], k) for k in range(1, 8)]
        load_map = load(rmap_ref, rmap, 8)
        load_cls = load(cls_ref, cls, 9)
        load_ang = load(ang_ref, ang, 10)
        load_map.start()
        for k in (0, 1, 2, 3, 6, 7):
            loads[k].start()
        load_cls.start()
        load_ang.start()
        loads[4].start()
        loads[5].start()

        load_map.wait()
        source = jnp.broadcast_to(rmap[0].astype(F32), (8, COLS)).T[:, 0:1]
        spot = lax.broadcasted_iota(jnp.int32, (COLS, COLS), 1).astype(F32)
        perm[...] = jnp.where(jnp.broadcast_to(source, (COLS, COLS)) == spot, 1.0, 0.0).astype(BF16)

        for k in (0, 1, 2, 3, 6, 7):
            loads[k].wait()

        def tension_plane(x, carry):
            rows = rows_of(x)
            v = ext0[0, rows_of(x + 1)]
            c, d, f, b, s = inp[1, rows], inp[2, rows], inp[3, rows], inp[6, rows], inp[7, rows]
            square = c * c
            q = square / (square + 0.25)
            flow = 1.2 * d * f * (v - 2.0)
            binding = 2.0 * c * (1.0 - b) - 0.4 * b
            c = c + DT * (-0.3 * flow - 0.5 * c - binding)
            base[0, rows] = c
            base[1, rows] = q
            base[2, rows] = flow
            inp[6, rows] = b + DT * binding
            s = s + DT * (q - s) / 2.0
            square = c * c
            q = square / (square + 0.25)
            out_ref[1, rows] = q
            s = s + DT * (q - s) / 2.0
            out_ref[3, rows] = s
            for k, part in enumerate(split3(s)):
                parts[rows, k * NZ:(k + 1) * NZ] = part
            return carry

        lax.fori_loop(0, CX, tension_plane, 0)

        def permuted(low, high):
            moved = jnp.dot(perm[low * CY:high * CY], parts[...], preferred_element_type=F32)
            tbuf[low * CY:high * CY] = moved[:, 0:NZ] + (moved[:, NZ:2 * NZ] + moved[:, 2 * NZ:])

        permuted(CX - 1, CX)
        permuted(0, CX - 1)
        trow[0] = tbuf[pl.ds(CY - 1, CX, stride=CY)]
        trow[1] = tbuf[pl.ds(0, CX, stride=CY)]
        pack_rows(0, 1)
        pl.semaphore_wait(barrier, 4)
        first_halo = halo_copies(0, 1)
        tension = [
            remote(tbuf.at[rows_of(CX - 1)], tbuf.at[rows_of(CX - 1)], TEN_LAST, partner),
            remote(trow, trow, TEN_ROWS, partner),
            remote(tbuf.at[rows_of(0)], tbuf.at[rows_of(0)], TEN_FIRST, partner),
        ]
        tension[0].start()
        first_halo[ACROSS].start()
        start_side(first_halo, 0)
        start_side(first_halo, 1)
        for k, ((low, high), _) in enumerate(CHUNKS):
            rows = rows_of(low, high - low)
            tension.append(remote(tbuf.at[rows], tbuf.at[rows], TEN_BULK + k, partner))
        for copy in tension[1:]:
            copy.start()
        loads[4].wait()
        loads[5].wait()

        def first_ions(x, carry):
            rows = rows_of(x)
            v = ext0[0, rows_of(x + 1)]
            d, f, n, r = inp[2, rows], inp[3, rows], inp[4, rows], inp[5, rows]
            flow, q = base[2, rows], base[1, rows]
            current = flow + 0.8 * n * (v + 1.0) + 0.6 * q * r * (v + 1.0) + 0.1 * v
            base[1, rows] = v - DT * current
            inp[2, rows] = d + DT * (sig(2.0 * v + 1.0) - d) / 0.5
            inp[3, rows] = f + DT * (sig(-2.0 * v) - f) / 3.0
            inp[4, rows] = n + DT * (sig(2.0 * v) - n)
            inp[5, rows] = r + DT * (sig(v - 0.5) - r) / 5.0
            return carry

        lax.fori_loop(0, CX, first_ions, 0)

        load_ang.wait()
        load_cls.wait()
        spread_fibers()

        def fiber_plane(x, carry):
            for k, value in enumerate(fiber_of(x)):
                fib[k, rows_of(x)] = value
            return carry

        lax.fori_loop(0, CX, fiber_plane, 0)
        for side in range(2):
            for part in range(2):
                row = plane_row(part, side) - CY
                factor = (0.375 * DT) * fib[0, row:row + 1] * fib[1, row:row + 1]
                edge_out[side, part:part + 1] = factor
                corner_out[side, 4 + part:5 + part] = factor
        edges = (
            remote(edge_out.at[0], edge_in.at[1], EDGE_LEFT, near[LEFT]),
            remote(edge_out.at[1], edge_in.at[0], EDGE_RIGHT, near[RIGHT]),
        )
        for copy in edges:
            copy.start()

        def added(k, where, part, side, old):
            if where == "own":
                factor = edge_out[side, part:part + 1]
            elif where == "far":
                factor = edge_in[side, part:part + 1]
            else:
                factor = corner_in[side + (2 if where == "across" else 0), 4 + part:5 + part]
            return factor * old(0)

        added.raw_at = lambda part, k: 2 + part

        def combined(fiber, c, v00, v11, v22, x01, x02, x12):
            f0, f1, f2 = fiber
            along = (f0 * (f0 * v00 + 0.5 * (f1 * x01 + f2 * x02))
                     + f1 * (f1 * v11 + 0.5 * (f2 * x12)) + f2 * f2 * v22)
            return 0.25 * (v00 + v11 + v22) + 0.75 * along

        def diffusion(phase, x, inner=False):
            here = ext[phase]
            c, p, m = here[0, rows_of(x + 1)], here[0, rows_of(x + 2)], here[0, rows_of(x)]
            d = p - m
            yu, yd = y_up(c, row_at(0, x, inner)), y_down(c, row_at(1, x, inner))
            e = yu - yd
            twice = 2.0 * c
            return combined(
                [fib[k, rows_of(x)] for k in range(3)], c, p + m - twice, yu + yd - twice, z_up(c) + z_down(c) - twice,
                y_up(d, row_at(2, x, inner)) - y_down(d, row_at(3, x, inner)), z_up(d) - z_down(d), z_up(e) - z_down(e))

        def diffusion_row(phase, y):
            ((c, p, m),), ((cu, pu, mu),), ((cd, pd, md),) = row_set(phase, 1, y)
            d, e, twice = p - m, cu - cd, 2.0 * c
            return combined(
                [fib[k, pl.ds(y, CX, stride=CY)] for k in range(3)], c, p + m - twice, cu + cd - twice,
                z_up(c) + z_down(c) - twice, (pu - mu) - (pd - md), z_up(d) - z_down(d), z_up(e) - z_down(e))

        def halo_rows(phase):
            hal[0] = halo_row(phase, 1)
            hal[1] = halo_row(phase, 0)
            hal[2] = halo_diff(phase, 1)
            hal[3] = halo_diff(phase, 0)

        def first_step(x, carry, inner=False):
            ext1[0, rows_of(x + 1)] = base[1, rows_of(x)] + DT * diffusion(0, x, inner)
            return carry

        lax.fori_loop(1, CX - 1, functools.partial(first_step, inner=True), 0)
        second_halo = halo_copies(1, 1)
        first_halo[ACROSS].wait_recv()
        for side, y in ((0, CY - 1), (1, 0)):
            row = base[1, pl.ds(y, CX, stride=CY)] + DT * diffusion_row(0, y)
            ypk[1, side] = row
            ext1[0, pl.ds(CY + y, CX, stride=CY)] = row
        second_halo[ACROSS].start()
        for side in (1, 0):
            wait_side(first_halo, side)
            halo_rows(0)
            first_step(ENDS[side], 0)
            pack_corners(1, 1, side)
            start_side(second_halo, side)

        def second_ions(x, carry):
            rows = rows_of(x)
            v, c, q = ext1[0, rows_of(x + 1)], base[0, rows], out_ref[1, rows]
            d, f, n, r, b = inp[2, rows], inp[3, rows], inp[4, rows], inp[5, rows], inp[6, rows]
            flow = 1.2 * d * f * (v - 2.0)
            current = flow + 0.8 * n * (v + 1.0) + 0.6 * q * r * (v + 1.0) + 0.1 * v
            binding = 2.0 * c * (1.0 - b) - 0.4 * b
            base[1, rows] = v - DT * current
            out_ref[1, rows] = c + DT * (-0.3 * flow - 0.5 * c - binding)
            out_ref[2, rows] = n + DT * (sig(2.0 * v) - n)
            return carry

        lax.fori_loop(1, CX - 1, second_ions, 0)

        def second_step(x, carry, inner=False):
            rows = rows_of(x)
            out_ref[0, rows] = base[1, rows] + DT * diffusion(1, x, inner)
            return carry

        lax.fori_loop(2, CX - 2, functools.partial(second_step, inner=True), 0)
        second_halo[ACROSS].wait_recv()
        for y in (CY - 1, 0):
            row = pl.ds(y, CX, stride=CY)
            out_ref[0, row] = base[1, row] + DT * diffusion_row(1, y)
        for side in (1, 0):
            wait_side(second_halo, side)
            edges[1 - side].wait_recv()
            second_halo[side].wait_send()
            finish_side(1, side, added)
            halo_rows(1)
            second_ions(ENDS[side], 0)
            second_step(ENDS[side], 0)
            second_step((1, CX - 2)[side], 0)
        for copy in (*first_halo, *second_halo[2:], *edges, *tension):
            copy.wait_send()


    @pl.when(sec == 1)
    def _():
        pl.semaphore_signal(barrier, inc=1, device_id=partner, device_id_type=MESH)
        load_u = load(sec_ref.at[pl.ds(0, 3)], ext0.at[:, pl.ds(CY, COLS)], 0)
        load_rest = load(sec_ref.at[pl.ds(3, 5)], inp.at[pl.ds(3, 5)], 1)
        load_row = load(irow_ref, irow, 8)
        load_cls = load(cls_ref, cls, 9)
        load_ang = load(ang_ref, ang, 10)
        load_u.start()
        load_ang.start()
        load_cls.start()
        load_row.start()
        load_rest.start()

        load_u.wait()
        pack_rows(0, 3)
        load_rest.wait()
        pl.semaphore_wait(barrier, 3)
        first_halo = halo_copies(0, 3)
        stiff = (
            remote(inp.at[6, pl.ds(0, CY)], kx.at[1], STIFF_LEFT, near[STIFF_LEFT]),
            remote(inp.at[6, pl.ds(COLS - CY, CY)], kx.at[0], STIFF_RIGHT, near[STIFF_RIGHT]),
        )
        first_halo[ACROSS].start()
        for side in range(2):
            start_side(first_halo, side)
            stiff[side].start()

        load_ang.wait()
        load_cls.wait()
        spread_fibers()
        load_row.wait()
        for side in range(2):
            source = jnp.broadcast_to(irow[side, 0].astype(F32), (CY, CY)).T
            spot = lax.broadcasted_iota(jnp.int32, (CY, CY), 1).astype(F32)
            rperm[side] = jnp.where(source == spot, 1.0, 0.0).astype(BF16)

        def weight_plane(x, carry):
            rows = rows_of(x)
            relax = 0.06 / inp[6, rows]
            rel[rows] = relax
            drive = relax * inp[7, rows]
            for k, value in enumerate(fiber_of(x)):
                fib[k, rows] = drive * value
                inp[3 + k, rows] = relax * inp[3 + k, rows]
            return carry

        lax.fori_loop(0, CX, weight_plane, 0)

        def halo_rows(phase):
            for side, sign in ((1, 0.5), (0, -0.5)):
                k = 3 * side
                at = 4 * (1 - side)
                hal[at] = halo_row(phase, k) + sign * halo_diff(phase, k + 1)
                hal[at + 1] = 3.0 * halo_row(phase, k + 1) + sign * halo_diff(phase, k)
                hal[at + 2] = halo_row(phase, k + 1)
                hal[at + 3] = halo_row(phase, k + 2)

        def relaxed(phase, x, inner):
            here = ext[phase]
            mid, p, m = rows_of(x + 1), rows_of(x + 2), rows_of(x)
            c0, c1, c2 = here[0, mid], here[1, mid], here[2, mid]
            p0, p1, p2 = here[0, p], here[1, p], here[2, p]
            m0, m1, m2 = here[0, m], here[1, m], here[2, m]
            row = [row_at(k, x, inner) for k in range(8)]
            d0, d1, d2 = 0.5 * (p0 - m0), 0.5 * (p1 - m1), 0.5 * (p2 - m2)
            y2u, y2d = y_up(c2, row[3]), y_down(c2, row[7])
            e1 = 0.5 * (y_up(c1, row[2]) - y_down(c1, row[6]))
            e2 = 0.5 * (y2u - y2d)
            t1, t2 = 3.0 * c1, 3.0 * c2
            cross = d0 + e1
            s0 = (3.0 * (p0 + m0) + (y_up(c0 + d1, row[0]) + y_down(c0 - d1, row[4]))
                  + (z_up(c0 + d2) + z_down(c0 - d2)))
            s1 = ((p1 + m1) + (y_up(t1 + d0, row[1]) + y_down(t1 - d0, row[5]))
                  + (z_up(c1 + e2) + z_down(c1 - e2)))
            s2 = (p2 + m2) + (y2u + y2d) + (z_up(t2 + cross) + z_down(t2 - cross))
            return 0.4 * c0 + 0.06 * s0, 0.4 * c1 + 0.06 * s1, 0.4 * c2 + 0.06 * s2

        def relaxed_row(phase, y):
            here, up, down = row_set(phase, 3, y)
            (c0, p0, m0), (c1, p1, m1), (c2, p2, m2) = here
            d0, d2 = 0.5 * (p0 - m0), 0.5 * (p2 - m2)
            u0, u1 = 0.5 * (up[0][1] - up[0][2]), 0.5 * (up[1][1] - up[1][2])
            b0, b1 = 0.5 * (down[0][1] - down[0][2]), 0.5 * (down[1][1] - down[1][2])
            e2 = 0.5 * (up[2][0] - down[2][0])
            cross = d0 + 0.5 * (up[1][0] - down[1][0])
            t2 = 3.0 * c2
            s0 = (3.0 * (p0 + m0) + ((up[0][0] + u1) + (down[0][0] - b1)) + (z_up(c0 + d2) + z_down(c0 - d2)))
            s1 = ((p1 + m1) + ((3.0 * up[1][0] + u0) + (3.0 * down[1][0] - b0)) + (z_up(c1 + e2) + z_down(c1 - e2)))
            s2 = (p2 + m2) + (up[2][0] + down[2][0]) + (z_up(t2 + cross) + z_down(t2 - cross))
            return 0.4 * c0 + 0.06 * s0, 0.4 * c1 + 0.06 * s1, 0.4 * c2 + 0.06 * s2

        def added(k, where, part, side, old):
            return 0.03 * old(1 - k) if k < 2 else 0.0

        added.raw_at = lambda part, k: 6 + 2 * part + k

        def tie_forces(phase, side):
            here = ext[phase]
            far = pl.ds((0, TOP)[side], CY)
            pieces = []
            for k in range(3):
                pieces += list(split3((2.0 * kx[side]) * here[k, far]))
            got = jnp.dot(rperm[side], jnp.concatenate(pieces, axis=1), preferred_element_type=F32)
            x = ENDS[side]
            relax = rel[rows_of(x)]
            result = []
            for k in range(3):
                at = 3 * NZ * k
                picked = got[:, at:at + NZ] + (got[:, at + NZ:at + 2 * NZ] + got[:, at + 2 * NZ:at + 3 * NZ])
                result.append(relax * picked - 0.12 * here[k, rows_of(x + 1)])
            return result

        def receive(slot, ref):
            remote(ref, ref, slot, partner).wait_recv()

        def base_plane(x, carry, inner=False):
            rows = rows_of(x)
            for k, value in enumerate(relaxed(0, x, inner)):
                base[k, rows] = value + inp[3 + k, rows]
            return carry

        def activate_plane(x, carry):
            rows = rows_of(x)
            tension = tbuf[rows]
            out_ref[3, rows] = inp[7, rows] * tension
            for k in range(3):
                ext1[k, rows_of(x + 1)] = base[k, rows] + fib[k, rows] * tension
            return carry

        def last_plane(x, carry, inner=False):
            rows = rows_of(x)
            tension = tbuf[rows]
            for k, value in enumerate(relaxed(1, x, inner)):
                out_ref[k, rows] = value + inp[3 + k, rows] + fib[k, rows] * tension
            return carry

        lax.fori_loop(1, CX - 1, functools.partial(base_plane, inner=True), 0)
        second_halo = halo_copies(1, 3)
        first_halo[ACROSS].wait_recv()
        receive(TEN_ROWS, trow)
        for side, y in ((0, CY - 1), (1, 0)):
            own = pl.ds(y, CX, stride=CY)
            for k, value in enumerate(relaxed_row(0, y)):
                value = value + inp[3 + k, own]
                base[k, own] = value
                ypk[1, 3 * side + k] = value + fib[k, own] * trow[side]
        second_halo[ACROSS].start()
        for side, slot in ((1, TEN_LAST), (0, TEN_FIRST)):
            x = ENDS[side]
            wait_side(first_halo, side)
            stiff[1 - side].wait_recv()
            halo_rows(0)
            base_plane(x, 0)
            for k, value in enumerate(tie_forces(0, side)):
                base[k, rows_of(x)] += value
            receive(slot, tbuf.at[rows_of(x)])
            activate_plane(x, 0)
            pack_corners(3, 2, side)
            start_side(second_halo, side)

        for index, ((low, high), ready_planes) in enumerate(CHUNKS):
            rows = rows_of(low, high - low)
            receive(TEN_BULK + index, tbuf.at[rows])
            lax.fori_loop(low, high, activate_plane, 0)
            lax.fori_loop(*ready_planes, functools.partial(last_plane, inner=True), 0)
        second_halo[ACROSS].wait_recv()
        for side, y in ((0, CY - 1), (1, 0)):
            own = pl.ds(y, CX, stride=CY)
            for k, value in enumerate(relaxed_row(1, y)):
                out_ref[k, own] = value + inp[3 + k, own] + fib[k, own] * trow[side]
        for side in (1, 0):
            x = ENDS[side]
            wait_side(second_halo, side)
            second_halo[side].wait_send()
            finish_side(3, side, added)
            halo_rows(1)
            last_plane((1, CX - 2)[side], 0)
            last_plane(x, 0)
            for k, value in enumerate(tie_forces(1, side)):
                out_ref[k, rows_of(x)] += value
        for copy in (*first_halo, *second_halo[2:], *stiff):
            copy.wait_send()


def solution(mesh):
    n_gx = mesh.shape["gx"]

    def local(sections, fiber_angles, fiber_class, row_map, interface_rows):
        vmem = pltpu.VMEM
        field, padded = (COLS, NZ), (EXT, NZ)
        out = pl.pallas_call(
            functools.partial(kernel, n_gx),
            out_shape=jax.ShapeDtypeStruct((4, COLS, NZ), F32),
            in_specs=[pl.BlockSpec(memory_space=pltpu.HBM)] * 5,
            out_specs=pl.BlockSpec(memory_space=pltpu.VMEM),
            scratch_shapes=[
                vmem((8, *field), F32),
                vmem((3, *padded), F32),
                vmem((3, *padded), F32),
                vmem((3, *field), F32),
                vmem((3, *field), F32),
                vmem(field, F32),
                vmem((3, CLASSES, NZ), F32),
                vmem(field, F32),
                vmem(field, F32),
                vmem((2, CX, NZ), F32),
                vmem((COLS, COLS), BF16),
                vmem((COLS, 3 * NZ), BF16),
                vmem((2, CY, CY), BF16),
                vmem((2, 3, CY, NZ), F32),
                vmem((2, 6, 32, NZ), F32),
                vmem((2, 6, CX, NZ), F32),
                vmem((2, 16, NZ), F32),
                vmem((4, 16, NZ), F32),
                vmem((2, 8, NZ), F32),
                vmem((2, 8, NZ), F32),
                vmem((8, CX, NZ), F32),
                vmem((2, CY, NZ), F32),
                vmem((2, CLASSES), F32),
                vmem((CX * 8, CY), jnp.int32),
                vmem((1, 1, COLS), jnp.int32),
                vmem((2, 1, 1, CY), jnp.int32),
                pltpu.SemaphoreType.DMA((11,)),
                pltpu.SemaphoreType.DMA((N_COPIES,)),
                pltpu.SemaphoreType.DMA((N_COPIES,)),
            ],
            compiler_params=pltpu.CompilerParams(
                collective_id=0, has_side_effects=True, vmem_limit_bytes=24 * 1024 * 1024),
        )(*[pltpu.with_memory_space_constraint(operand, pltpu.HBM) for operand in (
            sections.reshape(8, COLS, NZ), fiber_angles.T, fiber_class.transpose(0, 2, 1).reshape(CX * 8, CY), row_map,
            interface_rows)])
        return out.reshape(1, 4, CX, CY, NZ)

    in_specs = (
        P("sec", None, "gx", "gy", None),
        P(),
        P("gx", "gy", None),
        P("gx", "gy", None),
        P(None, "gx", "gy", None),
    )
    out_specs = P("sec", None, "gx", "gy", None)
    return jax.shard_map(local, mesh=mesh, in_specs=in_specs, out_specs=out_specs, check_vma=False)
```

```python
import functools

import jax
import jax.numpy as jnp
from jax import lax
from jax.experimental import pallas as pl
from jax.experimental.pallas import tpu as pltpu
from jax.sharding import PartitionSpec as P

MESH = pl.DeviceIdType.MESH
F32, BF16 = jnp.float32, jnp.bfloat16

CX, CY, NZ = 16, 32, 128
COLS = CX * CY
TOP = COLS + CY
EXT = COLS + 2 * CY
CLASSES = 8
DT = 0.1

CHUNKS = (((1, 5), (2, 4)), ((5, 9), (4, 8)), ((9, 13), (8, 12)), ((13, 15), (12, 14)))

LEFT, RIGHT, ACROSS, DIAG_LEFT, DIAG_RIGHT, STIFF_LEFT, STIFF_RIGHT = range(7)
ACROSS_FIRST, ACROSS_LAST = 5, 6
LIST_LEFT, LIST_RIGHT = 3, 4
EDGE_LEFT, EDGE_RIGHT = 7, 15
TEN_FIRST, TEN_LAST, TEN_ROWS, TEN_BULK = 16, 17, 18, 19
SHARE_FIRST, SHARE_LAST = TEN_BULK + len(CHUNKS), TEN_BULK + len(CHUNKS) + 1
N_COPIES = SHARE_LAST + 1
ENDS = (0, CX - 1)


def rows_of(x, count=1):
    if isinstance(x, int):
        return pl.ds(x * CY, count * CY)
    return pl.ds(pl.multiple_of(x * CY, CY), count * CY)


def lanes(count=CY):
    return lax.broadcasted_iota(jnp.int32, (count, NZ), 1)


def sublanes():
    return lax.broadcasted_iota(jnp.int32, (CY, NZ), 0)


def z_up(a):
    return jnp.where(lanes(a.shape[0]) == NZ - 1, 0.0, pltpu.roll(a, NZ - 1, 1))


def z_down(a):
    return jnp.where(lanes(a.shape[0]) == 0, 0.0, pltpu.roll(a, 1, 1))


def y_up(a, row):
    moved = pltpu.roll(a, CY - 1, 0)
    return moved if row is None else jnp.where(sublanes() == CY - 1, jnp.broadcast_to(row, (CY, NZ)), moved)


def y_down(a, row):
    moved = pltpu.roll(a, 1, 0)
    return moved if row is None else jnp.where(sublanes() == 0, jnp.broadcast_to(row, (CY, NZ)), moved)


def sig(v):
    return 1.0 / (1.0 + jnp.exp(-v))


def split3(a):
    high = a.astype(BF16)
    rest = a - high.astype(F32)
    mid = rest.astype(BF16)
    low = (rest - mid.astype(F32)).astype(BF16)
    return high, mid, low


def kernel(n_gx, sec_ref, ang_ref, cls_ref, rmap_ref, irow_ref, out_ref,
           inp, ext0, ext1, fib, base, rel, tbl, clsx, tbuf, trow, perm, parts, rperm,
           halo, ypk, corner_out, corner_in, edge_out, edge_in, hal, kx, ang, cls, rmap, irow,
           far_irow, unfinished, share, share_out, share_in, end_out,
           load_sem, send_sem, recv_sem):
    sec, gx, gy = lax.axis_index("sec"), lax.axis_index("gx"), lax.axis_index("gy")
    left, right = lax.rem(gx + n_gx - 1, n_gx), lax.rem(gx + 1, n_gx)
    across = 1 - gy
    near = {
        LEFT: (sec, left, gy), RIGHT: (sec, right, gy), ACROSS: (sec, gx, across),
        DIAG_LEFT: (sec, left, across), DIAG_RIGHT: (sec, right, across),
    }
    near[STIFF_LEFT], near[STIFF_RIGHT] = near[LEFT], near[RIGHT]
    partner = (1 - sec, gx, gy)
    ext = (ext0, ext1)

    barrier = pltpu.get_barrier_semaphore()
    for direction in (LEFT, RIGHT, ACROSS):
        pl.semaphore_signal(barrier, inc=1, device_id=near[direction], device_id_type=MESH)

    def load(src, dst, slot):
        return pltpu.make_async_copy(src, dst, load_sem.at[slot])

    def remote(src, dst, slot, device):
        return pltpu.make_async_remote_copy(
            src_ref=src, dst_ref=dst, send_sem=send_sem.at[slot], recv_sem=recv_sem.at[slot],
            device_id=device, device_id_type=MESH)

    def halo_copies(phase, fields):
        first, own = pl.ds(0, fields), ext[phase]
        low, high = own.at[first, pl.ds(CY, CY)], own.at[first, pl.ds(COLS, CY)]
        ends = corner_out
        if phase == 1 and fields == 3:
            low, high, ends = unfinished.at[0], unfinished.at[1], end_out
        both = pl.ds(0, 2 * fields)
        slot = phase * 8
        copies = (
            remote(low, own.at[first, pl.ds(TOP, CY)], slot + LEFT, near[LEFT]),
            remote(high, own.at[first, pl.ds(0, CY)], slot + RIGHT, near[RIGHT]),
            remote(ypk.at[phase, both], halo.at[phase, both, pl.ds(8, CX)], slot + ACROSS, near[ACROSS]),
        )
        if phase == 1:
            copies += (
                remote(corner_out.at[0], corner_in.at[1], slot + DIAG_LEFT, near[DIAG_LEFT]),
                remote(corner_out.at[1], corner_in.at[0], slot + DIAG_RIGHT, near[DIAG_RIGHT]),
                remote(ends.at[0], corner_in.at[2], slot + ACROSS_FIRST, near[ACROSS]),
                remote(ends.at[1], corner_in.at[3], slot + ACROSS_LAST, near[ACROSS]),
            )
        return copies

    def plane_row(part, side):
        return CY + ENDS[side] * CY + (CY - 1, 0)[part]

    def far_row(part, side):
        return (0, TOP)[side] + (CY - 1, 0)[part]

    def pack_corners(fields, side, into=corner_out):
        for part in range(2):
            row = plane_row(part, side)
            for k in range(fields):
                at = part * fields + k
                into[side, at:at + 1] = ext1[k, row:row + 1]

    def pack_edges(fields):
        for side in range(2):
            row = (8, 7 + CX)[side]
            for k in range(2 * fields):
                edge_out[side, k:k + 1] = halo[0, k, row:row + 1]

    edges = (
        remote(edge_out.at[0], edge_in.at[1], EDGE_LEFT, near[LEFT]),
        remote(edge_out.at[1], edge_in.at[0], EDGE_RIGHT, near[RIGHT]),
    )

    def pack_rows(phase, fields):
        for field in range(fields):
            ypk[phase, field] = ext[phase][field, pl.ds(CY + CY - 1, CX, stride=CY)]
            ypk[phase, fields + field] = ext[phase][field, pl.ds(CY, CX, stride=CY)]

    def wait_side(copies, side):
        copies[1 - side].wait_recv()
        if len(copies) > 3:
            copies[ACROSS_FIRST + side].wait_recv()
            edges[1 - side].wait_recv()
            copies[side].wait_send()

    def start_side(copies, side):
        copies[side].start()
        if len(copies) > 3:
            copies[DIAG_LEFT + side].start()
            copies[ACROSS_FIRST + side].start()

    def finish_side(fields, side, added):
        sign = (-1.0, 1.0)[side]
        row = (8, 7 + CX)[side]
        for part in range(2):
            own, far = plane_row(part, side), far_row(part, side)
            signed = sign * (1.0, -1.0)[part]

            def diag_old(k, part=part):
                at = (1 - part) * fields + k
                return edge_in[side, at:at + 1]

            def across_old(k, part=part):
                at = (1 - part) * fields + k
                return halo[0, at, row:row + 1]

            def far_old(k, part=part):
                at = far_row(1 - part, side)
                return ext0[k, at:at + 1]

            for k in range(min(fields, 2)):
                at = part * fields + k
                ext1[k, own:own + 1] += signed * added(k, "own", part, side, diag_old)
                if fields == 1:
                    ext1[k, far:far + 1] -= signed * added(k, "far", part, side, across_old)
                halo[1, at, row:row + 1] = (
                    corner_in[2 + side, at:at + 1] + signed * added(k, "across", part, side, far_old))
            if fields == 3:
                at = part * fields + 2
                halo[1, at, row:row + 1] = corner_in[2 + side, at:at + 1]

    def add_corners(fields, side, added, copies):
        copies[DIAG_RIGHT - side].wait_recv()
        sign = (-1.0, 1.0)[side]
        corner = []
        for part in range(2):
            signed = sign * (1.0, -1.0)[part]

            def own_old(k, part=part):
                at = plane_row(1 - part, side)
                return ext0[k, at:at + 1]

            corner.append([corner_in[side, part * fields + k:part * fields + k + 1] for k in range(min(fields, 2))])
            if fields == 1:
                corner[part][0] -= signed * added(0, "diag", part, side, own_old)
            else:
                corner[part] = [value + share_in[side, 2 * part + k:2 * part + k + 1]
                                for k, value in enumerate(corner[part])]
        for part in range(2):
            signed = sign * (1.0, -1.0)[part]
            own = plane_row(part, side) - CY
            for k in range(min(fields, 2)):
                out_ref[k, own:own + 1] += signed * added(k, "own", part, side, lambda c, part=part: corner[1 - part][c])

    for k in range(6):
        for row in (7, 8 + CX):
            halo[0, k, row:row + 1] = jnp.zeros((1, NZ), F32)
            halo[1, k, row:row + 1] = jnp.zeros((1, NZ), F32)

    def halo_row(phase, k):
        return halo[phase, k, 8:8 + CX]

    def halo_diff(phase, k):
        return halo[phase, k, 9:9 + CX] - halo[phase, k, 7:7 + CX]

    def row_at(k, x, inner):
        return None if inner else hal[k, pl.ds(x, 1)]

    def row_set(phase, fields, y):
        sets = []
        for at in (y, y + 1, y - 1):
            if at in (-1, CY):
                first = fields if at == CY else 0
                rows = [halo[phase, first + field, 8:8 + CX] for field in range(fields)]
            else:
                rows = [ext[phase][field, pl.ds(CY + at, CX, stride=CY)] for field in range(fields)]
            sets.append([(row, pltpu.roll(row, CX - 1, 0), pltpu.roll(row, 1, 0)) for row in rows])
        return sets

    def spread_fibers():
        azimuth, elevation = ang[0:1, :], ang[1:2, :]
        flat = jnp.cos(elevation)
        for k, value in enumerate((jnp.cos(azimuth) * flat, jnp.sin(azimuth) * flat, jnp.sin(elevation))):
            for c in range(CLASSES):
                tbl[k, c:c + 1] = jnp.broadcast_to(value[:, c:c + 1], (1, NZ))
        kind = cls[...].astype(F32).T.astype(BF16)
        from_lane = lax.broadcasted_iota(jnp.int32, (NZ, CX * NZ), 0)
        to_lane = lax.broadcasted_iota(jnp.int32, (NZ, CX * NZ), 1) // 16
        spread = jnp.where(from_lane == to_lane, 1.0, 0.0).astype(BF16)
        wide = jnp.dot(kind, spread, preferred_element_type=F32)
        for x in range(CX):
            clsx[x * CY:(x + 1) * CY] = wide[:, x * NZ:(x + 1) * NZ]

    def fiber_of(x):
        kind = clsx[rows_of(x)]
        bit2 = kind >= 3.5
        kind = jnp.where(bit2, kind - 4.0, kind)
        bit1 = kind >= 1.5
        bit0 = jnp.where(bit1, kind - 2.0, kind) >= 0.5
        fields = []
        for k in range(3):
            pick = [jnp.broadcast_to(tbl[k, c:c + 1], (CY, NZ)) for c in range(CLASSES)]
            pick = [jnp.where(bit0, pick[2 * c + 1], pick[2 * c]) for c in range(4)]
            pick = [jnp.where(bit1, pick[2 * c + 1], pick[2 * c]) for c in range(2)]
            fields.append(jnp.where(bit2, pick[1], pick[0]))
        return fields


    @pl.when(sec == 0)
    def _():
        loads = [load(sec_ref.at[0], ext0.at[0, pl.ds(CY, COLS)], 0)]
        loads += [load(sec_ref.at[k], inp.at[k], k) for k in range(1, 8)]
        load_map = load(rmap_ref, rmap, 8)
        load_cls = load(cls_ref, cls, 9)
        load_ang = load(ang_ref, ang, 10)
        load_map.start()
        for k in (0, 1, 2, 3, 6, 7):
            loads[k].start()
        load_cls.start()
        load_ang.start()
        loads[4].start()
        loads[5].start()

        load_map.wait()
        source = jnp.broadcast_to(rmap[0].astype(F32), (8, COLS)).T[:, 0:1]
        spot = lax.broadcasted_iota(jnp.int32, (COLS, COLS), 1).astype(F32)
        perm[...] = jnp.where(jnp.broadcast_to(source, (COLS, COLS)) == spot, 1.0, 0.0).astype(BF16)

        for k in (0, 1, 2, 3, 6, 7):
            loads[k].wait()

        def tension_plane(x, carry):
            rows = rows_of(x)
            v = ext0[0, rows_of(x + 1)]
            c, d, f, b, s = inp[1, rows], inp[2, rows], inp[3, rows], inp[6, rows], inp[7, rows]
            square = c * c
            q = square / (square + 0.25)
            flow = 1.2 * d * f * (v - 2.0)
            binding = 2.0 * c * (1.0 - b) - 0.4 * b
            c = c + DT * (-0.3 * flow - 0.5 * c - binding)
            base[0, rows] = c
            base[1, rows] = q
            base[2, rows] = flow
            inp[6, rows] = b + DT * binding
            s = s + DT * (q - s) / 2.0
            square = c * c
            q = square / (square + 0.25)
            out_ref[1, rows] = q
            s = s + DT * (q - s) / 2.0
            out_ref[3, rows] = s
            for k, part in enumerate(split3(s)):
                parts[rows, k * NZ:(k + 1) * NZ] = part
            return carry

        lax.fori_loop(0, CX, tension_plane, 0)

        def permuted(low, high):
            moved = jnp.dot(perm[low * CY:high * CY], parts[...], preferred_element_type=F32)
            tbuf[low * CY:high * CY] = moved[:, 0:NZ] + (moved[:, NZ:2 * NZ] + moved[:, 2 * NZ:])

        permuted(CX - 1, CX)
        permuted(0, CX - 1)
        trow[0] = tbuf[pl.ds(CY - 1, CX, stride=CY)]
        trow[1] = tbuf[pl.ds(0, CX, stride=CY)]
        pack_rows(0, 1)
        pl.semaphore_wait(barrier, 4)
        first_halo = halo_copies(0, 1)
        tension = [
            remote(tbuf.at[rows_of(CX - 1)], tbuf.at[rows_of(CX - 1)], TEN_LAST, partner),
            remote(trow, trow, TEN_ROWS, partner),
            remote(tbuf.at[rows_of(0)], tbuf.at[rows_of(0)], TEN_FIRST, partner),
        ]
        tension[0].start()
        first_halo[ACROSS].start()
        start_side(first_halo, 0)
        start_side(first_halo, 1)
        for k, ((low, high), _) in enumerate(CHUNKS):
            rows = rows_of(low, high - low)
            tension.append(remote(tbuf.at[rows], tbuf.at[rows], TEN_BULK + k, partner))
        for copy in tension[1:]:
            copy.start()
        loads[4].wait()
        loads[5].wait()

        def first_ions(x, carry):
            rows = rows_of(x)
            v = ext0[0, rows_of(x + 1)]
            d, f, n, r = inp[2, rows], inp[3, rows], inp[4, rows], inp[5, rows]
            flow, q = base[2, rows], base[1, rows]
            current = flow + 0.8 * n * (v + 1.0) + 0.6 * q * r * (v + 1.0) + 0.1 * v
            base[1, rows] = v - DT * current
            inp[2, rows] = d + DT * (sig(2.0 * v + 1.0) - d) / 0.5
            inp[3, rows] = f + DT * (sig(-2.0 * v) - f) / 3.0
            inp[4, rows] = n + DT * (sig(2.0 * v) - n)
            inp[5, rows] = r + DT * (sig(v - 0.5) - r) / 5.0
            return carry

        lax.fori_loop(0, CX, first_ions, 0)

        load_ang.wait()
        load_cls.wait()
        spread_fibers()

        def fiber_plane(x, carry):
            for k, value in enumerate(fiber_of(x)):
                fib[k, rows_of(x)] = value
            return carry

        lax.fori_loop(0, CX, fiber_plane, 0)
        for side in range(2):
            for part in range(2):
                row = plane_row(part, side) - CY
                factor = (0.375 * DT) * fib[0, row:row + 1] * fib[1, row:row + 1]
                edge_out[side, 2 + part:3 + part] = factor
                corner_out[side, 4 + part:5 + part] = factor

        def added(k, where, part, side, old):
            if where == "own":
                factor = edge_out[side, 2 + part:3 + part]
            elif where == "far":
                factor = edge_in[side, 2 + part:3 + part]
            else:
                factor = corner_in[side + (2 if where == "across" else 0), 4 + part:5 + part]
            return factor * old(0)

        def combined(fiber, c, v00, v11, v22, x01, x02, x12):
            f0, f1, f2 = fiber
            along = (f0 * (f0 * v00 + 0.5 * (f1 * x01 + f2 * x02))
                     + f1 * (f1 * v11 + 0.5 * (f2 * x12)) + f2 * f2 * v22)
            return 0.25 * (v00 + v11 + v22) + 0.75 * along

        def diffusion(phase, x, inner=False):
            here = ext[phase]
            c, p, m = here[0, rows_of(x + 1)], here[0, rows_of(x + 2)], here[0, rows_of(x)]
            d = p - m
            yu, yd = y_up(c, row_at(0, x, inner)), y_down(c, row_at(1, x, inner))
            e = yu - yd
            twice = 2.0 * c
            return combined(
                [fib[k, rows_of(x)] for k in range(3)], c, p + m - twice, yu + yd - twice, z_up(c) + z_down(c) - twice,
                y_up(d, row_at(2, x, inner)) - y_down(d, row_at(3, x, inner)), z_up(d) - z_down(d), z_up(e) - z_down(e))

        def diffusion_row(phase, y):
            ((c, p, m),), ((cu, pu, mu),), ((cd, pd, md),) = row_set(phase, 1, y)
            d, e, twice = p - m, cu - cd, 2.0 * c
            return combined(
                [fib[k, pl.ds(y, CX, stride=CY)] for k in range(3)], c, p + m - twice, cu + cd - twice,
                z_up(c) + z_down(c) - twice, (pu - mu) - (pd - md), z_up(d) - z_down(d), z_up(e) - z_down(e))

        def halo_rows(phase):
            hal[0] = halo_row(phase, 1)
            hal[1] = halo_row(phase, 0)
            hal[2] = halo_diff(phase, 1)
            hal[3] = halo_diff(phase, 0)

        def first_step(x, carry, inner=False):
            ext1[0, rows_of(x + 1)] = base[1, rows_of(x)] + DT * diffusion(0, x, inner)
            return carry

        lax.fori_loop(1, CX - 1, functools.partial(first_step, inner=True), 0)
        second_halo = halo_copies(1, 1)
        first_halo[ACROSS].wait_recv()
        pack_edges(1)
        for copy in edges:
            copy.start()
        for side, y in ((0, CY - 1), (1, 0)):
            row = base[1, pl.ds(y, CX, stride=CY)] + DT * diffusion_row(0, y)
            ypk[1, side] = row
            ext1[0, pl.ds(CY + y, CX, stride=CY)] = row
        second_halo[ACROSS].start()
        for side in (1, 0):
            wait_side(first_halo, side)
            halo_rows(0)
            first_step(ENDS[side], 0)
            pack_corners(1, side)
            start_side(second_halo, side)

        def second_ions(x, carry):
            rows = rows_of(x)
            v, c, q = ext1[0, rows_of(x + 1)], base[0, rows], out_ref[1, rows]
            d, f, n, r, b = inp[2, rows], inp[3, rows], inp[4, rows], inp[5, rows], inp[6, rows]
            flow = 1.2 * d * f * (v - 2.0)
            current = flow + 0.8 * n * (v + 1.0) + 0.6 * q * r * (v + 1.0) + 0.1 * v
            binding = 2.0 * c * (1.0 - b) - 0.4 * b
            base[1, rows] = v - DT * current
            out_ref[1, rows] = c + DT * (-0.3 * flow - 0.5 * c - binding)
            out_ref[2, rows] = n + DT * (sig(2.0 * v) - n)
            return carry

        lax.fori_loop(1, CX - 1, second_ions, 0)

        def second_step(x, carry, inner=False):
            rows = rows_of(x)
            out_ref[0, rows] = base[1, rows] + DT * diffusion(1, x, inner)
            return carry

        lax.fori_loop(2, CX - 2, functools.partial(second_step, inner=True), 0)
        second_halo[ACROSS].wait_recv()
        for y in (CY - 1, 0):
            row = pl.ds(y, CX, stride=CY)
            out_ref[0, row] = base[1, row] + DT * diffusion_row(1, y)
        for side in (1, 0):
            wait_side(second_halo, side)
            finish_side(1, side, added)
            halo_rows(1)
            second_ions(ENDS[side], 0)
            second_step(ENDS[side], 0)
            second_step((1, CX - 2)[side], 0)
            add_corners(1, side, added, second_halo)
        for copy in (*first_halo, *second_halo[2:], *edges, *tension):
            copy.wait_send()


    @pl.when(sec == 1)
    def _():
        pl.semaphore_signal(barrier, inc=1, device_id=partner, device_id_type=MESH)
        load_u = load(sec_ref.at[pl.ds(0, 3)], ext0.at[:, pl.ds(CY, COLS)], 0)
        load_rest = load(sec_ref.at[pl.ds(3, 5)], inp.at[pl.ds(3, 5)], 1)
        load_row = load(irow_ref, irow, 8)
        load_cls = load(cls_ref, cls, 9)
        load_ang = load(ang_ref, ang, 10)
        load_u.start()
        load_ang.start()
        load_cls.start()
        load_row.start()
        load_rest.start()

        load_u.wait()
        pack_rows(0, 3)
        load_rest.wait()
        load_row.wait()
        pl.semaphore_wait(barrier, 3)
        first_halo = halo_copies(0, 3)
        stiff = (
            remote(inp.at[6, pl.ds(0, CY)], kx.at[1], STIFF_LEFT, near[STIFF_LEFT]),
            remote(inp.at[6, pl.ds(COLS - CY, CY)], kx.at[0], STIFF_RIGHT, near[STIFF_RIGHT]),
        )
        lists = (
            remote(irow.at[0], far_irow.at[1], LIST_LEFT, near[LEFT]),
            remote(irow.at[1], far_irow.at[0], LIST_RIGHT, near[RIGHT]),
        )
        first_halo[ACROSS].start()
        for side in range(2):
            start_side(first_halo, side)
            stiff[side].start()
            lists[side].start()

        load_ang.wait()
        load_cls.wait()
        spread_fibers()

        def take_list(values, slot):
            source = jnp.broadcast_to(values.astype(F32), (CY, CY)).T
            spot = lax.broadcasted_iota(jnp.int32, (CY, CY), 1).astype(F32)
            rperm[slot] = jnp.where(source == spot, 1.0, 0.0).astype(BF16)

        for side in range(2):
            take_list(irow[side, 0], side)

        def weight_plane(x, carry):
            rows = rows_of(x)
            relax = 0.06 / inp[6, rows]
            rel[rows] = relax
            drive = relax * inp[7, rows]
            for k, value in enumerate(fiber_of(x)):
                fib[k, rows] = drive * value
                inp[3 + k, rows] = relax * inp[3 + k, rows]
            return carry

        lax.fori_loop(0, CX, weight_plane, 0)

        def halo_rows(phase):
            for side, sign in ((1, 0.5), (0, -0.5)):
                k = 3 * side
                at = 4 * (1 - side)
                hal[at] = halo_row(phase, k) + sign * halo_diff(phase, k + 1)
                hal[at + 1] = 3.0 * halo_row(phase, k + 1) + sign * halo_diff(phase, k)
                hal[at + 2] = halo_row(phase, k + 1)
                hal[at + 3] = halo_row(phase, k + 2)

        def relaxed(phase, x, inner, without=None):
            here = ext[phase]
            mid, p, m = rows_of(x + 1), rows_of(x + 2), rows_of(x)
            c0, c1, c2 = here[0, mid], here[1, mid], here[2, mid]
            p0, p1, p2 = here[0, p], here[1, p], here[2, p]
            m0, m1, m2 = here[0, m], here[1, m], here[2, m]
            if without == 0:
                m0 = m1 = m2 = jnp.zeros_like(c0)
            if without == 1:
                p0 = p1 = p2 = jnp.zeros_like(c0)
            row = [row_at(k, x, inner) for k in range(8)]
            d0, d1, d2 = 0.5 * (p0 - m0), 0.5 * (p1 - m1), 0.5 * (p2 - m2)
            y2u, y2d = y_up(c2, row[3]), y_down(c2, row[7])
            e1 = 0.5 * (y_up(c1, row[2]) - y_down(c1, row[6]))
            e2 = 0.5 * (y2u - y2d)
            t1, t2 = 3.0 * c1, 3.0 * c2
            cross = d0 + e1
            s0 = (3.0 * (p0 + m0) + (y_up(c0 + d1, row[0]) + y_down(c0 - d1, row[4]))
                  + (z_up(c0 + d2) + z_down(c0 - d2)))
            s1 = ((p1 + m1) + (y_up(t1 + d0, row[1]) + y_down(t1 - d0, row[5]))
                  + (z_up(c1 + e2) + z_down(c1 - e2)))
            s2 = (p2 + m2) + (y2u + y2d) + (z_up(t2 + cross) + z_down(t2 - cross))
            return 0.4 * c0 + 0.06 * s0, 0.4 * c1 + 0.06 * s1, 0.4 * c2 + 0.06 * s2

        def relaxed_row(phase, y):
            here, up, down = row_set(phase, 3, y)
            (c0, p0, m0), (c1, p1, m1), (c2, p2, m2) = here
            d0, d2 = 0.5 * (p0 - m0), 0.5 * (p2 - m2)
            u0, u1 = 0.5 * (up[0][1] - up[0][2]), 0.5 * (up[1][1] - up[1][2])
            b0, b1 = 0.5 * (down[0][1] - down[0][2]), 0.5 * (down[1][1] - down[1][2])
            e2 = 0.5 * (up[2][0] - down[2][0])
            cross = d0 + 0.5 * (up[1][0] - down[1][0])
            t2 = 3.0 * c2
            s0 = (3.0 * (p0 + m0) + ((up[0][0] + u1) + (down[0][0] - b1)) + (z_up(c0 + d2) + z_down(c0 - d2)))
            s1 = ((p1 + m1) + ((3.0 * up[1][0] + u0) + (3.0 * down[1][0] - b0)) + (z_up(c1 + e2) + z_down(c1 - e2)))
            s2 = (p2 + m2) + (up[2][0] + down[2][0]) + (z_up(t2 + cross) + z_down(t2 - cross))
            return 0.4 * c0 + 0.06 * s0, 0.4 * c1 + 0.06 * s1, 0.4 * c2 + 0.06 * s2

        def added(k, where, part, side, old):
            return 0.03 * old(1 - k) if k < 2 else 0.0

        def picked(slot, stiffness, planes):
            pieces = []
            for plane in planes:
                pieces += list(split3((2.0 * stiffness) * plane))
            got = jnp.dot(rperm[slot], jnp.concatenate(pieces, axis=1), preferred_element_type=F32)
            return [got[:, at:at + NZ] + (got[:, at + NZ:at + 2 * NZ] + got[:, at + 2 * NZ:at + 3 * NZ])
                    for at in (0, 3 * NZ, 6 * NZ)]

        def far_plane(phase, side):
            return [ext[phase][k, pl.ds((0, TOP)[side], CY)] for k in range(3)]

        def tie_forces(phase, side):
            x = ENDS[side]
            relax = rel[rows_of(x)]
            got = picked(side, kx[side], far_plane(phase, side))
            return [relax * got[k] - 0.12 * ext[phase][k, rows_of(x + 1)] for k in range(3)]

        def contribution(planes, above, below, sign, relax, got):
            p0, p1, p2 = planes
            half = 0.5 * sign
            across0 = half * (y_up(p0, above[0]) - y_down(p0, below[0]))
            across1 = half * (y_up(p1, above[1]) - y_down(p1, below[1]))
            s0 = 3.0 * p0 + across1 + half * (z_up(p2) - z_down(p2))
            s1 = p1 + across0
            s2 = p2 + half * (z_up(p0) - z_down(p0))
            return [0.06 * value + relax * got[k] for k, value in enumerate((s0, s1, s2))]

        def receive(slot, ref):
            remote(ref, ref, slot, partner).wait_recv()

        def base_plane(x, carry, inner=False):
            rows = rows_of(x)
            for k, value in enumerate(relaxed(0, x, inner)):
                base[k, rows] = value + inp[3 + k, rows]
            return carry

        def activate_plane(x, carry):
            rows = rows_of(x)
            tension = tbuf[rows]
            out_ref[3, rows] = inp[7, rows] * tension
            for k in range(3):
                ext1[k, rows_of(x + 1)] = base[k, rows] + fib[k, rows] * tension
            return carry

        def last_plane(x, carry, inner=False):
            rows = rows_of(x)
            tension = tbuf[rows]
            for k, value in enumerate(relaxed(1, x, inner)):
                out_ref[k, rows] = value + inp[3 + k, rows] + fib[k, rows] * tension
            return carry

        lax.fori_loop(1, CX - 1, functools.partial(base_plane, inner=True), 0)
        second_halo = halo_copies(1, 3)
        def send_end(side, slot):
            x = ENDS[side]
            rows = rows_of(x)
            receive(slot, tbuf.at[rows])
            tension = tbuf[rows]
            out_ref[3, rows] = inp[7, rows] * tension
            for k, value in enumerate(relaxed(0, x, False, without=side)):
                value = value + inp[3 + k, rows] + fib[k, rows] * tension - 0.12 * ext0[k, rows_of(x + 1)]
                unfinished[side, k] = value
                for part, y in ((0, CY - 1), (1, 0)):
                    at = 3 * part + k
                    corner_out[side, at:at + 1] = value[y:y + 1]
            second_halo[side].start()
            second_halo[DIAG_LEFT + side].start()

        nothing = jnp.zeros((1, NZ), F32)

        def finish_end(side):
            x = ENDS[side]
            sign = (-1.0, 1.0)[side]
            stiff[1 - side].wait_recv()
            lists[1 - side].wait_recv()
            take_list(far_irow[side, 0], 2 + side)
            own = [ext0[k, rows_of(x + 1)] for k in range(3)]
            row = (8, 7 + CX)[side]
            below, above = ([halo[0, 3 * half + k, row:row + 1] for k in range(3)] for half in range(2))
            got = picked(2 + side, inp[6, rows_of(x)], own)
            for k, value in enumerate(contribution(own, above, below, -sign, 0.06 / kx[side], got)):
                share[side, k] = value
                for part, y in ((0, CY - 1), (1, 0)):
                    if k < 2:
                        share_out[side, 2 * part + k:2 * part + k + 1] = value[y:y + 1]
            shares[side].start()
            wait_side(first_halo, side)
            far = far_plane(0, side)
            got = picked(side, kx[side], far)
            added_here = contribution(far, [nothing] * 3, [nothing] * 3, sign, rel[rows_of(x)], got)
            for k, value in enumerate(added_here):
                ext1[k, rows_of(x + 1)] = unfinished[side, k] + value
            pack_corners(3, side, end_out)
            second_halo[ACROSS_FIRST + side].start()

        shares = (
            remote(share_out.at[0], share_in.at[0], SHARE_FIRST, near[ACROSS]),
            remote(share_out.at[1], share_in.at[1], SHARE_LAST, near[ACROSS]),
        )
        first_halo[ACROSS].wait_recv()
        halo_rows(0)
        pack_edges(3)
        for copy in edges:
            copy.start()
        send_end(1, TEN_LAST)
        send_end(0, TEN_FIRST)
        receive(TEN_ROWS, trow)
        for side, y in ((0, CY - 1), (1, 0)):
            own = pl.ds(y, CX, stride=CY)
            for k, value in enumerate(relaxed_row(0, y)):
                value = value + inp[3 + k, own]
                base[k, own] = value
                ypk[1, 3 * side + k] = value + fib[k, own] * trow[side]
        second_halo[ACROSS].start()
        for side in (1, 0):
            finish_end(side)

        for index, ((low, high), ready_planes) in enumerate(CHUNKS):
            rows = rows_of(low, high - low)
            receive(TEN_BULK + index, tbuf.at[rows])
            lax.fori_loop(low, high, activate_plane, 0)
            lax.fori_loop(*ready_planes, functools.partial(last_plane, inner=True), 0)
        second_halo[ACROSS].wait_recv()
        for side, y in ((0, CY - 1), (1, 0)):
            own = pl.ds(y, CX, stride=CY)
            for k, value in enumerate(relaxed_row(1, y)):
                out_ref[k, own] = value + inp[3 + k, own] + fib[k, own] * trow[side]
        for side in (1, 0):
            x = ENDS[side]
            second_halo[1 - side].wait_recv()
            for k in range(3):
                ext1[k, pl.ds((0, TOP)[side], CY)] += share[side, k]
            second_halo[ACROSS_FIRST + side].wait_recv()
            edges[1 - side].wait_recv()
            finish_side(3, side, added)
            halo_rows(1)
            last_plane((1, CX - 2)[side], 0)
            last_plane(x, 0)
            for k, value in enumerate(tie_forces(1, side)):
                out_ref[k, rows_of(x)] += value
            shares[side].wait_recv()
            add_corners(3, side, added, second_halo)
        for copy in (*first_halo, *second_halo, *edges, *stiff, *lists, *shares):
            copy.wait_send()


def solution(mesh):
    n_gx = mesh.shape["gx"]

    def local(sections, fiber_angles, fiber_class, row_map, interface_rows):
        vmem = pltpu.VMEM
        field, padded = (COLS, NZ), (EXT, NZ)
        out = pl.pallas_call(
            functools.partial(kernel, n_gx),
            out_shape=jax.ShapeDtypeStruct((4, COLS, NZ), F32),
            in_specs=[pl.BlockSpec(memory_space=pltpu.HBM)] * 5,
            out_specs=pl.BlockSpec(memory_space=pltpu.VMEM),
            scratch_shapes=[
                vmem((8, *field), F32),
                vmem((3, *padded), F32),
                vmem((3, *padded), F32),
                vmem((3, *field), F32),
                vmem((3, *field), F32),
                vmem(field, F32),
                vmem((3, CLASSES, NZ), F32),
                vmem(field, F32),
                vmem(field, F32),
                vmem((2, CX, NZ), F32),
                vmem((COLS, COLS), BF16),
                vmem((COLS, 3 * NZ), BF16),
                vmem((4, CY, CY), BF16),
                vmem((2, 6, 32, NZ), F32),
                vmem((2, 6, CX, NZ), F32),
                vmem((2, 8, NZ), F32),
                vmem((4, 8, NZ), F32),
                vmem((2, 8, NZ), F32),
                vmem((2, 8, NZ), F32),
                vmem((8, CX, NZ), F32),
                vmem((2, CY, NZ), F32),
                vmem((2, CLASSES), F32),
                vmem((CX * 8, CY), jnp.int32),
                vmem((1, 1, COLS), jnp.int32),
                vmem((2, 1, 1, CY), jnp.int32),
                vmem((2, 1, 1, CY), jnp.int32),
                vmem((2, 3, CY, NZ), F32),
                vmem((2, 3, CY, NZ), F32),
                vmem((2, 8, NZ), F32),
                vmem((2, 8, NZ), F32),
                vmem((2, 8, NZ), F32),
                pltpu.SemaphoreType.DMA((11,)),
                pltpu.SemaphoreType.DMA((N_COPIES,)),
                pltpu.SemaphoreType.DMA((N_COPIES,)),
            ],
            compiler_params=pltpu.CompilerParams(
                collective_id=0, has_side_effects=True, vmem_limit_bytes=24 * 1024 * 1024),
        )(*[pltpu.with_memory_space_constraint(operand, pltpu.HBM) for operand in (
            sections.reshape(8, COLS, NZ), fiber_angles.T, fiber_class.transpose(0, 2, 1).reshape(CX * 8, CY), row_map,
            interface_rows)])
        return out.reshape(1, 4, CX, CY, NZ)

    in_specs = (
        P("sec", None, "gx", "gy", None),
        P(),
        P("gx", "gy", None),
        P("gx", "gy", None),
        P(None, "gx", "gy", None),
    )
    out_specs = P("sec", None, "gx", "gy", None)
    return jax.shard_map(local, mesh=mesh, in_specs=in_specs, out_specs=out_specs, check_vma=False)
```

```python
import functools

import jax
import jax.numpy as jnp
from jax import lax
from jax.experimental import pallas as pl
from jax.experimental.pallas import tpu as pltpu
from jax.sharding import PartitionSpec as P

MESH = pl.DeviceIdType.MESH
F32, BF16 = jnp.float32, jnp.bfloat16

CX, CY, NZ = 16, 32, 128
COLS = CX * CY
TOP = COLS + CY
EXT = COLS + 2 * CY
CLASSES = 8
DT = 0.1

CHUNKS = (((1, 5), (2, 4)), ((5, 9), (4, 8)), ((9, 13), (8, 12)), ((13, 15), (12, 14)))

LEFT, RIGHT, ACROSS, DIAG_LEFT, DIAG_RIGHT, STIFF_LEFT, STIFF_RIGHT = range(7)
ACROSS_FIRST, ACROSS_LAST = 5, 6
LIST_LEFT, LIST_RIGHT = 3, 4
EDGE_LEFT, EDGE_RIGHT = 7, 15
TEN_FIRST, TEN_LAST, TEN_ROWS, TEN_BULK = 16, 17, 18, 19
SHARE_FIRST, SHARE_LAST = TEN_BULK + len(CHUNKS), TEN_BULK + len(CHUNKS) + 1
N_COPIES = SHARE_LAST + 1
ENDS = (0, CX - 1)


def rows_of(x, count=1):
    if isinstance(x, int):
        return pl.ds(x * CY, count * CY)
    return pl.ds(pl.multiple_of(x * CY, CY), count * CY)


def lanes(count=CY):
    return lax.broadcasted_iota(jnp.int32, (count, NZ), 1)


def sublanes():
    return lax.broadcasted_iota(jnp.int32, (CY, NZ), 0)


def z_up(a):
    return jnp.where(lanes(a.shape[0]) == NZ - 1, 0.0, pltpu.roll(a, NZ - 1, 1))


def z_down(a):
    return jnp.where(lanes(a.shape[0]) == 0, 0.0, pltpu.roll(a, 1, 1))


def y_up(a, row):
    moved = pltpu.roll(a, CY - 1, 0)
    return moved if row is None else jnp.where(sublanes() == CY - 1, jnp.broadcast_to(row, (CY, NZ)), moved)


def y_down(a, row):
    moved = pltpu.roll(a, 1, 0)
    return moved if row is None else jnp.where(sublanes() == 0, jnp.broadcast_to(row, (CY, NZ)), moved)


def sig(v):
    return 1.0 / (1.0 + jnp.exp(-v))


def split3(a):
    high = a.astype(BF16)
    rest = a - high.astype(F32)
    mid = rest.astype(BF16)
    low = (rest - mid.astype(F32)).astype(BF16)
    return high, mid, low


def kernel(n_gx, sec_ref, ang_ref, cls_ref, rmap_ref, irow_ref, out_ref,
           inp, ext0, ext1, fib, base, rel, tbl, clsx, tbuf, trow, perm, parts, rperm,
           halo, ypk, corner_out, corner_in, edge_out, edge_in, hal, kx, ang, cls, rmap, irow,
           far_irow, unfinished, share, share_out, share_in, end_out,
           load_sem, send_sem, recv_sem):
    sec, gx, gy = lax.axis_index("sec"), lax.axis_index("gx"), lax.axis_index("gy")
    left, right = lax.rem(gx + n_gx - 1, n_gx), lax.rem(gx + 1, n_gx)
    across = 1 - gy
    near = {
        LEFT: (sec, left, gy), RIGHT: (sec, right, gy), ACROSS: (sec, gx, across),
        DIAG_LEFT: (sec, left, across), DIAG_RIGHT: (sec, right, across),
    }
    near[STIFF_LEFT], near[STIFF_RIGHT] = near[LEFT], near[RIGHT]
    partner = (1 - sec, gx, gy)
    ext = (ext0, ext1)

    barrier = pltpu.get_barrier_semaphore()
    for direction in (LEFT, RIGHT, ACROSS):
        pl.semaphore_signal(barrier, inc=1, device_id=near[direction], device_id_type=MESH)

    def load(src, dst, slot):
        return pltpu.make_async_copy(src, dst, load_sem.at[slot])

    def remote(src, dst, slot, device):
        return pltpu.make_async_remote_copy(
            src_ref=src, dst_ref=dst, send_sem=send_sem.at[slot], recv_sem=recv_sem.at[slot],
            device_id=device, device_id_type=MESH)

    def halo_copies(phase, fields):
        first, own = pl.ds(0, fields), ext[phase]
        low, high = own.at[first, pl.ds(CY, CY)], own.at[first, pl.ds(COLS, CY)]
        ends = corner_out
        if phase == 1 and fields == 3:
            low, high, ends = unfinished.at[0], unfinished.at[1], end_out
        both = pl.ds(0, 2 * fields)
        slot = phase * 8
        copies = (
            remote(low, own.at[first, pl.ds(TOP, CY)], slot + LEFT, near[LEFT]),
            remote(high, own.at[first, pl.ds(0, CY)], slot + RIGHT, near[RIGHT]),
            remote(ypk.at[phase, both], halo.at[phase, both, pl.ds(8, CX)], slot + ACROSS, near[ACROSS]),
        )
        if phase == 1:
            copies += (
                remote(corner_out.at[0], corner_in.at[1], slot + DIAG_LEFT, near[DIAG_LEFT]),
                remote(corner_out.at[1], corner_in.at[0], slot + DIAG_RIGHT, near[DIAG_RIGHT]),
                remote(ends.at[0], corner_in.at[2], slot + ACROSS_FIRST, near[ACROSS]),
                remote(ends.at[1], corner_in.at[3], slot + ACROSS_LAST, near[ACROSS]),
            )
        return copies

    def plane_row(part, side):
        return CY + ENDS[side] * CY + (CY - 1, 0)[part]

    def far_row(part, side):
        return (0, TOP)[side] + (CY - 1, 0)[part]

    def pack_corners(fields, side, into=corner_out):
        for part in range(2):
            row = plane_row(part, side)
            for k in range(fields):
                at = part * fields + k
                into[side, at:at + 1] = ext1[k, row:row + 1]

    def pack_edges(fields):
        for side in range(2):
            row = (8, 7 + CX)[side]
            for k in range(2 * fields):
                edge_out[side, k:k + 1] = halo[0, k, row:row + 1]

    edges = (
        remote(edge_out.at[0], edge_in.at[1], EDGE_LEFT, near[LEFT]),
        remote(edge_out.at[1], edge_in.at[0], EDGE_RIGHT, near[RIGHT]),
    )

    def pack_rows(phase, fields):
        for field in range(fields):
            ypk[phase, field] = ext[phase][field, pl.ds(CY + CY - 1, CX, stride=CY)]
            ypk[phase, fields + field] = ext[phase][field, pl.ds(CY, CX, stride=CY)]

    def wait_side(copies, side):
        copies[1 - side].wait_recv()

    def start_side(copies, side):
        copies[side].start()
        if len(copies) > 3:
            copies[DIAG_LEFT + side].start()
            copies[ACROSS_FIRST + side].start()

    def finish_side(fields, side, added):
        sign = (-1.0, 1.0)[side]
        row = (8, 7 + CX)[side]
        for part in range(2):
            own = plane_row(part, side)
            signed = sign * (1.0, -1.0)[part]

            def diag_old(k, part=part):
                at = (1 - part) * fields + k
                return edge_in[side, at:at + 1]

            def far_old(k, part=part):
                at = far_row(1 - part, side)
                return ext0[k, at:at + 1]

            for k in range(min(fields, 2)):
                at = part * fields + k
                ext1[k, own:own + 1] += signed * added(k, "own", part, side, diag_old)
                halo[1, at, row:row + 1] = (
                    corner_in[2 + side, at:at + 1] + signed * added(k, "across", part, side, far_old))
            if fields == 3:
                at = part * fields + 2
                halo[1, at, row:row + 1] = corner_in[2 + side, at:at + 1]

    def finish_far(side, added):
        sign = (-1.0, 1.0)[side]
        row = (8, 7 + CX)[side]
        for part in range(2):
            far = far_row(part, side)
            old = halo[0, 1 - part, row:row + 1]
            ext1[0, far:far + 1] -= sign * (1.0, -1.0)[part] * added(0, "far", part, side, lambda k, old=old: old)

    def add_corners(fields, side, added, copies):
        copies[DIAG_RIGHT - side].wait_recv()
        sign = (-1.0, 1.0)[side]
        corner = []
        for part in range(2):
            signed = sign * (1.0, -1.0)[part]

            def own_old(k, part=part):
                at = plane_row(1 - part, side)
                return ext0[k, at:at + 1]

            corner.append([corner_in[side, part * fields + k:part * fields + k + 1] for k in range(min(fields, 2))])
            if fields == 1:
                corner[part][0] -= signed * added(0, "diag", part, side, own_old)
            else:
                corner[part] = [value + share_in[side, 2 * part + k:2 * part + k + 1]
                                for k, value in enumerate(corner[part])]
        for part in range(2):
            signed = sign * (1.0, -1.0)[part]
            own = plane_row(part, side) - CY
            for k in range(min(fields, 2)):
                out_ref[k, own:own + 1] += signed * added(k, "own", part, side, lambda c, part=part: corner[1 - part][c])

    for k in range(6):
        for row in (7, 8 + CX):
            halo[0, k, row:row + 1] = jnp.zeros((1, NZ), F32)
            halo[1, k, row:row + 1] = jnp.zeros((1, NZ), F32)

    def halo_row(phase, k):
        return halo[phase, k, 8:8 + CX]

    def halo_diff(phase, k):
        return halo[phase, k, 9:9 + CX] - halo[phase, k, 7:7 + CX]

    def row_at(k, x, inner):
        return None if inner else hal[k, pl.ds(x, 1)]

    def row_set(phase, fields, y):
        sets = []
        for at in (y, y + 1, y - 1):
            if at in (-1, CY):
                first = fields if at == CY else 0
                rows = [halo[phase, first + field, 8:8 + CX] for field in range(fields)]
            else:
                rows = [ext[phase][field, pl.ds(CY + at, CX, stride=CY)] for field in range(fields)]
            sets.append([(row, pltpu.roll(row, CX - 1, 0), pltpu.roll(row, 1, 0)) for row in rows])
        return sets

    def spread_fibers():
        azimuth, elevation = ang[0:1, :], ang[1:2, :]
        flat = jnp.cos(elevation)
        for k, value in enumerate((jnp.cos(azimuth) * flat, jnp.sin(azimuth) * flat, jnp.sin(elevation))):
            for c in range(CLASSES):
                tbl[k, c:c + 1] = jnp.broadcast_to(value[:, c:c + 1], (1, NZ))
        kind = cls[...].astype(F32).T.astype(BF16)
        from_lane = lax.broadcasted_iota(jnp.int32, (NZ, CX * NZ), 0)
        to_lane = lax.broadcasted_iota(jnp.int32, (NZ, CX * NZ), 1) // 16
        spread = jnp.where(from_lane == to_lane, 1.0, 0.0).astype(BF16)
        wide = jnp.dot(kind, spread, preferred_element_type=F32)
        for x in range(CX):
            clsx[x * CY:(x + 1) * CY] = wide[:, x * NZ:(x + 1) * NZ]

    def fiber_of(x):
        kind = clsx[rows_of(x)]
        bit2 = kind >= 3.5
        kind = jnp.where(bit2, kind - 4.0, kind)
        bit1 = kind >= 1.5
        bit0 = jnp.where(bit1, kind - 2.0, kind) >= 0.5
        fields = []
        for k in range(3):
            pick = [jnp.broadcast_to(tbl[k, c:c + 1], (CY, NZ)) for c in range(CLASSES)]
            pick = [jnp.where(bit0, pick[2 * c + 1], pick[2 * c]) for c in range(4)]
            pick = [jnp.where(bit1, pick[2 * c + 1], pick[2 * c]) for c in range(2)]
            fields.append(jnp.where(bit2, pick[1], pick[0]))
        return fields


    @pl.when(sec == 0)
    def _():
        loads = [load(sec_ref.at[0], ext0.at[0, pl.ds(CY, COLS)], 0)]
        loads += [load(sec_ref.at[k], inp.at[k], k) for k in range(1, 8)]
        load_map = load(rmap_ref, rmap, 8)
        load_cls = load(cls_ref, cls, 9)
        load_ang = load(ang_ref, ang, 10)
        load_map.start()
        load_cls.start()
        load_ang.start()
        for k in (0, 1, 2, 3, 6, 7):
            loads[k].start()
        loads[4].start()
        loads[5].start()

        load_map.wait()
        source = jnp.broadcast_to(rmap[0].astype(F32), (8, COLS)).T[:, 0:1]
        spot = lax.broadcasted_iota(jnp.int32, (COLS, COLS), 1).astype(F32)
        perm[...] = jnp.where(jnp.broadcast_to(source, (COLS, COLS)) == spot, 1.0, 0.0).astype(BF16)

        load_ang.wait()
        load_cls.wait()
        spread_fibers()

        def fiber_plane(x, carry):
            for k, value in enumerate(fiber_of(x)):
                fib[k, rows_of(x)] = value
            return carry

        lax.fori_loop(0, CX, fiber_plane, 0)
        for side in range(2):
            for part in range(2):
                row = plane_row(part, side) - CY
                factor = (0.375 * DT) * fib[0, row:row + 1] * fib[1, row:row + 1]
                edge_out[side, 2 + part:3 + part] = factor
                corner_out[side, 4 + part:5 + part] = factor

        for k in (0, 1, 2, 3, 6, 7):
            loads[k].wait()

        def tension_plane(x, carry):
            rows = rows_of(x)
            v = ext0[0, rows_of(x + 1)]
            c, d, f, b, s = inp[1, rows], inp[2, rows], inp[3, rows], inp[6, rows], inp[7, rows]
            square = c * c
            q = square / (square + 0.25)
            flow = 1.2 * d * f * (v - 2.0)
            binding = 2.0 * c * (1.0 - b) - 0.4 * b
            c = c + DT * (-0.3 * flow - 0.5 * c - binding)
            base[0, rows] = c
            base[1, rows] = q
            base[2, rows] = flow
            inp[6, rows] = b + DT * binding
            s = s + DT * (q - s) / 2.0
            square = c * c
            q = square / (square + 0.25)
            out_ref[1, rows] = q
            s = s + DT * (q - s) / 2.0
            out_ref[3, rows] = s
            for k, part in enumerate(split3(s)):
                parts[rows, k * NZ:(k + 1) * NZ] = part
            return carry

        lax.fori_loop(0, CX, tension_plane, 0)

        def permuted(low, high):
            moved = jnp.dot(perm[low * CY:high * CY], parts[...], preferred_element_type=F32)
            tbuf[low * CY:high * CY] = moved[:, 0:NZ] + (moved[:, NZ:2 * NZ] + moved[:, 2 * NZ:])

        permuted(CX - 1, CX)
        permuted(0, CX - 1)
        trow[0] = tbuf[pl.ds(CY - 1, CX, stride=CY)]
        trow[1] = tbuf[pl.ds(0, CX, stride=CY)]
        pack_rows(0, 1)
        pl.semaphore_wait(barrier, 4)
        first_halo = halo_copies(0, 1)
        tension = [
            remote(tbuf.at[rows_of(CX - 1)], tbuf.at[rows_of(CX - 1)], TEN_LAST, partner),
            remote(trow, trow, TEN_ROWS, partner),
            remote(tbuf.at[rows_of(0)], tbuf.at[rows_of(0)], TEN_FIRST, partner),
        ]
        tension[0].start()
        first_halo[ACROSS].start()
        start_side(first_halo, 0)
        start_side(first_halo, 1)
        for k, ((low, high), _) in enumerate(CHUNKS):
            rows = rows_of(low, high - low)
            tension.append(remote(tbuf.at[rows], tbuf.at[rows], TEN_BULK + k, partner))
        for copy in tension[1:]:
            copy.start()
        loads[4].wait()
        loads[5].wait()

        def first_ions(x, carry):
            rows = rows_of(x)
            v = ext0[0, rows_of(x + 1)]
            d, f, n, r = inp[2, rows], inp[3, rows], inp[4, rows], inp[5, rows]
            flow, q = base[2, rows], base[1, rows]
            current = flow + 0.8 * n * (v + 1.0) + 0.6 * q * r * (v + 1.0) + 0.1 * v
            base[1, rows] = v - DT * current
            inp[2, rows] = d + DT * (sig(2.0 * v + 1.0) - d) / 0.5
            inp[3, rows] = f + DT * (sig(-2.0 * v) - f) / 3.0
            inp[4, rows] = n + DT * (sig(2.0 * v) - n)
            inp[5, rows] = r + DT * (sig(v - 0.5) - r) / 5.0
            return carry

        lax.fori_loop(0, CX, first_ions, 0)

        def added(k, where, part, side, old):
            if where == "own":
                factor = edge_out[side, 2 + part:3 + part]
            elif where == "far":
                factor = edge_in[side, 2 + part:3 + part]
            else:
                factor = corner_in[side + (2 if where == "across" else 0), 4 + part:5 + part]
            return factor * old(0)

        def combined(fiber, c, v00, v11, v22, x01, x02, x12):
            f0, f1, f2 = fiber
            along = (f0 * (f0 * v00 + 0.5 * (f1 * x01 + f2 * x02))
                     + f1 * (f1 * v11 + 0.5 * (f2 * x12)) + f2 * f2 * v22)
            return 0.25 * (v00 + v11 + v22) + 0.75 * along

        def diffusion(phase, x, inner=False):
            here = ext[phase]
            c, p, m = here[0, rows_of(x + 1)], here[0, rows_of(x + 2)], here[0, rows_of(x)]
            d = p - m
            yu, yd = y_up(c, row_at(0, x, inner)), y_down(c, row_at(1, x, inner))
            e = yu - yd
            twice = 2.0 * c
            return combined(
                [fib[k, rows_of(x)] for k in range(3)], c, p + m - twice, yu + yd - twice, z_up(c) + z_down(c) - twice,
                y_up(d, row_at(2, x, inner)) - y_down(d, row_at(3, x, inner)), z_up(d) - z_down(d), z_up(e) - z_down(e))

        def diffusion_row(phase, y):
            ((c, p, m),), ((cu, pu, mu),), ((cd, pd, md),) = row_set(phase, 1, y)
            d, e, twice = p - m, cu - cd, 2.0 * c
            return combined(
                [fib[k, pl.ds(y, CX, stride=CY)] for k in range(3)], c, p + m - twice, cu + cd - twice,
                z_up(c) + z_down(c) - twice, (pu - mu) - (pd - md), z_up(d) - z_down(d), z_up(e) - z_down(e))

        def halo_rows(phase):
            hal[0] = halo_row(phase, 1)
            hal[1] = halo_row(phase, 0)
            hal[2] = halo_diff(phase, 1)
            hal[3] = halo_diff(phase, 0)

        def first_step(x, carry, inner=False):
            ext1[0, rows_of(x + 1)] = base[1, rows_of(x)] + DT * diffusion(0, x, inner)
            return carry

        lax.fori_loop(1, CX - 1, functools.partial(first_step, inner=True), 0)
        second_halo = halo_copies(1, 1)
        first_halo[ACROSS].wait_recv()
        pack_edges(1)
        for copy in edges:
            copy.start()
        halo_rows(0)
        for side in (1, 0):
            wait_side(first_halo, side)
            first_step(ENDS[side], 0)
            pack_corners(1, side)
            start_side(second_halo, side)
            if side == 1:
                for part, y in ((0, CY - 1), (1, 0)):
                    row = base[1, pl.ds(y, CX, stride=CY)] + DT * diffusion_row(0, y)
                    ypk[1, part] = row
                    ext1[0, pl.ds(2 * CY + y, CX - 2, stride=CY)] = row[1:CX - 1]
                second_halo[ACROSS].start()

        def second_ions(x, carry):
            rows = rows_of(x)
            v, c, q = ext1[0, rows_of(x + 1)], base[0, rows], out_ref[1, rows]
            d, f, n, r, b = inp[2, rows], inp[3, rows], inp[4, rows], inp[5, rows], inp[6, rows]
            flow = 1.2 * d * f * (v - 2.0)
            current = flow + 0.8 * n * (v + 1.0) + 0.6 * q * r * (v + 1.0) + 0.1 * v
            binding = 2.0 * c * (1.0 - b) - 0.4 * b
            base[1, rows] = v - DT * current
            out_ref[1, rows] = c + DT * (-0.3 * flow - 0.5 * c - binding)
            out_ref[2, rows] = n + DT * (sig(2.0 * v) - n)
            return carry

        lax.fori_loop(1, CX - 1, second_ions, 0)

        def second_step(x, carry, inner=False):
            rows = rows_of(x)
            out_ref[0, rows] = base[1, rows] + DT * diffusion(1, x, inner)
            return carry

        lax.fori_loop(2, CX - 2, functools.partial(second_step, inner=True), 0)
        second_halo[ACROSS].wait_recv()
        for y in (CY - 1, 0):
            row = pl.ds(y, CX, stride=CY)
            out_ref[0, row] = base[1, row] + DT * diffusion_row(1, y)
        for side in (1, 0):
            second_halo[ACROSS_FIRST + side].wait_recv()
            edges[1 - side].wait_recv()
            second_halo[side].wait_send()
            finish_side(1, side, added)
            halo_rows(1)
            second_ions(ENDS[side], 0)
            second_step((1, CX - 2)[side], 0)
            if side == 0:
                for copy in (*first_halo, *second_halo[2:], *edges, *tension):
                    copy.wait_send()
            wait_side(second_halo, side)
            finish_far(side, added)
            second_step(ENDS[side], 0)
            add_corners(1, side, added, second_halo)


    @pl.when(sec == 1)
    def _():
        pl.semaphore_signal(barrier, inc=1, device_id=partner, device_id_type=MESH)
        load_u = load(sec_ref.at[pl.ds(0, 3)], ext0.at[:, pl.ds(CY, COLS)], 0)
        load_rest = load(sec_ref.at[pl.ds(3, 5)], inp.at[pl.ds(3, 5)], 1)
        load_row = load(irow_ref, irow, 8)
        load_cls = load(cls_ref, cls, 9)
        load_ang = load(ang_ref, ang, 10)
        load_ang.start()
        load_cls.start()
        load_row.start()
        load_u.start()
        load_rest.start()

        load_ang.wait()
        load_cls.wait()
        spread_fibers()

        def take_list(values, slot):
            source = jnp.broadcast_to(values.astype(F32), (CY, CY)).T
            spot = lax.broadcasted_iota(jnp.int32, (CY, CY), 1).astype(F32)
            rperm[slot] = jnp.where(source == spot, 1.0, 0.0).astype(BF16)

        load_row.wait()
        for side in range(2):
            take_list(irow[side, 0], side)

        def fiber_plane(x, carry):
            for k, value in enumerate(fiber_of(x)):
                fib[k, rows_of(x)] = value
            return carry

        lax.fori_loop(0, CX, fiber_plane, 0)
        load_u.wait()
        pack_rows(0, 3)
        load_rest.wait()
        pl.semaphore_wait(barrier, 3)
        first_halo = halo_copies(0, 3)
        stiff = (
            remote(inp.at[6, pl.ds(0, CY)], kx.at[1], STIFF_LEFT, near[STIFF_LEFT]),
            remote(inp.at[6, pl.ds(COLS - CY, CY)], kx.at[0], STIFF_RIGHT, near[STIFF_RIGHT]),
        )
        lists = (
            remote(irow.at[0], far_irow.at[1], LIST_LEFT, near[LEFT]),
            remote(irow.at[1], far_irow.at[0], LIST_RIGHT, near[RIGHT]),
        )
        first_halo[ACROSS].start()
        for side in range(2):
            start_side(first_halo, side)
            stiff[side].start()
            lists[side].start()

        def weight_plane(x, carry):
            rows = rows_of(x)
            relax = 0.06 / inp[6, rows]
            rel[rows] = relax
            drive = relax * inp[7, rows]
            for k in range(3):
                fib[k, rows] = drive * fib[k, rows]
                inp[3 + k, rows] = relax * inp[3 + k, rows]
            return carry

        lax.fori_loop(0, CX, weight_plane, 0)

        def halo_rows(phase):
            for side, sign in ((1, 0.5), (0, -0.5)):
                k = 3 * side
                at = 4 * (1 - side)
                hal[at] = halo_row(phase, k) + sign * halo_diff(phase, k + 1)
                hal[at + 1] = 3.0 * halo_row(phase, k + 1) + sign * halo_diff(phase, k)
                hal[at + 2] = halo_row(phase, k + 1)
                hal[at + 3] = halo_row(phase, k + 2)

        def relaxed(phase, x, inner, without=None):
            here = ext[phase]
            mid, p, m = rows_of(x + 1), rows_of(x + 2), rows_of(x)
            c0, c1, c2 = here[0, mid], here[1, mid], here[2, mid]
            p0, p1, p2 = here[0, p], here[1, p], here[2, p]
            m0, m1, m2 = here[0, m], here[1, m], here[2, m]
            if without == 0:
                m0 = m1 = m2 = jnp.zeros_like(c0)
            if without == 1:
                p0 = p1 = p2 = jnp.zeros_like(c0)
            row = [row_at(k, x, inner) for k in range(8)]
            d0, d1, d2 = 0.5 * (p0 - m0), 0.5 * (p1 - m1), 0.5 * (p2 - m2)
            y2u, y2d = y_up(c2, row[3]), y_down(c2, row[7])
            e1 = 0.5 * (y_up(c1, row[2]) - y_down(c1, row[6]))
            e2 = 0.5 * (y2u - y2d)
            t1, t2 = 3.0 * c1, 3.0 * c2
            cross = d0 + e1
            s0 = (3.0 * (p0 + m0) + (y_up(c0 + d1, row[0]) + y_down(c0 - d1, row[4]))
                  + (z_up(c0 + d2) + z_down(c0 - d2)))
            s1 = ((p1 + m1) + (y_up(t1 + d0, row[1]) + y_down(t1 - d0, row[5]))
                  + (z_up(c1 + e2) + z_down(c1 - e2)))
            s2 = (p2 + m2) + (y2u + y2d) + (z_up(t2 + cross) + z_down(t2 - cross))
            return 0.4 * c0 + 0.06 * s0, 0.4 * c1 + 0.06 * s1, 0.4 * c2 + 0.06 * s2

        def relaxed_row(phase, y):
            here, up, down = row_set(phase, 3, y)
            (c0, p0, m0), (c1, p1, m1), (c2, p2, m2) = here
            d0, d2 = 0.5 * (p0 - m0), 0.5 * (p2 - m2)
            u0, u1 = 0.5 * (up[0][1] - up[0][2]), 0.5 * (up[1][1] - up[1][2])
            b0, b1 = 0.5 * (down[0][1] - down[0][2]), 0.5 * (down[1][1] - down[1][2])
            e2 = 0.5 * (up[2][0] - down[2][0])
            cross = d0 + 0.5 * (up[1][0] - down[1][0])
            t2 = 3.0 * c2
            s0 = (3.0 * (p0 + m0) + ((up[0][0] + u1) + (down[0][0] - b1)) + (z_up(c0 + d2) + z_down(c0 - d2)))
            s1 = ((p1 + m1) + ((3.0 * up[1][0] + u0) + (3.0 * down[1][0] - b0)) + (z_up(c1 + e2) + z_down(c1 - e2)))
            s2 = (p2 + m2) + (up[2][0] + down[2][0]) + (z_up(t2 + cross) + z_down(t2 - cross))
            return 0.4 * c0 + 0.06 * s0, 0.4 * c1 + 0.06 * s1, 0.4 * c2 + 0.06 * s2

        def added(k, where, part, side, old):
            return 0.03 * old(1 - k) if k < 2 else 0.0

        def picked(slot, stiffness, planes):
            pieces = []
            for plane in planes:
                pieces += list(split3((2.0 * stiffness) * plane))
            got = jnp.dot(rperm[slot], jnp.concatenate(pieces, axis=1), preferred_element_type=F32)
            return [got[:, at:at + NZ] + (got[:, at + NZ:at + 2 * NZ] + got[:, at + 2 * NZ:at + 3 * NZ])
                    for at in (0, 3 * NZ, 6 * NZ)]

        def far_plane(phase, side):
            return [ext[phase][k, pl.ds((0, TOP)[side], CY)] for k in range(3)]

        def tie_forces(phase, side):
            x = ENDS[side]
            relax = rel[rows_of(x)]
            got = picked(side, kx[side], far_plane(phase, side))
            return [relax * got[k] - 0.12 * ext[phase][k, rows_of(x + 1)] for k in range(3)]

        def contribution(planes, above, below, sign, relax, got):
            p0, p1, p2 = planes
            half = 0.5 * sign
            across0 = half * (y_up(p0, above[0]) - y_down(p0, below[0]))
            across1 = half * (y_up(p1, above[1]) - y_down(p1, below[1]))
            s0 = 3.0 * p0 + across1 + half * (z_up(p2) - z_down(p2))
            s1 = p1 + across0
            s2 = p2 + half * (z_up(p0) - z_down(p0))
            return [0.06 * value + relax * got[k] for k, value in enumerate((s0, s1, s2))]

        def receive(slot, ref):
            remote(ref, ref, slot, partner).wait_recv()

        def base_plane(x, carry, inner=False):
            rows = rows_of(x)
            for k, value in enumerate(relaxed(0, x, inner)):
                base[k, rows] = value + inp[3 + k, rows]
            return carry

        def activate_plane(x, carry):
            rows = rows_of(x)
            tension = tbuf[rows]
            out_ref[3, rows] = inp[7, rows] * tension
            for k in range(3):
                ext1[k, rows_of(x + 1)] = base[k, rows] + fib[k, rows] * tension
            return carry

        def last_plane(x, carry, inner=False):
            rows = rows_of(x)
            tension = tbuf[rows]
            for k, value in enumerate(relaxed(1, x, inner)):
                out_ref[k, rows] = value + inp[3 + k, rows] + fib[k, rows] * tension
            return carry

        lax.fori_loop(1, CX - 1, functools.partial(base_plane, inner=True), 0)
        second_halo = halo_copies(1, 3)
        def send_end(side, slot):
            x = ENDS[side]
            rows = rows_of(x)
            receive(slot, tbuf.at[rows])
            tension = tbuf[rows]
            out_ref[3, rows] = inp[7, rows] * tension
            for k, value in enumerate(relaxed(0, x, False, without=side)):
                value = value + inp[3 + k, rows] + fib[k, rows] * tension - 0.12 * ext0[k, rows_of(x + 1)]
                unfinished[side, k] = value
                for part, y in ((0, CY - 1), (1, 0)):
                    at = 3 * part + k
                    corner_out[side, at:at + 1] = value[y:y + 1]
            second_halo[side].start()
            second_halo[DIAG_LEFT + side].start()

        nothing = jnp.zeros((1, NZ), F32)

        def finish_end(side):
            x = ENDS[side]
            sign = (-1.0, 1.0)[side]
            stiff[1 - side].wait_recv()
            lists[1 - side].wait_recv()
            take_list(far_irow[side, 0], 2 + side)
            own = [ext0[k, rows_of(x + 1)] for k in range(3)]
            row = (8, 7 + CX)[side]
            below, above = ([halo[0, 3 * half + k, row:row + 1] for k in range(3)] for half in range(2))
            got = picked(2 + side, inp[6, rows_of(x)], own)
            for k, value in enumerate(contribution(own, above, below, -sign, 0.06 / kx[side], got)):
                share[side, k] = value
                for part, y in ((0, CY - 1), (1, 0)):
                    if k < 2:
                        share_out[side, 2 * part + k:2 * part + k + 1] = value[y:y + 1]
            shares[side].start()
            wait_side(first_halo, side)
            far = far_plane(0, side)
            got = picked(side, kx[side], far)
            added_here = contribution(far, [nothing] * 3, [nothing] * 3, sign, rel[rows_of(x)], got)
            for k, value in enumerate(added_here):
                ext1[k, rows_of(x + 1)] = unfinished[side, k] + value
            pack_corners(3, side, end_out)
            second_halo[ACROSS_FIRST + side].start()

        shares = (
            remote(share_out.at[0], share_in.at[0], SHARE_FIRST, near[ACROSS]),
            remote(share_out.at[1], share_in.at[1], SHARE_LAST, near[ACROSS]),
        )
        first_halo[ACROSS].wait_recv()
        halo_rows(0)
        send_end(1, TEN_LAST)
        send_end(0, TEN_FIRST)
        pack_edges(3)
        for copy in edges:
            copy.start()
        receive(TEN_ROWS, trow)
        for side, y in ((0, CY - 1), (1, 0)):
            own = pl.ds(y, CX, stride=CY)
            for k, value in enumerate(relaxed_row(0, y)):
                value = value + inp[3 + k, own]
                base[k, own] = value
                ypk[1, 3 * side + k] = value + fib[k, own] * trow[side]
        second_halo[ACROSS].start()
        for side in (1, 0):
            finish_end(side)

        for index, ((low, high), ready_planes) in enumerate(CHUNKS):
            rows = rows_of(low, high - low)
            receive(TEN_BULK + index, tbuf.at[rows])
            lax.fori_loop(low, high, activate_plane, 0)
            lax.fori_loop(*ready_planes, functools.partial(last_plane, inner=True), 0)
        second_halo[ACROSS].wait_recv()
        for side, y in ((0, CY - 1), (1, 0)):
            own = pl.ds(y, CX, stride=CY)
            for k, value in enumerate(relaxed_row(1, y)):
                out_ref[k, own] = value + inp[3 + k, own] + fib[k, own] * trow[side]
        for side in (1, 0):
            x = ENDS[side]
            second_halo[ACROSS_FIRST + side].wait_recv()
            edges[1 - side].wait_recv()
            finish_side(3, side, added)
            halo_rows(1)
            last_plane((1, CX - 2)[side], 0)
            shares[side].wait_recv()
            if side == 0:
                for copy in (*first_halo, *second_halo, *edges, *stiff, *lists, *shares):
                    copy.wait_send()
            second_halo[1 - side].wait_recv()
            for k in range(3):
                ext1[k, pl.ds((0, TOP)[side], CY)] += share[side, k]
            last_plane(x, 0)
            for k, value in enumerate(tie_forces(1, side)):
                out_ref[k, rows_of(x)] += value
            add_corners(3, side, added, second_halo)


def solution(mesh):
    n_gx = mesh.shape["gx"]

    def local(sections, fiber_angles, fiber_class, row_map, interface_rows):
        vmem = pltpu.VMEM
        field, padded = (COLS, NZ), (EXT, NZ)
        out = pl.pallas_call(
            functools.partial(kernel, n_gx),
            out_shape=jax.ShapeDtypeStruct((4, COLS, NZ), F32),
            in_specs=[pl.BlockSpec(memory_space=pltpu.HBM)] * 5,
            out_specs=pl.BlockSpec(memory_space=pltpu.VMEM),
            scratch_shapes=[
                vmem((8, *field), F32),
                vmem((3, *padded), F32),
                vmem((3, *padded), F32),
                vmem((3, *field), F32),
                vmem((3, *field), F32),
                vmem(field, F32),
                vmem((3, CLASSES, NZ), F32),
                vmem(field, F32),
                vmem(field, F32),
                vmem((2, CX, NZ), F32),
                vmem((COLS, COLS), BF16),
                vmem((COLS, 3 * NZ), BF16),
                vmem((4, CY, CY), BF16),
                vmem((2, 6, 32, NZ), F32),
                vmem((2, 6, CX, NZ), F32),
                vmem((2, 8, NZ), F32),
                vmem((4, 8, NZ), F32),
                vmem((2, 8, NZ), F32),
                vmem((2, 8, NZ), F32),
                vmem((8, CX, NZ), F32),
                vmem((2, CY, NZ), F32),
                vmem((2, CLASSES), F32),
                vmem((CX * 8, CY), jnp.int32),
                vmem((1, 1, COLS), jnp.int32),
                vmem((2, 1, 1, CY), jnp.int32),
                vmem((2, 1, 1, CY), jnp.int32),
                vmem((2, 3, CY, NZ), F32),
                vmem((2, 3, CY, NZ), F32),
                vmem((2, 8, NZ), F32),
                vmem((2, 8, NZ), F32),
                vmem((2, 8, NZ), F32),
                pltpu.SemaphoreType.DMA((11,)),
                pltpu.SemaphoreType.DMA((N_COPIES,)),
                pltpu.SemaphoreType.DMA((N_COPIES,)),
            ],
            compiler_params=pltpu.CompilerParams(
                collective_id=0, has_side_effects=True, vmem_limit_bytes=24 * 1024 * 1024),
        )(*[pltpu.with_memory_space_constraint(operand, pltpu.HBM) for operand in (
            sections.reshape(8, COLS, NZ), fiber_angles.T, fiber_class.transpose(0, 2, 1).reshape(CX * 8, CY), row_map,
            interface_rows)])
        return out.reshape(1, 4, CX, CY, NZ)

    in_specs = (
        P("sec", None, "gx", "gy", None),
        P(),
        P("gx", "gy", None),
        P("gx", "gy", None),
        P(None, "gx", "gy", None),
    )
    out_specs = P("sec", None, "gx", "gy", None)
    return jax.shard_map(local, mesh=mesh, in_specs=in_specs, out_specs=out_specs, check_vma=False)
```

```python
import functools

import jax
import jax.numpy as jnp
from jax import lax
from jax.experimental import pallas as pl
from jax.experimental.pallas import tpu as pltpu
from jax.sharding import PartitionSpec as P

MESH = pl.DeviceIdType.MESH
F32, BF16 = jnp.float32, jnp.bfloat16

CX, CY, NZ = 16, 32, 128
COLS = CX * CY
TOP = COLS + CY
EXT = COLS + 2 * CY
CLASSES = 8
DT = 0.1

CHUNKS = (((1, 5), (2, 4)), ((5, 9), (4, 8)), ((9, 13), (8, 12)), ((13, 15), (12, 14)))

LEFT, RIGHT, ACROSS, DIAG_LEFT, DIAG_RIGHT, STIFF_LEFT, STIFF_RIGHT = range(7)
ACROSS_FIRST, ACROSS_LAST = 5, 6
LIST_LEFT, LIST_RIGHT = 3, 4
EDGE_LEFT, EDGE_RIGHT = 7, 15
TEN_FIRST, TEN_LAST, TEN_ROWS, TEN_BULK = 16, 17, 18, 19
SHARE_FIRST, SHARE_LAST = TEN_BULK + len(CHUNKS), TEN_BULK + len(CHUNKS) + 1
N_COPIES = SHARE_LAST + 1
ENDS = (0, CX - 1)


def rows_of(x, count=1):
    if isinstance(x, int):
        return pl.ds(x * CY, count * CY)
    return pl.ds(pl.multiple_of(x * CY, CY), count * CY)


def lanes(count=CY):
    return lax.broadcasted_iota(jnp.int32, (count, NZ), 1)


def sublanes():
    return lax.broadcasted_iota(jnp.int32, (CY, NZ), 0)


def z_up(a):
    return jnp.where(lanes(a.shape[0]) == NZ - 1, 0.0, pltpu.roll(a, NZ - 1, 1))


def z_down(a):
    return jnp.where(lanes(a.shape[0]) == 0, 0.0, pltpu.roll(a, 1, 1))


def y_up(a, row):
    moved = pltpu.roll(a, CY - 1, 0)
    return moved if row is None else jnp.where(sublanes() == CY - 1, jnp.broadcast_to(row, (CY, NZ)), moved)


def y_down(a, row):
    moved = pltpu.roll(a, 1, 0)
    return moved if row is None else jnp.where(sublanes() == 0, jnp.broadcast_to(row, (CY, NZ)), moved)


def sig(v):
    return 1.0 / (1.0 + jnp.exp(-v))


def split3(a):
    high = a.astype(BF16)
    rest = a - high.astype(F32)
    mid = rest.astype(BF16)
    low = (rest - mid.astype(F32)).astype(BF16)
    return high, mid, low


def kernel(n_gx, sec_ref, ang_ref, cls_ref, rmap_ref, irow_ref, out_ref,
           inp, ext0, ext1, fib, base, rel, tbl, clsx, tbuf, trow, perm, parts, rperm,
           halo, ypk, corner_out, corner_in, edge_out, edge_in, hal, kx, ang, cls, rmap, irow,
           far_irow, unfinished, share, share_out, share_in, end_out,
           load_sem, send_sem, recv_sem):
    sec, gx, gy = lax.axis_index("sec"), lax.axis_index("gx"), lax.axis_index("gy")
    left, right = lax.rem(gx + n_gx - 1, n_gx), lax.rem(gx + 1, n_gx)
    across = 1 - gy
    near = {
        LEFT: (sec, left, gy), RIGHT: (sec, right, gy), ACROSS: (sec, gx, across),
        DIAG_LEFT: (sec, left, across), DIAG_RIGHT: (sec, right, across),
    }
    near[STIFF_LEFT], near[STIFF_RIGHT] = near[LEFT], near[RIGHT]
    partner = (1 - sec, gx, gy)
    ext = (ext0, ext1)

    barrier = pltpu.get_barrier_semaphore()
    for direction in (LEFT, RIGHT, ACROSS):
        pl.semaphore_signal(barrier, inc=1, device_id=near[direction], device_id_type=MESH)

    def load(src, dst, slot):
        return pltpu.make_async_copy(src, dst, load_sem.at[slot])

    def remote(src, dst, slot, device):
        return pltpu.make_async_remote_copy(
            src_ref=src, dst_ref=dst, send_sem=send_sem.at[slot], recv_sem=recv_sem.at[slot],
            device_id=device, device_id_type=MESH)

    def halo_copies(phase, fields):
        first, own = pl.ds(0, fields), ext[phase]
        low, high = own.at[first, pl.ds(CY, CY)], own.at[first, pl.ds(COLS, CY)]
        ends = corner_out
        if phase == 1 and fields == 3:
            low, high, ends = unfinished.at[0], unfinished.at[1], end_out
        both = pl.ds(0, 2 * fields)
        slot = phase * 8
        copies = (
            remote(low, own.at[first, pl.ds(TOP, CY)], slot + LEFT, near[LEFT]),
            remote(high, own.at[first, pl.ds(0, CY)], slot + RIGHT, near[RIGHT]),
            remote(ypk.at[phase, both], halo.at[phase, both, pl.ds(8, CX)], slot + ACROSS, near[ACROSS]),
        )
        if phase == 1:
            copies += (
                remote(corner_out.at[0], corner_in.at[1], slot + DIAG_LEFT, near[DIAG_LEFT]),
                remote(corner_out.at[1], corner_in.at[0], slot + DIAG_RIGHT, near[DIAG_RIGHT]),
                remote(ends.at[0], corner_in.at[2], slot + ACROSS_FIRST, near[ACROSS]),
                remote(ends.at[1], corner_in.at[3], slot + ACROSS_LAST, near[ACROSS]),
            )
        return copies

    def plane_row(part, side):
        return CY + ENDS[side] * CY + (CY - 1, 0)[part]

    def far_row(part, side):
        return (0, TOP)[side] + (CY - 1, 0)[part]

    def pack_corners(fields, side, into=corner_out):
        for part in range(2):
            row = plane_row(part, side)
            for k in range(fields):
                at = part * fields + k
                into[side, at:at + 1] = ext1[k, row:row + 1]

    def pack_edges(fields):
        for side in range(2):
            row = (8, 7 + CX)[side]
            for k in range(2 * fields):
                edge_out[side, k:k + 1] = halo[0, k, row:row + 1]

    edges = (
        remote(edge_out.at[0], edge_in.at[1], EDGE_LEFT, near[LEFT]),
        remote(edge_out.at[1], edge_in.at[0], EDGE_RIGHT, near[RIGHT]),
    )

    def pack_rows(phase, fields):
        for field in range(fields):
            ypk[phase, field] = ext[phase][field, pl.ds(CY + CY - 1, CX, stride=CY)]
            ypk[phase, fields + field] = ext[phase][field, pl.ds(CY, CX, stride=CY)]

    def wait_side(copies, side):
        copies[1 - side].wait_recv()

    def start_side(copies, side):
        copies[side].start()
        if len(copies) > 3:
            copies[DIAG_LEFT + side].start()
            copies[ACROSS_FIRST + side].start()

    def finish_side(fields, side, added):
        sign = (-1.0, 1.0)[side]
        row = (8, 7 + CX)[side]
        for part in range(2):
            own = plane_row(part, side)
            signed = sign * (1.0, -1.0)[part]

            def diag_old(k, part=part):
                at = (1 - part) * fields + k
                return edge_in[side, at:at + 1]

            def far_old(k, part=part):
                at = far_row(1 - part, side)
                return ext0[k, at:at + 1]

            for k in range(min(fields, 2)):
                at = part * fields + k
                ext1[k, own:own + 1] += signed * added(k, "own", part, side, diag_old)
                halo[1, at, row:row + 1] = (
                    corner_in[2 + side, at:at + 1] + signed * added(k, "across", part, side, far_old))
            if fields == 3:
                at = part * fields + 2
                halo[1, at, row:row + 1] = corner_in[2 + side, at:at + 1]

    def finish_far(side, added):
        sign = (-1.0, 1.0)[side]
        row = (8, 7 + CX)[side]
        for part in range(2):
            far = far_row(part, side)
            old = halo[0, 1 - part, row:row + 1]
            ext1[0, far:far + 1] -= sign * (1.0, -1.0)[part] * added(0, "far", part, side, lambda k, old=old: old)

    def add_corners(fields, side, added, copies):
        copies[DIAG_RIGHT - side].wait_recv()
        sign = (-1.0, 1.0)[side]
        corner = []
        for part in range(2):
            signed = sign * (1.0, -1.0)[part]

            def own_old(k, part=part):
                at = plane_row(1 - part, side)
                return ext0[k, at:at + 1]

            corner.append([corner_in[side, part * fields + k:part * fields + k + 1] for k in range(min(fields, 2))])
            if fields == 1:
                corner[part][0] -= signed * added(0, "diag", part, side, own_old)
            else:
                corner[part] = [value + share_in[side, 2 * part + k:2 * part + k + 1]
                                for k, value in enumerate(corner[part])]
        for part in range(2):
            signed = sign * (1.0, -1.0)[part]
            own = plane_row(part, side) - CY
            for k in range(min(fields, 2)):
                out_ref[k, own:own + 1] += signed * added(k, "own", part, side, lambda c, part=part: corner[1 - part][c])

    for k in range(6):
        for row in (7, 8 + CX):
            halo[0, k, row:row + 1] = jnp.zeros((1, NZ), F32)
            halo[1, k, row:row + 1] = jnp.zeros((1, NZ), F32)

    def halo_row(phase, k):
        return halo[phase, k, 8:8 + CX]

    def halo_diff(phase, k):
        return halo[phase, k, 9:9 + CX] - halo[phase, k, 7:7 + CX]

    def row_at(k, x, inner):
        return None if inner else hal[k, pl.ds(x, 1)]

    def row_set(phase, fields, y):
        sets = []
        for at in (y, y + 1, y - 1):
            if at in (-1, CY):
                first = fields if at == CY else 0
                rows = [halo[phase, first + field, 8:8 + CX] for field in range(fields)]
            else:
                rows = [ext[phase][field, pl.ds(CY + at, CX, stride=CY)] for field in range(fields)]
            sets.append([(row, pltpu.roll(row, CX - 1, 0), pltpu.roll(row, 1, 0)) for row in rows])
        return sets

    def spread_fibers():
        azimuth, elevation = ang[0:1, :], ang[1:2, :]
        flat = jnp.cos(elevation)
        for k, value in enumerate((jnp.cos(azimuth) * flat, jnp.sin(azimuth) * flat, jnp.sin(elevation))):
            for c in range(CLASSES):
                tbl[k, c:c + 1] = jnp.broadcast_to(value[:, c:c + 1], (1, NZ))
        kind = cls[...].astype(F32).T.astype(BF16)
        from_lane = lax.broadcasted_iota(jnp.int32, (NZ, CX * NZ), 0)
        to_lane = lax.broadcasted_iota(jnp.int32, (NZ, CX * NZ), 1) // 16
        spread = jnp.where(from_lane == to_lane, 1.0, 0.0).astype(BF16)
        wide = jnp.dot(kind, spread, preferred_element_type=F32)
        for x in range(CX):
            clsx[x * CY:(x + 1) * CY] = wide[:, x * NZ:(x + 1) * NZ]

    def fiber_of(x):
        kind = clsx[rows_of(x)]
        bit2 = kind >= 3.5
        kind = jnp.where(bit2, kind - 4.0, kind)
        bit1 = kind >= 1.5
        bit0 = jnp.where(bit1, kind - 2.0, kind) >= 0.5
        fields = []
        for k in range(3):
            pick = [jnp.broadcast_to(tbl[k, c:c + 1], (CY, NZ)) for c in range(CLASSES)]
            pick = [jnp.where(bit0, pick[2 * c + 1], pick[2 * c]) for c in range(4)]
            pick = [jnp.where(bit1, pick[2 * c + 1], pick[2 * c]) for c in range(2)]
            fields.append(jnp.where(bit2, pick[1], pick[0]))
        return fields


    @pl.when(sec == 0)
    def _():
        loads = [load(sec_ref.at[0], ext0.at[0, pl.ds(CY, COLS)], 0)]
        loads += [load(sec_ref.at[k], inp.at[k], k) for k in range(1, 8)]
        load_map = load(rmap_ref, rmap, 8)
        load_cls = load(cls_ref, cls, 9)
        load_ang = load(ang_ref, ang, 10)
        load_map.start()
        load_cls.start()
        load_ang.start()
        for k in (0, 1, 2, 3, 6, 7):
            loads[k].start()
        loads[4].start()
        loads[5].start()

        load_map.wait()
        source = jnp.broadcast_to(rmap[0].astype(F32), (8, COLS)).T[:, 0:1]
        spot = lax.broadcasted_iota(jnp.int32, (COLS, COLS), 1).astype(F32)
        perm[...] = jnp.where(jnp.broadcast_to(source, (COLS, COLS)) == spot, 1.0, 0.0).astype(BF16)

        load_ang.wait()
        load_cls.wait()
        spread_fibers()

        def fiber_plane(x, carry):
            for k, value in enumerate(fiber_of(x)):
                fib[k, rows_of(x)] = value
            return carry

        lax.fori_loop(0, CX, fiber_plane, 0)
        for side in range(2):
            for part in range(2):
                row = plane_row(part, side) - CY
                factor = (0.375 * DT) * fib[0, row:row + 1] * fib[1, row:row + 1]
                edge_out[side, 2 + part:3 + part] = factor
                corner_out[side, 4 + part:5 + part] = factor

        for k in (0, 1, 2, 3, 6, 7):
            loads[k].wait()

        def tension_plane(x, carry):
            rows = rows_of(x)
            v = ext0[0, rows_of(x + 1)]
            c, d, f, b, s = inp[1, rows], inp[2, rows], inp[3, rows], inp[6, rows], inp[7, rows]
            square = c * c
            q = square / (square + 0.25)
            flow = 1.2 * d * f * (v - 2.0)
            binding = 2.0 * c * (1.0 - b) - 0.4 * b
            c = c + DT * (-0.3 * flow - 0.5 * c - binding)
            base[0, rows] = c
            base[1, rows] = q
            base[2, rows] = flow
            inp[6, rows] = b + DT * binding
            s = s + DT * (q - s) / 2.0
            square = c * c
            q = square / (square + 0.25)
            out_ref[1, rows] = q
            s = s + DT * (q - s) / 2.0
            out_ref[3, rows] = s
            for k, part in enumerate(split3(s)):
                parts[rows, k * NZ:(k + 1) * NZ] = part
            return carry

        lax.fori_loop(0, CX, tension_plane, 0)

        def permuted(low, high):
            moved = jnp.dot(perm[low * CY:high * CY], parts[...], preferred_element_type=F32)
            tbuf[low * CY:high * CY] = moved[:, 0:NZ] + (moved[:, NZ:2 * NZ] + moved[:, 2 * NZ:])

        permuted(CX - 1, CX)
        permuted(0, CX - 1)
        trow[0] = tbuf[pl.ds(CY - 1, CX, stride=CY)]
        trow[1] = tbuf[pl.ds(0, CX, stride=CY)]
        pack_rows(0, 1)
        pl.semaphore_wait(barrier, 4)
        first_halo = halo_copies(0, 1)
        tension = [
            remote(tbuf.at[rows_of(CX - 1)], tbuf.at[rows_of(CX - 1)], TEN_LAST, partner),
            remote(trow, trow, TEN_ROWS, partner),
            remote(tbuf.at[rows_of(0)], tbuf.at[rows_of(0)], TEN_FIRST, partner),
        ]
        tension[0].start()
        first_halo[ACROSS].start()
        start_side(first_halo, 0)
        start_side(first_halo, 1)
        for k, ((low, high), _) in enumerate(CHUNKS):
            rows = rows_of(low, high - low)
            tension.append(remote(tbuf.at[rows], tbuf.at[rows], TEN_BULK + k, partner))
        for copy in tension[1:]:
            copy.start()
        loads[4].wait()
        loads[5].wait()

        def first_ions(x, carry):
            rows = rows_of(x)
            v = ext0[0, rows_of(x + 1)]
            d, f, n, r = inp[2, rows], inp[3, rows], inp[4, rows], inp[5, rows]
            flow, q = base[2, rows], base[1, rows]
            current = flow + 0.8 * n * (v + 1.0) + 0.6 * q * r * (v + 1.0) + 0.1 * v
            base[1, rows] = v - DT * current
            inp[2, rows] = d + DT * (sig(2.0 * v + 1.0) - d) / 0.5
            inp[3, rows] = f + DT * (sig(-2.0 * v) - f) / 3.0
            inp[4, rows] = n + DT * (sig(2.0 * v) - n)
            inp[5, rows] = r + DT * (sig(v - 0.5) - r) / 5.0
            return carry

        lax.fori_loop(0, CX, first_ions, 0)

        def added(k, where, part, side, old):
            if where == "own":
                factor = edge_out[side, 2 + part:3 + part]
            elif where == "far":
                factor = edge_in[side, 2 + part:3 + part]
            else:
                factor = corner_in[side + (2 if where == "across" else 0), 4 + part:5 + part]
            return factor * old(0)

        def combined(fiber, c, v00, v11, v22, x01, x02, x12):
            f0, f1, f2 = fiber
            along = (f0 * (f0 * v00 + 0.5 * (f1 * x01 + f2 * x02))
                     + f1 * (f1 * v11 + 0.5 * (f2 * x12)) + f2 * f2 * v22)
            return 0.25 * (v00 + v11 + v22) + 0.75 * along

        def diffusion(phase, x, inner=False):
            here = ext[phase]
            c, p, m = here[0, rows_of(x + 1)], here[0, rows_of(x + 2)], here[0, rows_of(x)]
            d = p - m
            yu, yd = y_up(c, row_at(0, x, inner)), y_down(c, row_at(1, x, inner))
            e = yu - yd
            twice = 2.0 * c
            return combined(
                [fib[k, rows_of(x)] for k in range(3)], c, p + m - twice, yu + yd - twice, z_up(c) + z_down(c) - twice,
                y_up(d, row_at(2, x, inner)) - y_down(d, row_at(3, x, inner)), z_up(d) - z_down(d), z_up(e) - z_down(e))

        def diffusion_row(phase, y):
            ((c, p, m),), ((cu, pu, mu),), ((cd, pd, md),) = row_set(phase, 1, y)
            d, e, twice = p - m, cu - cd, 2.0 * c
            return combined(
                [fib[k, pl.ds(y, CX, stride=CY)] for k in range(3)], c, p + m - twice, cu + cd - twice,
                z_up(c) + z_down(c) - twice, (pu - mu) - (pd - md), z_up(d) - z_down(d), z_up(e) - z_down(e))

        def halo_rows(phase):
            hal[0] = halo_row(phase, 1)
            hal[1] = halo_row(phase, 0)
            hal[2] = halo_diff(phase, 1)
            hal[3] = halo_diff(phase, 0)

        def first_step(x, carry, inner=False):
            ext1[0, rows_of(x + 1)] = base[1, rows_of(x)] + DT * diffusion(0, x, inner)
            return carry

        lax.fori_loop(1, CX - 1, functools.partial(first_step, inner=True), 0)
        second_halo = halo_copies(1, 1)
        first_halo[ACROSS].wait_recv()
        pack_edges(1)
        for copy in edges:
            copy.start()
        halo_rows(0)
        for side in (1, 0):
            wait_side(first_halo, side)
            first_step(ENDS[side], 0)
            pack_corners(1, side)
            start_side(second_halo, side)
            if side == 1:
                for part, y in ((0, CY - 1), (1, 0)):
                    row = base[1, pl.ds(y, CX, stride=CY)] + DT * diffusion_row(0, y)
                    ypk[1, part] = row
                    ext1[0, pl.ds(2 * CY + y, CX - 2, stride=CY)] = row[1:CX - 1]
                second_halo[ACROSS].start()

        def second_ions(x, carry):
            rows = rows_of(x)
            v, c, q = ext1[0, rows_of(x + 1)], base[0, rows], out_ref[1, rows]
            d, f, n, r, b = inp[2, rows], inp[3, rows], inp[4, rows], inp[5, rows], inp[6, rows]
            flow = 1.2 * d * f * (v - 2.0)
            current = flow + 0.8 * n * (v + 1.0) + 0.6 * q * r * (v + 1.0) + 0.1 * v
            binding = 2.0 * c * (1.0 - b) - 0.4 * b
            base[1, rows] = v - DT * current
            out_ref[1, rows] = c + DT * (-0.3 * flow - 0.5 * c - binding)
            out_ref[2, rows] = n + DT * (sig(2.0 * v) - n)
            return carry

        lax.fori_loop(1, CX - 1, second_ions, 0)

        def second_step(x, carry, inner=False):
            rows = rows_of(x)
            out_ref[0, rows] = base[1, rows] + DT * diffusion(1, x, inner)
            return carry

        lax.fori_loop(2, CX - 2, functools.partial(second_step, inner=True), 0)
        second_halo[ACROSS].wait_recv()
        for y in (CY - 1, 0):
            row = pl.ds(y, CX, stride=CY)
            out_ref[0, row] = base[1, row] + DT * diffusion_row(1, y)
        for side in (1, 0):
            second_halo[ACROSS_FIRST + side].wait_recv()
            edges[1 - side].wait_recv()
            second_halo[side].wait_send()
            finish_side(1, side, added)
            halo_rows(1)
            second_ions(ENDS[side], 0)
            second_step((1, CX - 2)[side], 0)
            if side == 0:
                for copy in (*first_halo, *second_halo[2:], *edges, *tension):
                    copy.wait_send()
            wait_side(second_halo, side)
            finish_far(side, added)
            second_step(ENDS[side], 0)
            add_corners(1, side, added, second_halo)


    @pl.when(sec == 1)
    def _():
        pl.semaphore_signal(barrier, inc=1, device_id=partner, device_id_type=MESH)
        load_u = load(sec_ref.at[pl.ds(0, 3)], ext0.at[:, pl.ds(CY, COLS)], 0)
        load_rest = load(sec_ref.at[pl.ds(3, 5)], inp.at[pl.ds(3, 5)], 1)
        load_row = load(irow_ref, irow, 8)
        load_cls = load(cls_ref, cls, 9)
        load_ang = load(ang_ref, ang, 10)
        load_ang.start()
        load_cls.start()
        load_row.start()
        load_u.start()
        load_rest.start()

        load_ang.wait()
        load_cls.wait()
        spread_fibers()

        def take_list(values, slot):
            source = jnp.broadcast_to(values.astype(F32), (CY, CY)).T
            spot = lax.broadcasted_iota(jnp.int32, (CY, CY), 1).astype(F32)
            rperm[slot] = jnp.where(source == spot, 1.0, 0.0).astype(BF16)

        load_row.wait()
        for side in range(2):
            take_list(irow[side, 0], side)

        def fiber_plane(x, carry):
            for k, value in enumerate(fiber_of(x)):
                fib[k, rows_of(x)] = value
            return carry

        lax.fori_loop(0, CX, fiber_plane, 0)
        load_u.wait()
        pack_rows(0, 3)
        load_rest.wait()
        pl.semaphore_wait(barrier, 3)
        first_halo = halo_copies(0, 3)
        stiff = (
            remote(inp.at[6, pl.ds(0, CY)], kx.at[1], STIFF_LEFT, near[STIFF_LEFT]),
            remote(inp.at[6, pl.ds(COLS - CY, CY)], kx.at[0], STIFF_RIGHT, near[STIFF_RIGHT]),
        )
        lists = (
            remote(irow.at[0], far_irow.at[1], LIST_LEFT, near[LEFT]),
            remote(irow.at[1], far_irow.at[0], LIST_RIGHT, near[RIGHT]),
        )
        first_halo[ACROSS].start()
        for side in range(2):
            start_side(first_halo, side)
            stiff[side].start()
            lists[side].start()

        def weight_plane(x, carry):
            rows = rows_of(x)
            relax = 0.06 / inp[6, rows]
            rel[rows] = relax
            drive = relax * inp[7, rows]
            for k in range(3):
                fib[k, rows] = drive * fib[k, rows]
                inp[3 + k, rows] = relax * inp[3 + k, rows]
            return carry

        lax.fori_loop(0, CX, weight_plane, 0)

        def halo_rows(phase):
            for side, sign in ((1, 0.5), (0, -0.5)):
                k = 3 * side
                at = 4 * (1 - side)
                hal[at] = halo_row(phase, k) + sign * halo_diff(phase, k + 1)
                hal[at + 1] = 3.0 * halo_row(phase, k + 1) + sign * halo_diff(phase, k)
                hal[at + 2] = halo_row(phase, k + 1)
                hal[at + 3] = halo_row(phase, k + 2)

        def relaxed(phase, x, inner, without=None):
            here = ext[phase]
            mid, p, m = rows_of(x + 1), rows_of(x + 2), rows_of(x)
            c0, c1, c2 = here[0, mid], here[1, mid], here[2, mid]
            p0, p1, p2 = here[0, p], here[1, p], here[2, p]
            m0, m1, m2 = here[0, m], here[1, m], here[2, m]
            if without == 0:
                m0 = m1 = m2 = jnp.zeros_like(c0)
            if without == 1:
                p0 = p1 = p2 = jnp.zeros_like(c0)
            row = [row_at(k, x, inner) for k in range(8)]
            d0, d1, d2 = 0.5 * (p0 - m0), 0.5 * (p1 - m1), 0.5 * (p2 - m2)
            y2u, y2d = y_up(c2, row[3]), y_down(c2, row[7])
            e1 = 0.5 * (y_up(c1, row[2]) - y_down(c1, row[6]))
            e2 = 0.5 * (y2u - y2d)
            t1, t2 = 3.0 * c1, 3.0 * c2
            cross = d0 + e1
            s0 = (3.0 * (p0 + m0) + (y_up(c0 + d1, row[0]) + y_down(c0 - d1, row[4]))
                  + (z_up(c0 + d2) + z_down(c0 - d2)))
            s1 = ((p1 + m1) + (y_up(t1 + d0, row[1]) + y_down(t1 - d0, row[5]))
                  + (z_up(c1 + e2) + z_down(c1 - e2)))
            s2 = (p2 + m2) + (y2u + y2d) + (z_up(t2 + cross) + z_down(t2 - cross))
            return 0.4 * c0 + 0.06 * s0, 0.4 * c1 + 0.06 * s1, 0.4 * c2 + 0.06 * s2

        def relaxed_row(phase, y):
            here, up, down = row_set(phase, 3, y)
            (c0, p0, m0), (c1, p1, m1), (c2, p2, m2) = here
            d0, d2 = 0.5 * (p0 - m0), 0.5 * (p2 - m2)
            u0, u1 = 0.5 * (up[0][1] - up[0][2]), 0.5 * (up[1][1] - up[1][2])
            b0, b1 = 0.5 * (down[0][1] - down[0][2]), 0.5 * (down[1][1] - down[1][2])
            e2 = 0.5 * (up[2][0] - down[2][0])
            cross = d0 + 0.5 * (up[1][0] - down[1][0])
            t2 = 3.0 * c2
            s0 = (3.0 * (p0 + m0) + ((up[0][0] + u1) + (down[0][0] - b1)) + (z_up(c0 + d2) + z_down(c0 - d2)))
            s1 = ((p1 + m1) + ((3.0 * up[1][0] + u0) + (3.0 * down[1][0] - b0)) + (z_up(c1 + e2) + z_down(c1 - e2)))
            s2 = (p2 + m2) + (up[2][0] + down[2][0]) + (z_up(t2 + cross) + z_down(t2 - cross))
            return 0.4 * c0 + 0.06 * s0, 0.4 * c1 + 0.06 * s1, 0.4 * c2 + 0.06 * s2

        def added(k, where, part, side, old):
            return 0.03 * old(1 - k) if k < 2 else 0.0

        def picked(slot, stiffness, planes):
            pieces = []
            for plane in planes:
                pieces += list(split3((2.0 * stiffness) * plane))
            got = jnp.dot(rperm[slot], jnp.concatenate(pieces, axis=1), preferred_element_type=F32)
            return [got[:, at:at + NZ] + (got[:, at + NZ:at + 2 * NZ] + got[:, at + 2 * NZ:at + 3 * NZ])
                    for at in (0, 3 * NZ, 6 * NZ)]

        def far_plane(phase, side):
            return [ext[phase][k, pl.ds((0, TOP)[side], CY)] for k in range(3)]

        def tie_forces(phase, side):
            x = ENDS[side]
            relax = rel[rows_of(x)]
            got = picked(side, kx[side], far_plane(phase, side))
            return [relax * got[k] - 0.12 * ext[phase][k, rows_of(x + 1)] for k in range(3)]

        def contribution(planes, above, below, sign, relax, got):
            p0, p1, p2 = planes
            half = 0.5 * sign
            across0 = half * (y_up(p0, above[0]) - y_down(p0, below[0]))
            across1 = half * (y_up(p1, above[1]) - y_down(p1, below[1]))
            s0 = 3.0 * p0 + across1 + half * (z_up(p2) - z_down(p2))
            s1 = p1 + across0
            s2 = p2 + half * (z_up(p0) - z_down(p0))
            return [0.06 * value + relax * got[k] for k, value in enumerate((s0, s1, s2))]

        def receive(slot, ref):
            remote(ref, ref, slot, partner).wait_recv()

        def base_plane(x, carry, inner=False):
            rows = rows_of(x)
            for k, value in enumerate(relaxed(0, x, inner)):
                base[k, rows] = value + inp[3 + k, rows]
            return carry

        def activate_plane(x, carry):
            rows = rows_of(x)
            tension = tbuf[rows]
            out_ref[3, rows] = inp[7, rows] * tension
            for k in range(3):
                ext1[k, rows_of(x + 1)] = base[k, rows] + fib[k, rows] * tension
            return carry

        def last_plane(x, carry, inner=False):
            rows = rows_of(x)
            tension = tbuf[rows]
            for k, value in enumerate(relaxed(1, x, inner)):
                out_ref[k, rows] = value + inp[3 + k, rows] + fib[k, rows] * tension
            return carry

        lax.fori_loop(1, CX - 1, functools.partial(base_plane, inner=True), 0)
        second_halo = halo_copies(1, 3)
        def send_end(side, slot):
            x = ENDS[side]
            rows = rows_of(x)
            receive(slot, tbuf.at[rows])
            tension = tbuf[rows]
            out_ref[3, rows] = inp[7, rows] * tension
            for k, value in enumerate(relaxed(0, x, False, without=side)):
                value = value + inp[3 + k, rows] + fib[k, rows] * tension - 0.12 * ext0[k, rows_of(x + 1)]
                unfinished[side, k] = value
                for part, y in ((0, CY - 1), (1, 0)):
                    at = 3 * part + k
                    corner_out[side, at:at + 1] = value[y:y + 1]
            second_halo[side].start()
            second_halo[DIAG_LEFT + side].start()

        nothing = jnp.zeros((1, NZ), F32)

        def finish_end(side):
            x = ENDS[side]
            sign = (-1.0, 1.0)[side]
            stiff[1 - side].wait_recv()
            lists[1 - side].wait_recv()
            take_list(far_irow[side, 0], 2 + side)
            own = [ext0[k, rows_of(x + 1)] for k in range(3)]
            row = (8, 7 + CX)[side]
            below, above = ([halo[0, 3 * half + k, row:row + 1] for k in range(3)] for half in range(2))
            got = picked(2 + side, inp[6, rows_of(x)], own)
            for k, value in enumerate(contribution(own, above, below, -sign, 0.06 / kx[side], got)):
                share[side, k] = value
                for part, y in ((0, CY - 1), (1, 0)):
                    if k < 2:
                        share_out[side, 2 * part + k:2 * part + k + 1] = value[y:y + 1]
            shares[side].start()
            wait_side(first_halo, side)
            far = far_plane(0, side)
            got = picked(side, kx[side], far)
            added_here = contribution(far, [nothing] * 3, [nothing] * 3, sign, rel[rows_of(x)], got)
            for k, value in enumerate(added_here):
                ext1[k, rows_of(x + 1)] = unfinished[side, k] + value
            pack_corners(3, side, end_out)
            second_halo[ACROSS_FIRST + side].start()

        shares = (
            remote(share_out.at[0], share_in.at[0], SHARE_FIRST, near[ACROSS]),
            remote(share_out.at[1], share_in.at[1], SHARE_LAST, near[ACROSS]),
        )
        first_halo[ACROSS].wait_recv()
        halo_rows(0)
        send_end(1, TEN_LAST)
        send_end(0, TEN_FIRST)
        pack_edges(3)
        for copy in edges:
            copy.start()
        receive(TEN_ROWS, trow)
        for side, y in ((0, CY - 1), (1, 0)):
            own = pl.ds(y, CX, stride=CY)
            for k, value in enumerate(relaxed_row(0, y)):
                value = value + inp[3 + k, own]
                base[k, own] = value
                ypk[1, 3 * side + k] = value + fib[k, own] * trow[side]
        second_halo[ACROSS].start()
        for side in (1, 0):
            finish_end(side)

        for index, ((low, high), ready_planes) in enumerate(CHUNKS):
            rows = rows_of(low, high - low)
            receive(TEN_BULK + index, tbuf.at[rows])
            lax.fori_loop(low, high, activate_plane, 0)
            lax.fori_loop(*ready_planes, functools.partial(last_plane, inner=True), 0)
        second_halo[ACROSS].wait_recv()
        for side, y in ((0, CY - 1), (1, 0)):
            own = pl.ds(y, CX, stride=CY)
            for k, value in enumerate(relaxed_row(1, y)):
                out_ref[k, own] = value + inp[3 + k, own] + fib[k, own] * trow[side]
        for side in (1, 0):
            x = ENDS[side]
            second_halo[ACROSS_FIRST + side].wait_recv()
            edges[1 - side].wait_recv()
            finish_side(3, side, added)
            halo_rows(1)
            last_plane((1, CX - 2)[side], 0)
            shares[side].wait_recv()
            if side == 0:
                for copy in (*first_halo, *second_halo, *edges, *stiff, *lists, *shares):
                    copy.wait_send()
            second_halo[1 - side].wait_recv()
            for k in range(3):
                ext1[k, pl.ds((0, TOP)[side], CY)] += share[side, k]
            last_plane(x, 0)
            for k, value in enumerate(tie_forces(1, side)):
                out_ref[k, rows_of(x)] += value
            add_corners(3, side, added, second_halo)


def deliver(from_ref, to_ref, sem):
    copies = []
    for k in range(8):
        part = pl.ds(k % 2 * (COLS // 2), COLS // 2)
        copies.append(pltpu.make_async_copy(from_ref.at[k // 2, part], to_ref.at[k // 2, part], sem.at[k]))
    for copy in copies:
        copy.start()
    for copy in copies:
        copy.wait()


def solution(mesh):
    n_gx = mesh.shape["gx"]

    def local(sections, fiber_angles, fiber_class, row_map, interface_rows):
        vmem = pltpu.VMEM
        field, padded = (COLS, NZ), (EXT, NZ)
        out = pl.pallas_call(
            functools.partial(kernel, n_gx),
            out_shape=jax.ShapeDtypeStruct((4, COLS, NZ), F32),
            in_specs=[pl.BlockSpec(memory_space=pltpu.HBM)] * 5,
            out_specs=pl.BlockSpec(memory_space=pltpu.VMEM),
            scratch_shapes=[
                vmem((8, *field), F32),
                vmem((3, *padded), F32),
                vmem((3, *padded), F32),
                vmem((3, *field), F32),
                vmem((3, *field), F32),
                vmem(field, F32),
                vmem((3, CLASSES, NZ), F32),
                vmem(field, F32),
                vmem(field, F32),
                vmem((2, CX, NZ), F32),
                vmem((COLS, COLS), BF16),
                vmem((COLS, 3 * NZ), BF16),
                vmem((4, CY, CY), BF16),
                vmem((2, 6, 32, NZ), F32),
                vmem((2, 6, CX, NZ), F32),
                vmem((2, 8, NZ), F32),
                vmem((4, 8, NZ), F32),
                vmem((2, 8, NZ), F32),
                vmem((2, 8, NZ), F32),
                vmem((8, CX, NZ), F32),
                vmem((2, CY, NZ), F32),
                vmem((2, CLASSES), F32),
                vmem((CX * 8, CY), jnp.int32),
                vmem((1, 1, COLS), jnp.int32),
                vmem((2, 1, 1, CY), jnp.int32),
                vmem((2, 1, 1, CY), jnp.int32),
                vmem((2, 3, CY, NZ), F32),
                vmem((2, 3, CY, NZ), F32),
                vmem((2, 8, NZ), F32),
                vmem((2, 8, NZ), F32),
                vmem((2, 8, NZ), F32),
                pltpu.SemaphoreType.DMA((11,)),
                pltpu.SemaphoreType.DMA((N_COPIES,)),
                pltpu.SemaphoreType.DMA((N_COPIES,)),
            ],
            compiler_params=pltpu.CompilerParams(
                collective_id=0, has_side_effects=True, vmem_limit_bytes=24 * 1024 * 1024),
        )(*[pltpu.with_memory_space_constraint(operand, pltpu.HBM) for operand in (
            sections.reshape(8, COLS, NZ), fiber_angles.T, fiber_class.transpose(0, 2, 1).reshape(CX * 8, CY), row_map,
            interface_rows)])
        out = pl.pallas_call(
            deliver,
            out_shape=jax.ShapeDtypeStruct((4, COLS, NZ), F32),
            in_specs=[pl.BlockSpec(memory_space=pltpu.VMEM)],
            out_specs=pl.BlockSpec(memory_space=pl.ANY),
            scratch_shapes=[pltpu.SemaphoreType.DMA((8,))],
            compiler_params=pltpu.CompilerParams(vmem_limit_bytes=24 * 1024 * 1024),
        )(pltpu.with_memory_space_constraint(out, pltpu.VMEM))
        return out.reshape(1, 4, CX, CY, NZ)

    in_specs = (
        P("sec", None, "gx", "gy", None),
        P(),
        P("gx", "gy", None),
        P("gx", "gy", None),
        P(None, "gx", "gy", None),
    )
    out_specs = P("sec", None, "gx", "gy", None)
    return jax.shard_map(local, mesh=mesh, in_specs=in_specs, out_specs=out_specs, check_vma=False)
```
